32 devices in a mesh: bunch: 8 (over y, x, core), tile: 4 (over z).
Axes of the slice: x: 2, y: 2, z: 4, core: 2. Of those that a mesh axis runs over, the one named last changes fastest.
Arguments:
- cell_index: int32 [2, 8, 2, 4096], P(None, 'bunch', None, 'tile'), may hold values from 0 to 255
- charges: bfloat16 [2, 8, 4096], P(None, 'bunch', 'tile'), may hold values from 0.5 to 2
- momenta: float32 [2, 8, 2, 4096], P(None, 'bunch', None, 'tile'), may hold values from -6 to 6
- fill_pattern: int32 [2, 8], P(None, 'bunch'), may hold values 0 or 1
- encounters: int32 [4, 2, 2, 8], P(None, None, None, 'bunch'), may hold values 0 or 1
- green_spectrum: float32 [256, 256], P(None, 'tile'), may hold values from 0.5 to 4
- stop_gain: float32 [4], replicated, may hold values from 0.5 to 2
- parasitic_gain: float32 [4], replicated, may hold values from 0.25 to 1
Outputs:
- kicked: float32 [2, 8, 2, 4096], P(None, 'bunch', None, 'tile')
The draws below stay inside these ranges and needn't reach their ends.
All inputs are finite; a program needn't handle non-finite values. No bound on the sum of `fill_pattern` or of `encounters` on one device may be relied on, other than what follows from the above.
Results may differ from the reference program's by a relative error of at most 0.0037.
Values may be sent and summed in bfloat16 or wider, within the bound.
No kernel may reach another device: no remote copies, remote signals or barrier semaphores. Data moves between devices by JAX's collectives and lax.ppermute only.
A program may use at most 128 MiB of HBM per device.

```python
import math
import jax
import jax.numpy as jnp
from jax import lax

GRID = 256
STOPS = 4
OFFSET_CELLS = 32
BUN_DEV = 1
BUNCHES = 8
PARTS_SIZE = 4096


def set_ends(array, stream_key, least, largest):
    index_at = [jax.random.randint(jax.random.fold_in(stream_key, axis), (), 0, length) for axis, length in enumerate(array.shape)]
    widest = array.shape.index(max(array.shape))
    next_to = index_at[:widest] + [(index_at[widest] + 1) % array.shape[widest]] + index_at[widest + 1:]
    return array.at[tuple(index_at)].set(least).at[tuple(next_to)].set(largest)


def steps_of(key, shape, cuts, low, high):
    loudness = 1.0
    for position, shards_of in cuts:
        heights = jax.random.uniform(jax.random.fold_in(jax.random.fold_in(key, 6), position), (shards_of,), jnp.float32, low / len(cuts), high / len(cuts))
        loudness = loudness * jnp.repeat(jnp.exp(heights), shape[position] // shards_of).reshape((-1,) + (1,) * (len(shape) - 1 - position))
    return loudness


def gaussian(rng, shape, spread, reach, split=(), held_as=jnp.bfloat16):
    result = spread * jax.random.normal(rng, shape, jnp.float32)
    if split:
        result = result * steps_of(rng, shape, split, -0.22, 0.18)
    return jnp.clip(result, -reach, reach).astype(held_as)


def setup_inputs(seed: int = 0) -> dict:
    arg_keys = jax.random.split(jax.random.key(seed), 9)
    return {
        "cell_index": set_ends(jax.random.randint(arg_keys[0], (2, BUNCHES, 2, PARTS_SIZE), 0, GRID), jax.random.fold_in(arg_keys[0], 1), 0, GRID - 1).astype(jnp.int32),
        "charges": jnp.clip(jnp.exp(math.log(2.0) - 1.3862944 * jax.random.uniform(arg_keys[1], (2, BUNCHES, PARTS_SIZE), jnp.float32) ** steps_of(arg_keys[1], (2, BUNCHES, PARTS_SIZE), ((1, 8), (2, 4)), -0.2, 0.2)), 0.5, 2.0).astype(jnp.bfloat16),
        "momenta": gaussian(arg_keys[2], (2, BUNCHES, 2, PARTS_SIZE), 1.0, 6.0, ((1, 8), (3, 4)), jnp.float32),
        "fill_pattern": set_ends((jax.random.randint(arg_keys[3], (2, BUNCHES), 0, 4) < 3).astype(jnp.int32), jax.random.fold_in(arg_keys[3], 1), 0, 1),
        "encounters": set_ends((jax.random.randint(arg_keys[4], (STOPS, 2, 2, BUNCHES), 0, 2) < 1).astype(jnp.int32), jax.random.fold_in(arg_keys[4], 1), 0, 1),
        "green_spectrum": jnp.clip(jnp.exp(math.log(4.0) - 2.0794415 * jax.random.uniform(arg_keys[5], (GRID, GRID), jnp.float32) ** steps_of(arg_keys[5], (GRID, GRID), ((1, 4),), -0.2, 0.2)), 0.5, 4.0),
        "stop_gain": jnp.clip(jnp.exp(jax.random.uniform(arg_keys[6], (STOPS,), jnp.float32, math.log(0.5), math.log(2.0))), 0.5, 2.0),
        "parasitic_gain": jnp.clip(jnp.exp(jax.random.uniform(arg_keys[7], (STOPS,), jnp.float32, math.log(0.25), math.log(1.0))), 0.25, 1.0),
    }


def shifted_up(operand, amount):
    kept = operand[..., :GRID - amount]
    widths = [(0, 0)] * (operand.ndim - 1) + [(amount, 0)]
    return jnp.pad(kept, widths)


def shifted_down(operand, amount):
    kept = operand[..., amount:]
    widths = [(0, 0)] * (operand.ndim - 1) + [(0, amount)]
    return jnp.pad(kept, widths)


def reference(cell_index, charges, momenta, fill_pattern, encounters, green_spectrum, stop_gain, parasitic_gain):
    flat_cells = cell_index.reshape(2 * BUNCHES, 2, PARTS_SIZE)
    flat_charges = charges.reshape(2 * BUNCHES, PARTS_SIZE)
    flat_fill = fill_pattern.reshape(2 * BUNCHES)

    def one_bunch(operands):
        cells_b, charge_b, fill_b = operands
        density = jnp.zeros((GRID, GRID), jnp.float32).at[cells_b[0], cells_b[1]].add(charge_b.astype(jnp.float32))
        density = density * fill_b.astype(jnp.float32)
        spectrum = jnp.fft.fft2(density)
        potential = jnp.real(jnp.fft.ifft2(green_spectrum * spectrum)).astype(density.dtype)
        along_x = -0.5 * (jnp.roll(potential, -1, 0) - jnp.roll(potential, 1, 0))
        along_y = -0.5 * (jnp.roll(potential, -1, 1) - jnp.roll(potential, 1, 1))
        return jnp.stack([along_x, along_y]).astype(jnp.bfloat16)

    fields = lax.map(one_bunch, (flat_cells, flat_charges, flat_fill)).reshape(2, BUNCHES, 2, GRID, GRID)
    outputs = []
    for beam_index in range(2):
        opposing = fields[1 - beam_index]
        direction = 1 if beam_index == 0 else -1
        partners = [jnp.roll(opposing, -direction * offset * BUN_DEV, axis=0) for offset in range(STOPS + 1)]
        summed = jnp.zeros((BUNCHES, 2, GRID, GRID), jnp.float32)
        for stop_number in range(STOPS):
            summed = summed + stop_gain[stop_number] * partners[stop_number].astype(jnp.float32)
            weight = stop_gain[stop_number] * parasitic_gain[stop_number]
            mark_up = encounters[stop_number, beam_index, 0].astype(jnp.float32)[:, None, None, None]
            following = shifted_up(partners[stop_number + 1].astype(jnp.float32), OFFSET_CELLS)
            summed = summed + weight * mark_up * following
            if stop_number >= 1:
                mark_down = encounters[stop_number, beam_index, 1].astype(jnp.float32)[:, None, None, None]
                earlier = shifted_down(partners[stop_number - 1].astype(jnp.float32), OFFSET_CELLS)
                summed = summed + weight * mark_down * earlier
        total_field = summed.astype(jnp.bfloat16)

        def kick_one(operands):
            field_b, cells_b = operands
            return field_b[:, cells_b[0], cells_b[1]].astype(jnp.float32)

        kick_sum = lax.map(kick_one, (total_field, cell_index[beam_index]))
        outputs.append(momenta[beam_index] + kick_sum)
    return jnp.stack(outputs)
```

```python
import functools
import math

import jax
import jax.numpy as jnp
import ml_dtypes
import numpy as np
from jax import lax
from jax.experimental import pallas as pl
from jax.experimental.pallas import tpu as pltpu
from jax.sharding import PartitionSpec as P

GRID = 256
HALF = GRID // 2
STOPS = 4
OFFSET_CELLS = 32
BANDS = GRID // OFFSET_CELLS
REACH = STOPS + 1
f32 = jnp.float32
bf16 = jnp.bfloat16


def split_table(table):
    high = table.astype(ml_dtypes.bfloat16)
    low = (table - high.astype(np.float64)).astype(ml_dtypes.bfloat16)
    return np.stack([high, low])


@functools.cache
def make_tables():
    cells = np.arange(GRID)
    wave = np.where(cells <= HALF, cells, cells - HALF)
    is_sin = cells > HALF
    angle = 2 * np.pi * ((cells[:, None] * wave[None, :]) % GRID) / GRID
    basis = np.where(is_sin[None, :], np.sin(angle), np.cos(angle))
    slope = -0.5 * (np.roll(basis, -1, 0) - np.roll(basis, 1, 0))
    order = OFFSET_CELLS * (cells % BANDS) + cells // BANDS
    here = (cells[None, :] == wave[:, None]).astype(np.float64)
    there = (cells[None, :] == (-wave[:, None]) % GRID).astype(np.float64)
    count = np.where((wave == 0) | (wave == HALF), 1.0, 2.0)[:, None] / GRID
    sign = np.where(is_sin, -1.0, 1.0)[:, None]
    even = 0.5 * (here + there) * count
    odd = 0.5 * (here - there) * count
    tables = np.stack(
        [
            split_table(basis.T),
            split_table(basis),
            split_table(slope.T),
            split_table(basis[order]),
            split_table(slope[order]),
        ]
    )
    mixers = np.stack([even, even, odd * sign, -odd * sign]).astype(ml_dtypes.bfloat16)
    return tables, mixers


def dot(a, b):
    return jnp.dot(a, b, preferred_element_type=f32)


def dot_nt(a, b):
    return lax.dot_general(a, b, (((1,), (1,)), ((), ())), preferred_element_type=f32)


def halves(x):
    high = x.astype(bf16)
    return high, (x - high.astype(f32)).astype(bf16)


def pack_kernel(cells, charges, fill, marks, gains, strengths, out, first, second):
    for beam in range(2):
        parts = [
            charges[beam].astype(f32) * fill[beam, 0].astype(f32),
            cells[beam, 0, 0:1, :].astype(f32),
            cells[beam, 0, 1:2, :].astype(f32),
        ]
        width = parts[0].shape[1] // 8
        weights = []
        for offset in range(1, REACH):
            stop = offset - 1
            mark = marks[stop, beam, 0, 0].astype(f32)
            weights.append(gains[stop] * strengths[stop] * mark)
        for offset in range(STOPS - 1):
            stop = offset + 1
            mark = marks[stop, beam, 1, 0].astype(f32)
            weights.append(gains[stop] * strengths[stop] * mark)
        weights.append(jnp.float32(0))
        own = first if beam == 0 else second
        for row, value in enumerate(parts):
            out[4 * beam + row : 4 * beam + row + 1, :] = value
            own[row : row + 1, :] = value
        for group, weight in enumerate(weights):
            value = jnp.full((1, width), weight, f32)
            out[4 * beam + 3 : 4 * beam + 4, group * width : (group + 1) * width] = value
            own[3:4, group * width : (group + 1) * width] = value


def field_kernel(tiles, index, *refs):
    packs = refs[:tiles]
    greens = refs[tiles : 2 * tiles]
    tables, mixers, out = refs[2 * tiles :]
    columns = greens[0].shape[1]
    gains = []
    for which in (0, 2):
        total = jnp.zeros((GRID, GRID), f32)
        for step in range(tiles):
            owner = lax.rem(index[0] - step + tiles, tiles)
            start = pl.multiple_of(owner * columns, columns)
            high, low = halves(greens[step][...])
            rest = greens[step][...] - high.astype(f32) - low.astype(f32)
            pieces = (high, low, rest.astype(bf16))
            left = mixers[which + 1]
            turned = sum(dot(left, piece) for piece in pieces)
            high, low = halves(turned)
            last = (turned - high.astype(f32) - low.astype(f32)).astype(bf16)
            columns_side = mixers[4 + which // 2, pl.ds(start, columns), :]
            for piece in (high, low, last):
                total = total + lax.dot_general(
                    columns_side, piece, (((0,), (1,)), ((), ())), preferred_element_type=f32
                )
        gains.append(total)
    alpha, beta = gains
    particles = packs[0].shape[1]
    cells = lax.broadcasted_iota(jnp.int32, (GRID, particles), 0).astype(f32)
    for beam in range(2):
        density = jnp.zeros((GRID, GRID), f32)
        for step in range(tiles):
            base = 4 * beam
            charge = packs[step][base : base + 1, :]
            rows = packs[step][base + 1 : base + 2, :]
            cols = packs[step][base + 2 : base + 3, :]
            row_hot = jnp.where(cells == rows, 1.0, 0.0).astype(bf16)
            col_hot = jnp.where(cells == cols, charge, 0.0).astype(bf16)
            density = density + dot_nt(col_hot, row_hot)
        high, low = halves(density)
        first = dot(tables[0, 0], high) + dot(tables[0, 0], low) + dot(tables[0, 1], high)
        high, low = halves(first)
        spectrum = dot(high, tables[1, 0]) + dot(low, tables[1, 0]) + dot(high, tables[1, 1])
        swapped = jnp.concatenate(
            [
                jnp.concatenate([spectrum[HALF:, HALF:], spectrum[HALF:, :HALF]], axis=1),
                jnp.concatenate([spectrum[:HALF, HALF:], spectrum[:HALF, :HALF]], axis=1),
            ],
            axis=0,
        )
        scaled = alpha * spectrum + beta * swapped
        high, low = halves(scaled)
        for axis, (inner, outer) in enumerate(((2, 3), (0, 4))):
            part = (
                dot(high, tables[inner, 0])
                + dot(low, tables[inner, 0])
                + dot(high, tables[inner, 1])
            )
            top, bottom = halves(part)
            field = (
                dot(tables[outer, 0], top) + dot(tables[outer, 0], bottom) + dot(tables[outer, 1], top)
            )
            out[beam, axis * GRID : (axis + 1) * GRID, :] = field.astype(bf16)


def kick_kernel(count, index, gains, *refs):
    fields = refs[0]
    queries = (refs[1 : 1 + REACH], refs[1 + REACH : 1 + 2 * REACH])
    out = refs[1 + 2 * REACH]
    particles = queries[0][0].shape[1]
    width = particles // 8
    here = index[0]
    block = 2 * width
    cells = lax.broadcasted_iota(jnp.int32, (GRID, block), 0).astype(f32)
    bands = lax.broadcasted_iota(jnp.int32, (BANDS, block), 0).astype(f32)
    for offset in reversed(range(REACH)):
        for beam in range(2):
            sign = 1 if beam == 0 else -1
            target = lax.rem(here - sign * offset + count, count)
            source = queries[beam][offset]
            middle = gains[offset] if offset < STOPS else None
            up = source[3:4, (offset - 1) * width : offset * width] if offset else None
            down = source[3:4, (offset + 4) * width : (offset + 5) * width] if offset < STOPS - 1 else None
            for start in range(0, particles, block):
                rows = source[1:2, start : start + block]
                cols = source[2:3, start : start + block]
                band = jnp.floor(cols * (1.0 / OFFSET_CELLS))
                inside = cols - band * OFFSET_CELLS
                hot = jnp.where(cells == rows, 1.0, 0.0).astype(bf16)
                values = dot(fields[1 - beam], hot)
                picked = [jnp.zeros((BANDS, block), f32) for _ in range(2)]
                for place in range(OFFSET_CELLS):
                    hit = jnp.broadcast_to(inside == place, (BANDS, block))
                    for axis in range(2):
                        at = axis * GRID + place * BANDS
                        picked[axis] = jnp.where(hit, values[at : at + BANDS, :], picked[axis])
                weight = jnp.zeros((BANDS, block), f32)
                if middle is not None:
                    weight = jnp.where(bands == band, middle, weight)
                if up is not None:
                    weight = jnp.where(bands == band - 1, jnp.concatenate([up, up], axis=1), weight)
                if down is not None:
                    weight = jnp.where(bands == band + 1, jnp.concatenate([down, down], axis=1), weight)
                for axis in range(2):
                    kick = jnp.sum(weight * picked[axis], axis=0, keepdims=True)
                    out[target, 2 * beam + axis : 2 * beam + axis + 1, start : start + block] = kick


def final_kernel(count, index, received, momenta, out):
    here = index[0]
    for beam in range(2):
        sign = 1 if beam == 0 else -1
        for axis in range(2):
            total = None
            for offset in range(REACH):
                source = lax.rem(here + sign * offset + count, count)
                part = received[source, 2 * beam + axis : 2 * beam + axis + 1, :]
                total = part if total is None else total + part
            out[beam, 0, axis : axis + 1, :] = momenta[beam, 0, axis : axis + 1, :] + total.astype(
                bf16
            ).astype(f32)


SMEM = pl.BlockSpec(memory_space=pltpu.SMEM)
VMEM = pl.BlockSpec(memory_space=pltpu.VMEM)
LIMIT = pltpu.CompilerParams(vmem_limit_bytes=48 * 1024 * 1024)


def shifted(value, axis, steps):
    count = lax.axis_size(axis)
    return lax.ppermute(value, axis, [(i, (i + steps) % count) for i in range(count)])


def body(cell_index, charges, momenta, fill_pattern, encounters, green_spectrum, stop_gain, parasitic_gain):
    particles = cell_index.shape[3]
    tiles = lax.axis_size("tile")
    count = lax.axis_size("bunch")
    tables, mixers = make_tables()
    mixers = np.concatenate([mixers, np.stack([mixers[0].T, mixers[2].T])])
    bunch = lax.axis_index("bunch").astype(jnp.int32).reshape(1)
    tile = lax.axis_index("tile").astype(jnp.int32).reshape(1)
    pack, first, second = pl.pallas_call(
        pack_kernel,
        out_shape=(
            jax.ShapeDtypeStruct((8, particles), f32),
            jax.ShapeDtypeStruct((4, particles), f32),
            jax.ShapeDtypeStruct((4, particles), f32),
        ),
        in_specs=[VMEM, VMEM, SMEM, SMEM, SMEM, SMEM],
        out_specs=(VMEM, VMEM, VMEM),
    )(cell_index, charges, fill_pattern, encounters, stop_gain, parasitic_gain)
    packs = [pack] + [shifted(pack, "tile", step) for step in range(1, tiles)]
    greens = [green_spectrum] + [shifted(green_spectrum, "tile", step) for step in range(1, tiles)]
    from_first = [first] + [shifted(first, "bunch", offset) for offset in range(1, REACH)]
    from_second = [second] + [shifted(second, "bunch", -offset) for offset in range(1, REACH)]
    fields = pl.pallas_call(
        functools.partial(field_kernel, tiles),
        out_shape=jax.ShapeDtypeStruct((2, 2 * GRID, GRID), bf16),
        in_specs=[SMEM] + [VMEM] * (2 * tiles + 2),
        out_specs=VMEM,
        compiler_params=LIMIT,
    )(tile, *packs, *greens, jnp.asarray(tables), jnp.asarray(mixers))
    kicks = pl.pallas_call(
        functools.partial(kick_kernel, count),
        out_shape=jax.ShapeDtypeStruct((count, 4, particles), f32),
        in_specs=[SMEM, SMEM] + [VMEM] * (1 + 2 * REACH),
        out_specs=VMEM,
        compiler_params=LIMIT,
    )(bunch, stop_gain, fields, *from_first, *from_second)
    received = lax.all_to_all(kicks, "bunch", split_axis=0, concat_axis=0, tiled=True)
    return pl.pallas_call(
        functools.partial(final_kernel, count),
        out_shape=jax.ShapeDtypeStruct(momenta.shape, f32),
        in_specs=[SMEM, VMEM, VMEM],
        out_specs=VMEM,
    )(bunch, received, momenta)


def solution(mesh):
    in_specs = (
        P(None, "bunch", None, "tile"),
        P(None, "bunch", "tile"),
        P(None, "bunch", None, "tile"),
        P(None, "bunch"),
        P(None, None, None, "bunch"),
        P(None, "tile"),
        P(),
        P(),
    )
    out_specs = P(None, "bunch", None, "tile")
    return jax.shard_map(body, mesh=mesh, in_specs=in_specs, out_specs=out_specs, check_vma=False)
```

```python
import functools
import math

import jax
import jax.numpy as jnp
import ml_dtypes
import numpy as np
from jax import lax
from jax.experimental import pallas as pl
from jax.experimental.pallas import tpu as pltpu
from jax.sharding import PartitionSpec as P

GRID = 256
HALF = GRID // 2
STOPS = 4
OFFSET_CELLS = 32
BANDS = GRID // OFFSET_CELLS
REACH = STOPS + 1
f32 = jnp.float32
bf16 = jnp.bfloat16


def split_table(table):
    high = table.astype(ml_dtypes.bfloat16)
    low = (table - high.astype(np.float64)).astype(ml_dtypes.bfloat16)
    return np.stack([high, low])


@functools.cache
def make_tables():
    cells = np.arange(GRID)
    wave = np.where(cells <= HALF, cells, cells - HALF)
    is_sin = cells > HALF
    angle = 2 * np.pi * ((cells[:, None] * wave[None, :]) % GRID) / GRID
    basis = np.where(is_sin[None, :], np.sin(angle), np.cos(angle))
    slope = -0.5 * (np.roll(basis, -1, 0) - np.roll(basis, 1, 0))
    order = OFFSET_CELLS * (cells % BANDS) + cells // BANDS
    here = (cells[None, :] == wave[:, None]).astype(np.float64)
    there = (cells[None, :] == (-wave[:, None]) % GRID).astype(np.float64)
    count = np.where((wave == 0) | (wave == HALF), 1.0, 2.0)[:, None] / GRID
    sign = np.where(is_sin, -1.0, 1.0)[:, None]
    even = 0.5 * (here + there) * count
    odd = 0.5 * (here - there) * count
    tables = np.stack(
        [
            split_table(basis.T),
            split_table(basis),
            split_table(slope.T),
            split_table(basis[order]),
            split_table(slope[order]),
        ]
    )
    mixers = np.stack([even, even.T, odd * sign, -(odd * sign).T]).astype(ml_dtypes.bfloat16)
    return np.concatenate([tables.reshape(-1, GRID, GRID), mixers])


def dot(a, b):
    return jnp.dot(a, b, preferred_element_type=f32)


def dot_nt(a, b):
    return lax.dot_general(a, b, (((1,), (1,)), ((), ())), preferred_element_type=f32)


def halves(x):
    high = x.astype(bf16)
    return high, (x - high.astype(f32)).astype(bf16)


def product(a, b):
    return dot(a[0], b[0]) + dot(a[0], b[1]) + dot(a[1], b[0])


def pack_kernel(cells, charges, fill, marks, green, out, copies, thin):
    particles = charges.shape[1]
    width = particles // 8
    for beam in range(2):
        rows = [
            charges[beam : beam + 1, :].astype(f32) * fill[0, beam].astype(f32),
            cells[beam, 0, 0:1, :].astype(f32),
            cells[beam, 0, 1:2, :].astype(f32),
        ]
        group = lax.broadcasted_iota(jnp.int32, (1, particles), 1) // width
        mark = jnp.zeros((1, particles), f32)
        for offset in range(1, REACH):
            mark = jnp.where(group == offset - 1, marks[beam, 0, 0, offset - 1].astype(f32), mark)
        for offset in range(STOPS - 1):
            mark = jnp.where(group == STOPS + offset, marks[beam, 1, 0, offset + 1].astype(f32), mark)
        rows.append(mark)
        for row, value in enumerate(rows):
            out[4 * beam + row : 4 * beam + row + 1, :] = value.astype(bf16)
    for copy in range(copies.shape[0]):
        copies[copy] = out[...]
    thin[...] = green[...].astype(bf16)


def field_kernel(tiles, index, *refs):
    packs = refs[1:tiles]
    greens = refs[tiles + 1 : 2 * tiles]
    far, out, near, own, gathered, arrived = refs[2 * tiles :]
    columns = greens[0].shape[0]
    places = [
        pl.ds(pl.multiple_of(relative(index[0], step, tiles) * columns, columns), columns)
        for step in range(tiles)
    ]
    fetch = [
        pltpu.make_async_copy(refs[0], own, arrived.at[0]),
        pltpu.make_async_copy(refs[tiles], gathered.at[places[0], :], arrived.at[1]),
        pltpu.make_async_copy(far, near, arrived.at[2]),
    ]
    for copy in fetch:
        copy.start()
    for step in range(1, tiles):
        gathered[places[step], :] = greens[step - 1][...]
    particles = packs[0].shape[1]
    cells = lax.broadcasted_iota(jnp.int32, (GRID, particles), 0).astype(f32)
    densities = [jnp.zeros((GRID, GRID), f32) for _ in range(2)]
    for pack in (*packs, own):
        if pack is own:
            fetch[0].wait()
        for beam in range(2):
            base = 4 * beam
            charge = pack[base : base + 1, :].astype(f32)
            rows = pack[base + 1 : base + 2, :].astype(f32)
            cols = pack[base + 2 : base + 3, :].astype(f32)
            row_hot = jnp.where(cells == rows, 1.0, 0.0).astype(bf16)
            col_hot = jnp.where(cells == cols, charge, 0.0).astype(bf16)
            densities[beam] = densities[beam] + dot_nt(col_hot, row_hot)
    densities = [halves(density) for density in densities]
    fetch[1].wait()
    fetch[2].wait()
    tables = [(near[2 * which], near[2 * which + 1]) for which in range(5)]
    mixers = [near[10 + which] for which in range(4)]
    alpha, beta = (
        dot(mixers[side], turned[0]) + dot(mixers[side], turned[1])
        for side, turned in (
            (side, halves(dot(gathered[...], mixers[side + 1]))) for side in (0, 2)
        )
    )
    for beam in range(2):
        first = halves(product(tables[0], densities[beam]))
        spectrum = product(first, tables[1])
        swapped = jnp.concatenate(
            [
                jnp.concatenate([spectrum[HALF:, HALF:], spectrum[HALF:, :HALF]], axis=1),
                jnp.concatenate([spectrum[:HALF, HALF:], spectrum[:HALF, :HALF]], axis=1),
            ],
            axis=0,
        )
        scaled = halves(alpha * spectrum + beta * swapped)
        for axis, (inner, outer) in enumerate(((2, 3), (0, 4))):
            part = halves(product(scaled, tables[inner]))
            field = product(tables[outer], part)
            out[beam, axis * GRID : (axis + 1) * GRID, :] = field.astype(bf16)


def kick_kernel(count, index, gains, strengths, fields, queries, out):
    particles = queries.shape[2]
    width = particles // 8
    here = index[0]
    block = 2 * width
    cells = lax.broadcasted_iota(jnp.int32, (GRID, block), 0).astype(f32)
    bands = lax.broadcasted_iota(jnp.int32, (BANDS, block), 0).astype(f32)
    for offset in reversed(range(REACH)):
        for beam in range(2):
            sign = 1 if beam == 0 else -1
            target = lax.rem(here - sign * offset + count, count)
            source = queries.at[target]
            base = 4 * beam

            def weight_of(stop, group):
                mark = source[base + 3 : base + 4, group * width : (group + 1) * width].astype(f32)
                mark = mark * (gains[stop] * strengths[stop])
                return jnp.concatenate([mark, mark], axis=1)

            middle = gains[offset] if offset < STOPS else None
            up = weight_of(offset - 1, offset - 1) if offset else None
            down = weight_of(offset + 1, STOPS + offset) if offset < STOPS - 1 else None
            for start in range(0, particles, block):
                rows = source[base + 1 : base + 2, start : start + block].astype(f32)
                cols = source[base + 2 : base + 3, start : start + block].astype(f32)
                band = jnp.floor(cols * (1.0 / OFFSET_CELLS))
                inside = cols - band * OFFSET_CELLS
                hot = jnp.where(cells == rows, 1.0, 0.0).astype(bf16)
                values = dot(fields[1 - beam], hot)
                picked = [jnp.zeros((BANDS, block), f32) for _ in range(2)]
                for place in range(OFFSET_CELLS):
                    hit = jnp.broadcast_to(inside == place, (BANDS, block))
                    for axis in range(2):
                        at = axis * GRID + place * BANDS
                        picked[axis] = jnp.where(hit, values[at : at + BANDS, :], picked[axis])
                weight = jnp.zeros((BANDS, block), f32)
                if middle is not None:
                    weight = jnp.where(bands == band, middle, weight)
                if up is not None:
                    weight = jnp.where(bands == band - 1, up, weight)
                if down is not None:
                    weight = jnp.where(bands == band + 1, down, weight)
                for axis in range(2):
                    kick = jnp.sum(weight * picked[axis], axis=0, keepdims=True)
                    out[target, 2 * beam + axis : 2 * beam + axis + 1, start : start + block] = kick


def final_kernel(count, index, received, momenta, out):
    here = index[0]
    for beam in range(2):
        sign = 1 if beam == 0 else -1
        for axis in range(2):
            total = None
            for offset in range(REACH):
                source = lax.rem(here + sign * offset + count, count)
                part = received[source, 2 * beam + axis : 2 * beam + axis + 1, :]
                total = part if total is None else total + part
            out[beam, 0, axis : axis + 1, :] = momenta[beam, 0, axis : axis + 1, :] + total.astype(
                bf16
            ).astype(f32)


SMEM = pl.BlockSpec(memory_space=pltpu.SMEM)
VMEM = pl.BlockSpec(memory_space=pltpu.VMEM)
FAR = pl.BlockSpec(memory_space=pltpu.HBM)
LIMIT = pltpu.CompilerParams(vmem_limit_bytes=48 * 1024 * 1024)
SMALL = pltpu.CompilerParams(vmem_limit_bytes=16 * 1024 * 1024)


def kept_far(value):
    return pltpu.with_memory_space_constraint(value, pltpu.HBM)


def is_power_of_two(count):
    return count & (count - 1) == 0


def relative(index, step, count):
    if is_power_of_two(count):
        return jnp.bitwise_xor(index, step)
    return lax.rem(index - step + count, count)


def exchanged(value, axis, step):
    count = lax.axis_size(axis)
    if is_power_of_two(count):
        pairs = [(i, i ^ step) for i in range(count)]
    else:
        pairs = [(i, (i + step) % count) for i in range(count)]
    return lax.ppermute(value, axis, pairs)


def body(cell_index, charges, momenta, fill_pattern, encounters, green_spectrum, stop_gain, parasitic_gain):
    particles = cell_index.shape[3]
    tiles = lax.axis_size("tile")
    count = lax.axis_size("bunch")
    tables = make_tables()
    bunch = lax.axis_index("bunch").astype(jnp.int32).reshape(1)
    tile = lax.axis_index("tile").astype(jnp.int32).reshape(1)
    columns = green_spectrum.shape[1]
    pack, copies, thin = pl.pallas_call(
        pack_kernel,
        out_shape=(
            jax.ShapeDtypeStruct((8, particles), bf16),
            jax.ShapeDtypeStruct((count, 8, particles), bf16),
            jax.ShapeDtypeStruct((columns, GRID), bf16),
        ),
        in_specs=[VMEM, VMEM, SMEM, SMEM, VMEM],
        out_specs=(VMEM, VMEM, VMEM),
        compiler_params=SMALL,
    )(
        kept_far(cell_index),
        kept_far(charges.reshape(2, particles)),
        kept_far(fill_pattern.T),
        kept_far(jnp.transpose(encounters, (1, 2, 3, 0))),
        kept_far(green_spectrum.T),
    )
    packs = [pack] + [exchanged(pack, "tile", step) for step in range(1, tiles)]
    greens = [thin] + [exchanged(thin, "tile", step) for step in range(1, tiles)]
    queries = lax.all_to_all(copies, "bunch", split_axis=0, concat_axis=0, tiled=True)
    fields = pl.pallas_call(
        functools.partial(field_kernel, tiles),
        out_shape=jax.ShapeDtypeStruct((2, 2 * GRID, GRID), bf16),
        in_specs=[SMEM] + ([FAR] + [VMEM] * (tiles - 1)) * 2 + [FAR],
        out_specs=VMEM,
        scratch_shapes=[
            pltpu.VMEM(tables.shape, bf16),
            pltpu.VMEM(pack.shape, bf16),
            pltpu.VMEM((GRID, GRID), bf16),
            pltpu.SemaphoreType.DMA((3,)),
        ],
        compiler_params=LIMIT,
    )(tile, *packs, *greens, kept_far(jnp.asarray(tables)))
    kicks = pl.pallas_call(
        functools.partial(kick_kernel, count),
        out_shape=jax.ShapeDtypeStruct((count, 4, particles), f32),
        in_specs=[SMEM, SMEM, SMEM, VMEM, VMEM],
        out_specs=VMEM,
        compiler_params=LIMIT,
    )(bunch, stop_gain, parasitic_gain, fields, queries)
    received = lax.all_to_all(kicks, "bunch", split_axis=0, concat_axis=0, tiled=True)
    return pl.pallas_call(
        functools.partial(final_kernel, count),
        out_shape=jax.ShapeDtypeStruct(momenta.shape, f32),
        in_specs=[SMEM, VMEM, VMEM],
        out_specs=VMEM,
        compiler_params=SMALL,
    )(bunch, received, momenta)


def solution(mesh):
    in_specs = (
        P(None, "bunch", None, "tile"),
        P(None, "bunch", "tile"),
        P(None, "bunch", None, "tile"),
        P(None, "bunch"),
        P(None, None, None, "bunch"),
        P(None, "tile"),
        P(),
        P(),
    )
    out_specs = P(None, "bunch", None, "tile")
    return jax.shard_map(body, mesh=mesh, in_specs=in_specs, out_specs=out_specs, check_vma=False)
```

```python
import functools
import math

import jax
import jax.numpy as jnp
import ml_dtypes
import numpy as np
from jax import lax
from jax.experimental import pallas as pl
from jax.experimental.pallas import tpu as pltpu
from jax.sharding import PartitionSpec as P

GRID = 256
HALF = GRID // 2
STOPS = 4
OFFSET_CELLS = 32
BANDS = GRID // OFFSET_CELLS
REACH = STOPS + 1
f32 = jnp.float32
bf16 = jnp.bfloat16


def split_table(table):
    high = table.astype(ml_dtypes.bfloat16)
    low = (table - high.astype(np.float64)).astype(ml_dtypes.bfloat16)
    return np.stack([high, low])


@functools.cache
def make_tables():
    cells = np.arange(GRID)
    wave = np.where(cells <= HALF, cells, cells - HALF)
    is_sin = cells > HALF
    angle = 2 * np.pi * ((cells[:, None] * wave[None, :]) % GRID) / GRID
    basis = np.where(is_sin[None, :], np.sin(angle), np.cos(angle))
    slope = -0.5 * (np.roll(basis, -1, 0) - np.roll(basis, 1, 0))
    order = OFFSET_CELLS * (cells % BANDS) + cells // BANDS
    here = (cells[None, :] == wave[:, None]).astype(np.float64)
    there = (cells[None, :] == (-wave[:, None]) % GRID).astype(np.float64)
    count = np.where((wave == 0) | (wave == HALF), 1.0, 2.0)[:, None] / GRID
    sign = np.where(is_sin, -1.0, 1.0)[:, None]
    even = 0.5 * (here + there) * count
    odd = 0.5 * (here - there) * count
    tables = np.stack(
        [
            split_table(basis.T),
            split_table(basis),
            split_table(slope.T),
            split_table(basis[order]),
            split_table(slope[order]),
        ]
    )
    mixers = np.stack([even, even.T, odd * sign, -(odd * sign).T]).astype(ml_dtypes.bfloat16)
    return np.concatenate([tables.reshape(-1, GRID, GRID), mixers])


def dot(a, b):
    return jnp.dot(a, b, preferred_element_type=f32)


def dot_nt(a, b):
    return lax.dot_general(a, b, (((1,), (1,)), ((), ())), preferred_element_type=f32)


def halves(x):
    high = x.astype(bf16)
    return high, (x - high.astype(f32)).astype(bf16)


def product(a, b):
    return dot(a[0], b[0]) + dot(a[0], b[1]) + dot(a[1], b[0])


def pack_kernel(cells, charges, fill, marks, green, out, copies, message):
    particles = charges.shape[1]
    width = particles // 8
    for beam in range(2):
        rows = [
            charges[beam : beam + 1, :].astype(f32) * fill[0, beam].astype(f32),
            cells[beam, 0, 0:1, :].astype(f32),
            cells[beam, 0, 1:2, :].astype(f32),
        ]
        group = lax.broadcasted_iota(jnp.int32, (1, particles), 1) // width
        mark = jnp.zeros((1, particles), f32)
        for offset in range(1, REACH):
            mark = jnp.where(group == offset - 1, marks[beam, 0, 0, offset - 1].astype(f32), mark)
        for offset in range(STOPS - 1):
            mark = jnp.where(group == STOPS + offset, marks[beam, 1, 0, offset + 1].astype(f32), mark)
        rows.append(mark)
        for row, value in enumerate(rows):
            out[4 * beam + row : 4 * beam + row + 1, :] = value.astype(bf16)
    for copy in range(copies.shape[0]):
        copies[copy] = out[...]
    lists = 8 * particles // GRID
    for part in range(particles // GRID):
        message[8 * part : 8 * part + 8, :] = out[:, part * GRID : (part + 1) * GRID]
    message[lists:, :] = green[...].astype(bf16)


def field_kernel(tiles, index, *refs):
    messages = refs[:tiles]
    far, out, near, gathered, arrived = refs[tiles:]
    fetch = pltpu.make_async_copy(far, near, arrived)
    fetch.start()
    lists = messages[0].shape[0] - GRID // tiles
    columns = GRID // tiles
    for step in range(tiles):
        start = pl.multiple_of(relative(index[0], step, tiles) * columns, columns)
        gathered[pl.ds(start, columns), :] = messages[step][lists:, :]
    cells = lax.broadcasted_iota(jnp.int32, (GRID, GRID), 0).astype(f32)
    densities = [jnp.zeros((GRID, GRID), f32) for _ in range(2)]
    for message in messages:
        for beam in range(2):
            row_hots, col_hots = [], []
            for part in range(lists // 8):
                base = 8 * part + 4 * beam
                charge = message[base : base + 1, :].astype(f32)
                rows = message[base + 1 : base + 2, :].astype(f32)
                cols = message[base + 2 : base + 3, :].astype(f32)
                row_hots.append(jnp.where(cells == rows, 1.0, 0.0).astype(bf16))
                col_hots.append(jnp.where(cells == cols, charge, 0.0).astype(bf16))
            densities[beam] = densities[beam] + dot_nt(
                jnp.concatenate(col_hots, axis=1), jnp.concatenate(row_hots, axis=1)
            )
    densities = [halves(density) for density in densities]
    fetch.wait()
    tables = [(near[2 * which], near[2 * which + 1]) for which in range(5)]
    mixers = [near[10 + which] for which in range(4)]
    alpha, beta = (
        dot(mixers[side], turned[0]) + dot(mixers[side], turned[1])
        for side, turned in (
            (side, halves(dot(gathered[...], mixers[side + 1]))) for side in (0, 2)
        )
    )
    for beam in range(2):
        first = halves(product(tables[0], densities[beam]))
        spectrum = product(first, tables[1])
        swapped = jnp.concatenate(
            [
                jnp.concatenate([spectrum[HALF:, HALF:], spectrum[HALF:, :HALF]], axis=1),
                jnp.concatenate([spectrum[:HALF, HALF:], spectrum[:HALF, :HALF]], axis=1),
            ],
            axis=0,
        )
        scaled = halves(alpha * spectrum + beta * swapped)
        for axis, (inner, outer) in enumerate(((2, 3), (0, 4))):
            part = halves(product(scaled, tables[inner]))
            field = product(tables[outer], part)
            out[beam, axis * GRID : (axis + 1) * GRID, :] = field.astype(bf16)


def kick_kernel(count, index, gains, strengths, fields, queries, out):
    particles = queries.shape[2]
    width = particles // 8
    here = index[0]
    block = 2 * width
    cells = lax.broadcasted_iota(jnp.int32, (GRID, block), 0).astype(f32)
    bands = lax.broadcasted_iota(jnp.int32, (BANDS, block), 0).astype(f32)
    for offset in reversed(range(REACH)):
        for beam in range(2):
            sign = 1 if beam == 0 else -1
            target = lax.rem(here - sign * offset + count, count)
            source = queries.at[target]
            base = 4 * beam

            def weight_of(stop, group):
                mark = source[base + 3 : base + 4, group * width : (group + 1) * width].astype(f32)
                mark = mark * (gains[stop] * strengths[stop])
                return jnp.concatenate([mark, mark], axis=1)

            middle = gains[offset] if offset < STOPS else None
            up = weight_of(offset - 1, offset - 1) if offset else None
            down = weight_of(offset + 1, STOPS + offset) if offset < STOPS - 1 else None
            for start in range(0, particles, block):
                rows = source[base + 1 : base + 2, start : start + block].astype(f32)
                cols = source[base + 2 : base + 3, start : start + block].astype(f32)
                band = jnp.floor(cols * (1.0 / OFFSET_CELLS))
                inside = cols - band * OFFSET_CELLS
                hot = jnp.where(cells == rows, 1.0, 0.0).astype(bf16)
                values = dot(fields[1 - beam], hot)
                picked = [jnp.zeros((BANDS, block), f32) for _ in range(2)]
                for place in range(OFFSET_CELLS):
                    hit = jnp.broadcast_to(inside == place, (BANDS, block))
                    for axis in range(2):
                        at = axis * GRID + place * BANDS
                        picked[axis] = jnp.where(hit, values[at : at + BANDS, :], picked[axis])
                weight = jnp.zeros((BANDS, block), f32)
                if middle is not None:
                    weight = jnp.where(bands == band, middle, weight)
                if up is not None:
                    weight = jnp.where(bands == band - 1, up, weight)
                if down is not None:
                    weight = jnp.where(bands == band + 1, down, weight)
                for axis in range(2):
                    kick = jnp.sum(weight * picked[axis], axis=0, keepdims=True)
                    out[target, 2 * beam + axis : 2 * beam + axis + 1, start : start + block] = kick


def final_kernel(count, index, received, momenta, out):
    here = index[0]
    for beam in range(2):
        sign = 1 if beam == 0 else -1
        for axis in range(2):
            total = None
            for offset in range(REACH):
                source = lax.rem(here + sign * offset + count, count)
                part = received[source, 2 * beam + axis : 2 * beam + axis + 1, :]
                total = part if total is None else total + part
            out[beam, 0, axis : axis + 1, :] = momenta[beam, 0, axis : axis + 1, :] + total.astype(
                bf16
            ).astype(f32)


SMEM = pl.BlockSpec(memory_space=pltpu.SMEM)
VMEM = pl.BlockSpec(memory_space=pltpu.VMEM)
FAR = pl.BlockSpec(memory_space=pltpu.HBM)
LIMIT = pltpu.CompilerParams(vmem_limit_bytes=48 * 1024 * 1024)
SMALL = pltpu.CompilerParams(vmem_limit_bytes=16 * 1024 * 1024)


def kept_far(value):
    return pltpu.with_memory_space_constraint(value, pltpu.HBM)


def is_power_of_two(count):
    return count & (count - 1) == 0


def relative(index, step, count):
    if is_power_of_two(count):
        return jnp.bitwise_xor(index, step)
    return lax.rem(index - step + count, count)


def exchanged(value, axis, step):
    count = lax.axis_size(axis)
    if is_power_of_two(count):
        pairs = [(i, i ^ step) for i in range(count)]
    else:
        pairs = [(i, (i + step) % count) for i in range(count)]
    return lax.ppermute(value, axis, pairs)


def body(cell_index, charges, momenta, fill_pattern, encounters, green_spectrum, stop_gain, parasitic_gain):
    particles = cell_index.shape[3]
    tiles = lax.axis_size("tile")
    count = lax.axis_size("bunch")
    tables = make_tables()
    bunch = lax.axis_index("bunch").astype(jnp.int32).reshape(1)
    tile = lax.axis_index("tile").astype(jnp.int32).reshape(1)
    columns = green_spectrum.shape[1]
    pack, copies, message = pl.pallas_call(
        pack_kernel,
        out_shape=(
            jax.ShapeDtypeStruct((8, particles), bf16),
            jax.ShapeDtypeStruct((count, 8, particles), bf16),
            jax.ShapeDtypeStruct((8 * particles // GRID + columns, GRID), bf16),
        ),
        in_specs=[VMEM, VMEM, SMEM, SMEM, VMEM],
        out_specs=(VMEM, VMEM, VMEM),
        compiler_params=SMALL,
    )(
        kept_far(cell_index),
        kept_far(charges.reshape(2, particles)),
        kept_far(fill_pattern.T),
        kept_far(jnp.transpose(encounters, (1, 2, 3, 0))),
        kept_far(green_spectrum.T),
    )
    messages = [message] + [exchanged(message, "tile", step) for step in range(1, tiles)]
    queries = lax.all_to_all(copies, "bunch", split_axis=0, concat_axis=0, tiled=True)
    fields = pl.pallas_call(
        functools.partial(field_kernel, tiles),
        out_shape=jax.ShapeDtypeStruct((2, 2 * GRID, GRID), bf16),
        in_specs=[SMEM] + [VMEM] * tiles + [FAR],
        out_specs=VMEM,
        scratch_shapes=[
            pltpu.VMEM(tables.shape, bf16),
            pltpu.VMEM((GRID, GRID), bf16),
            pltpu.SemaphoreType.DMA,
        ],
        compiler_params=LIMIT,
        cost_estimate=pl.CostEstimate(flops=3000000000, bytes_accessed=1000000, transcendentals=0),
    )(tile, *messages, kept_far(jnp.asarray(tables)))
    kicks = pl.pallas_call(
        functools.partial(kick_kernel, count),
        out_shape=jax.ShapeDtypeStruct((count, 4, particles), f32),
        in_specs=[SMEM, SMEM, SMEM, VMEM, VMEM],
        out_specs=VMEM,
        compiler_params=LIMIT,
    )(bunch, stop_gain, parasitic_gain, fields, queries)
    received = lax.all_to_all(kicks, "bunch", split_axis=0, concat_axis=0, tiled=True)
    return pl.pallas_call(
        functools.partial(final_kernel, count),
        out_shape=jax.ShapeDtypeStruct(momenta.shape, f32),
        in_specs=[SMEM, VMEM, VMEM],
        out_specs=VMEM,
        compiler_params=SMALL,
    )(bunch, received, momenta)


def solution(mesh):
    in_specs = (
        P(None, "bunch", None, "tile"),
        P(None, "bunch", "tile"),
        P(None, "bunch", None, "tile"),
        P(None, "bunch"),
        P(None, None, None, "bunch"),
        P(None, "tile"),
        P(),
        P(),
    )
    out_specs = P(None, "bunch", None, "tile")
    return jax.shard_map(body, mesh=mesh, in_specs=in_specs, out_specs=out_specs, check_vma=False)
```

```python
import functools
import math

import jax
import jax.numpy as jnp
import ml_dtypes
import numpy as np
from jax import lax
from jax.experimental import pallas as pl
from jax.experimental.pallas import tpu as pltpu
from jax.sharding import PartitionSpec as P

GRID = 256
HALF = GRID // 2
STOPS = 4
OFFSET_CELLS = 32
BANDS = GRID // OFFSET_CELLS
REACH = STOPS + 1
f32 = jnp.float32
bf16 = jnp.bfloat16


def split_table(table):
    high = table.astype(ml_dtypes.bfloat16)
    low = (table - high.astype(np.float64)).astype(ml_dtypes.bfloat16)
    return np.stack([high, low])


@functools.cache
def make_tables():
    cells = np.arange(GRID)
    wave = np.where(cells <= HALF, cells, cells - HALF)
    is_sin = cells > HALF
    angle = 2 * np.pi * ((cells[:, None] * wave[None, :]) % GRID) / GRID
    basis = np.where(is_sin[None, :], np.sin(angle), np.cos(angle))
    slope = -0.5 * (np.roll(basis, -1, 0) - np.roll(basis, 1, 0))
    order = OFFSET_CELLS * (cells % BANDS) + cells // BANDS
    here = (cells[None, :] == wave[:, None]).astype(np.float64)
    there = (cells[None, :] == (-wave[:, None]) % GRID).astype(np.float64)
    count = np.where((wave == 0) | (wave == HALF), 1.0, 2.0)[:, None] / GRID
    sign = np.where(is_sin, -1.0, 1.0)[:, None]
    even = 0.5 * (here + there) * count
    odd = 0.5 * (here - there) * count
    mixers = np.stack([even, even.T, odd * sign, -(odd * sign).T])
    tables = [basis.T, basis, slope.T, basis[order], slope[order]]
    tables = [*(split_table(table) for table in tables), mixers]
    return np.concatenate([table.astype(ml_dtypes.bfloat16) for table in tables])


def dot(a, b):
    return jnp.dot(a, b, preferred_element_type=f32)


def dot_nt(a, b):
    return lax.dot_general(a, b, (((1,), (1,)), ((), ())), preferred_element_type=f32)


def halves(x):
    high = x.astype(bf16)
    return high, (x - high.astype(f32)).astype(bf16)


def wide(x, axis):
    high, low = halves(x)
    return jnp.concatenate([high, low, high], axis=axis)


def long(table, axis):
    return jnp.concatenate([table[0], table[0], table[1]], axis=axis)


def pack_kernel(cells, charges, fill, marks, green, out, copies, message):
    particles = charges.shape[1]
    width = particles // 8
    for beam in range(2):
        rows = [
            charges[beam : beam + 1, :].astype(f32) * fill[0, beam].astype(f32),
            cells[beam, 0, 0:1, :].astype(f32),
            cells[beam, 0, 1:2, :].astype(f32),
        ]
        group = lax.broadcasted_iota(jnp.int32, (1, particles), 1) // width
        mark = jnp.zeros((1, particles), f32)
        for offset in range(1, REACH):
            mark = jnp.where(group == offset - 1, marks[beam, 0, 0, offset - 1].astype(f32), mark)
        for offset in range(STOPS - 1):
            mark = jnp.where(group == STOPS + offset, marks[beam, 1, 0, offset + 1].astype(f32), mark)
        rows.append(mark)
        for row, value in enumerate(rows):
            out[4 * beam + row : 4 * beam + row + 1, :] = value.astype(bf16)
    for copy in range(copies.shape[0]):
        copies[copy] = out[...]
    lists = 8 * particles // GRID
    for part in range(particles // GRID):
        message[8 * part : 8 * part + 8, :] = out[:, part * GRID : (part + 1) * GRID]
    message[lists:, :] = green[...].astype(bf16)


def field_kernel(tiles, index, *refs):
    messages = refs[:tiles]
    far, out, near, gathered, arrived = refs[tiles:]
    fetch = pltpu.make_async_copy(far, near, arrived)
    fetch.start()
    lists = messages[0].shape[0] - GRID // tiles
    columns = GRID // tiles
    for step in range(tiles):
        start = pl.multiple_of(relative(index[0], step, tiles) * columns, columns)
        gathered[pl.ds(start, columns), :] = messages[step][lists:, :]
    cells = lax.broadcasted_iota(jnp.int32, (GRID, GRID), 0).astype(f32)
    densities = [jnp.zeros((GRID, GRID), f32) for _ in range(2)]
    for message in messages:
        for beam in range(2):
            row_hots, col_hots = [], []
            for part in range(lists // 8):
                base = 8 * part + 4 * beam
                charge = message[base : base + 1, :].astype(f32)
                rows = message[base + 1 : base + 2, :].astype(f32)
                cols = message[base + 2 : base + 3, :].astype(f32)
                row_hots.append(jnp.where(cells == rows, 1.0, 0.0).astype(bf16))
                col_hots.append(jnp.where(cells == cols, charge, 0.0).astype(bf16))
            densities[beam] = densities[beam] + dot_nt(
                jnp.concatenate(col_hots, axis=1), jnp.concatenate(row_hots, axis=1)
            )
    fetch.wait()
    alpha, beta = (
        dot(near[side], turned[0]) + dot(near[side], turned[1])
        for side, turned in (
            (side, halves(dot(gathered[...], near[side + 1]))) for side in (10, 12)
        )
    )
    first = dot(long(near[0:2], 1), wide(jnp.concatenate(densities, axis=1), 0))
    first = jnp.concatenate([first[:, :GRID], first[:, GRID:]], axis=0)
    spectra = dot(wide(first, 1), long(near[2:4], 0))
    scaled = []
    for beam in range(2):
        spectrum = spectra[beam * GRID : (beam + 1) * GRID]
        swapped = jnp.concatenate(
            [
                jnp.concatenate([spectrum[HALF:, HALF:], spectrum[HALF:, :HALF]], axis=1),
                jnp.concatenate([spectrum[:HALF, HALF:], spectrum[:HALF, :HALF]], axis=1),
            ],
            axis=0,
        )
        scaled.append(alpha * spectrum + beta * swapped)
    scaled = wide(jnp.concatenate(scaled, axis=0), 1)
    for axis, (inner, outer) in enumerate(((4, 6), (0, 8))):
        part = dot(scaled, long(near[inner : inner + 2], 0)).astype(bf16)
        part = jnp.concatenate([part[:GRID], part[GRID:]], axis=1)
        table = jnp.concatenate([near[outer], near[outer + 1]], axis=1)
        field = dot(table, jnp.concatenate([part, part], axis=0))
        for beam in range(2):
            out[beam, axis * GRID : (axis + 1) * GRID, :] = field[
                :, beam * GRID : (beam + 1) * GRID
            ].astype(bf16)


def kick_kernel(count, index, gains, strengths, fields, queries, out):
    particles = queries.shape[2]
    width = particles // 8
    here = index[0]
    block = 2 * width
    cells = lax.broadcasted_iota(jnp.int32, (GRID, block), 0).astype(f32)
    bands = lax.broadcasted_iota(jnp.int32, (BANDS, block), 0).astype(f32)
    for offset in reversed(range(REACH)):
        for beam in range(2):
            sign = 1 if beam == 0 else -1
            target = lax.rem(here - sign * offset + count, count)
            source = queries.at[target]
            base = 4 * beam

            def weight_of(stop, group):
                mark = source[base + 3 : base + 4, group * width : (group + 1) * width].astype(f32)
                mark = mark * (gains[stop] * strengths[stop])
                return jnp.concatenate([mark, mark], axis=1)

            middle = gains[offset] if offset < STOPS else None
            up = weight_of(offset - 1, offset - 1) if offset else None
            down = weight_of(offset + 1, STOPS + offset) if offset < STOPS - 1 else None
            for start in range(0, particles, block):
                rows = source[base + 1 : base + 2, start : start + block].astype(f32)
                cols = source[base + 2 : base + 3, start : start + block].astype(f32)
                band = jnp.floor(cols * (1.0 / OFFSET_CELLS))
                inside = jnp.broadcast_to(cols - band * OFFSET_CELLS, (BANDS, block))
                hot = jnp.where(cells == rows, 1.0, 0.0).astype(bf16)
                values = dot(fields[1 - beam], hot)
                picked = [jnp.zeros((BANDS, block), f32) for _ in range(2)]
                for place in range(OFFSET_CELLS):
                    hit = inside == place
                    for axis in range(2):
                        at = axis * GRID + place * BANDS
                        picked[axis] = jnp.where(hit, values[at : at + BANDS, :], picked[axis])
                weight = jnp.zeros((BANDS, block), f32)
                if middle is not None:
                    weight = jnp.where(bands == band, middle, weight)
                if up is not None:
                    weight = jnp.where(bands == band - 1, up, weight)
                if down is not None:
                    weight = jnp.where(bands == band + 1, down, weight)
                for axis in range(2):
                    kick = jnp.sum(weight * picked[axis], axis=0, keepdims=True)
                    out[target, 2 * beam + axis : 2 * beam + axis + 1, start : start + block] = kick


def final_kernel(count, index, received, momenta, out):
    here = index[0]
    for beam in range(2):
        sign = 1 if beam == 0 else -1
        for axis in range(2):
            total = None
            for offset in range(REACH):
                source = lax.rem(here + sign * offset + count, count)
                part = received[source, 2 * beam + axis : 2 * beam + axis + 1, :]
                total = part if total is None else total + part
            out[beam, 0, axis : axis + 1, :] = momenta[beam, 0, axis : axis + 1, :] + total.astype(
                bf16
            ).astype(f32)


SMEM = pl.BlockSpec(memory_space=pltpu.SMEM)
VMEM = pl.BlockSpec(memory_space=pltpu.VMEM)
FAR = pl.BlockSpec(memory_space=pltpu.HBM)
LIMIT = pltpu.CompilerParams(vmem_limit_bytes=48 * 1024 * 1024)
SMALL = pltpu.CompilerParams(vmem_limit_bytes=16 * 1024 * 1024)


def kept_far(value):
    return pltpu.with_memory_space_constraint(value, pltpu.HBM)


def is_power_of_two(count):
    return count & (count - 1) == 0


def relative(index, step, count):
    if is_power_of_two(count):
        return jnp.bitwise_xor(index, step)
    return lax.rem(index - step + count, count)


def exchanged(value, axis, step):
    count = lax.axis_size(axis)
    if is_power_of_two(count):
        pairs = [(i, i ^ step) for i in range(count)]
    else:
        pairs = [(i, (i + step) % count) for i in range(count)]
    return lax.ppermute(value, axis, pairs)


def body(cell_index, charges, momenta, fill_pattern, encounters, green_spectrum, stop_gain, parasitic_gain):
    particles = cell_index.shape[3]
    tiles = lax.axis_size("tile")
    count = lax.axis_size("bunch")
    tables = make_tables()
    bunch = lax.axis_index("bunch").astype(jnp.int32).reshape(1)
    tile = lax.axis_index("tile").astype(jnp.int32).reshape(1)
    columns = green_spectrum.shape[1]
    pack, copies, message = pl.pallas_call(
        pack_kernel,
        out_shape=(
            jax.ShapeDtypeStruct((8, particles), bf16),
            jax.ShapeDtypeStruct((count, 8, particles), bf16),
            jax.ShapeDtypeStruct((8 * particles // GRID + columns, GRID), bf16),
        ),
        in_specs=[VMEM, VMEM, SMEM, SMEM, VMEM],
        out_specs=(VMEM, VMEM, VMEM),
        compiler_params=SMALL,
    )(
        kept_far(cell_index),
        kept_far(charges.reshape(2, particles)),
        kept_far(fill_pattern.T),
        kept_far(jnp.transpose(encounters, (1, 2, 3, 0))),
        kept_far(green_spectrum.T),
    )
    messages = [message] + [exchanged(message, "tile", step) for step in range(1, tiles)]
    queries = lax.all_to_all(copies, "bunch", split_axis=0, concat_axis=0, tiled=True)
    fields = pl.pallas_call(
        functools.partial(field_kernel, tiles),
        out_shape=jax.ShapeDtypeStruct((2, 2 * GRID, GRID), bf16),
        in_specs=[SMEM] + [VMEM] * tiles + [FAR],
        out_specs=VMEM,
        scratch_shapes=[
            pltpu.VMEM(tables.shape, bf16),
            pltpu.VMEM((GRID, GRID), bf16),
            pltpu.SemaphoreType.DMA,
        ],
        compiler_params=LIMIT,
        cost_estimate=pl.CostEstimate(flops=3000000000, bytes_accessed=1000000, transcendentals=0),
    )(tile, *messages, kept_far(jnp.asarray(tables)))
    kicks = pl.pallas_call(
        functools.partial(kick_kernel, count),
        out_shape=jax.ShapeDtypeStruct((count, 4, particles), f32),
        in_specs=[SMEM, SMEM, SMEM, VMEM, VMEM],
        out_specs=VMEM,
        compiler_params=LIMIT,
    )(bunch, stop_gain, parasitic_gain, fields, queries)
    received = lax.all_to_all(kicks, "bunch", split_axis=0, concat_axis=0, tiled=True)
    return pl.pallas_call(
        functools.partial(final_kernel, count),
        out_shape=jax.ShapeDtypeStruct(momenta.shape, f32),
        in_specs=[SMEM, VMEM, VMEM],
        out_specs=VMEM,
        compiler_params=SMALL,
    )(bunch, received, momenta)


def solution(mesh):
    in_specs = (
        P(None, "bunch", None, "tile"),
        P(None, "bunch", "tile"),
        P(None, "bunch", None, "tile"),
        P(None, "bunch"),
        P(None, None, None, "bunch"),
        P(None, "tile"),
        P(),
        P(),
    )
    out_specs = P(None, "bunch", None, "tile")
    return jax.shard_map(body, mesh=mesh, in_specs=in_specs, out_specs=out_specs, check_vma=False)
```

```python
import functools
import math

import jax
import jax.numpy as jnp
import ml_dtypes
import numpy as np
from jax import lax
from jax.experimental import pallas as pl
from jax.experimental.pallas import tpu as pltpu
from jax.sharding import PartitionSpec as P

GRID = 256
HALF = GRID // 2
STOPS = 4
OFFSET_CELLS = 32
BANDS = GRID // OFFSET_CELLS
REACH = STOPS + 1
f32 = jnp.float32
bf16 = jnp.bfloat16


def split_table(table):
    high = table.astype(ml_dtypes.bfloat16)
    low = (table - high.astype(np.float64)).astype(ml_dtypes.bfloat16)
    return np.stack([high, low])


@functools.cache
def make_tables():
    cells = np.arange(GRID)
    wave = np.where(cells <= HALF, cells, cells - HALF)
    is_sin = cells > HALF
    angle = 2 * np.pi * ((cells[:, None] * wave[None, :]) % GRID) / GRID
    basis = np.where(is_sin[None, :], np.sin(angle), np.cos(angle))
    slope = -0.5 * (np.roll(basis, -1, 0) - np.roll(basis, 1, 0))
    order = OFFSET_CELLS * (cells % BANDS) + cells // BANDS
    here = (cells[None, :] == wave[:, None]).astype(np.float64)
    there = (cells[None, :] == (-wave[:, None]) % GRID).astype(np.float64)
    count = np.where((wave == 0) | (wave == HALF), 1.0, 2.0)[:, None] / GRID
    sign = np.where(is_sin, -1.0, 1.0)[:, None]
    even = 0.5 * (here + there) * count
    odd = 0.5 * (here - there) * count
    mixers = np.stack([even, even.T, odd * sign, -(odd * sign).T])
    tables = [basis.T, basis, slope.T, basis[order], slope[order]]
    tables = [*(split_table(table) for table in tables), mixers]
    return np.concatenate([table.astype(ml_dtypes.bfloat16) for table in tables])


def dot(a, b):
    return jnp.dot(a, b, preferred_element_type=f32)


def dot_nt(a, b):
    return lax.dot_general(a, b, (((1,), (1,)), ((), ())), preferred_element_type=f32)


def halves(x):
    high = x.astype(bf16)
    return high, (x - high.astype(f32)).astype(bf16)


def wide(x, axis):
    high, low = halves(x)
    return jnp.concatenate([high, low, high], axis=axis)


def long(table, axis):
    return jnp.concatenate([table[0], table[0], table[1]], axis=axis)


def pack_kernel(cells, charges, fill, marks, green, out, copies, message):
    particles = charges.shape[1]
    width = particles // 8
    for beam in range(2):
        rows = [
            charges[beam : beam + 1, :].astype(f32) * fill[0, beam].astype(f32),
            cells[beam, 0, 0:1, :].astype(f32),
            cells[beam, 0, 1:2, :].astype(f32),
        ]
        group = lax.broadcasted_iota(jnp.int32, (1, particles), 1) // width
        mark = jnp.zeros((1, particles), f32)
        for offset in range(1, REACH):
            mark = jnp.where(group == offset - 1, marks[beam, 0, 0, offset - 1].astype(f32), mark)
        for offset in range(STOPS - 1):
            mark = jnp.where(group == STOPS + offset, marks[beam, 1, 0, offset + 1].astype(f32), mark)
        rows.append(mark)
        for row, value in enumerate(rows):
            out[4 * beam + row : 4 * beam + row + 1, :] = value.astype(bf16)
    for copy in range(copies.shape[0]):
        copies[copy] = out[...]
    lists = 8 * particles // GRID
    for part in range(particles // GRID):
        message[8 * part : 8 * part + 8, :] = out[:, part * GRID : (part + 1) * GRID]
    message[lists:, :] = green[...].astype(bf16)


def field_kernel(tiles, index, *refs):
    messages = refs[:tiles]
    far, out, near, gathered, densities, arrived = refs[tiles:]
    fetch = pltpu.make_async_copy(far, near, arrived)
    fetch.start()
    lists = messages[0].shape[0] - GRID // tiles
    columns = GRID // tiles
    for step in range(tiles):
        start = pl.multiple_of(relative(index[0], step, tiles) * columns, columns)
        gathered[pl.ds(start, columns), :] = messages[step][lists:, :]

    @pl.when(index[0] >= 0)
    def deposit():
        cells = lax.broadcasted_iota(jnp.int32, (GRID, GRID), 0).astype(f32)
        for beam in range(2):
            row_hots, col_hots = [], []
            for message in messages:
                for part in range(lists // 8):
                    base = 8 * part + 4 * beam
                    charge = message[base : base + 1, :].astype(f32)
                    rows = message[base + 1 : base + 2, :].astype(f32)
                    cols = message[base + 2 : base + 3, :].astype(f32)
                    row_hots.append(jnp.where(cells == rows, 1.0, 0.0).astype(bf16))
                    col_hots.append(jnp.where(cells == cols, charge, 0.0).astype(bf16))
            density = dot_nt(jnp.concatenate(col_hots, axis=1), jnp.concatenate(row_hots, axis=1))
            densities[:, beam * GRID : (beam + 1) * GRID] = wide(density, 0)

    fetch.wait()
    alpha, beta = (
        dot(near[side], turned[0]) + dot(near[side], turned[1])
        for side, turned in (
            (side, halves(dot(gathered[...], near[side + 1]))) for side in (10, 12)
        )
    )
    first = dot(long(near[0:2], 1), densities[...])
    first = jnp.concatenate([first[:, :GRID], first[:, GRID:]], axis=0)
    spectra = dot(wide(first, 1), long(near[2:4], 0))
    scaled = []
    for beam in range(2):
        spectrum = spectra[beam * GRID : (beam + 1) * GRID]
        swapped = jnp.concatenate(
            [
                jnp.concatenate([spectrum[HALF:, HALF:], spectrum[HALF:, :HALF]], axis=1),
                jnp.concatenate([spectrum[:HALF, HALF:], spectrum[:HALF, :HALF]], axis=1),
            ],
            axis=0,
        )
        scaled.append(alpha * spectrum + beta * swapped)
    scaled = wide(jnp.concatenate(scaled, axis=0), 1)
    for axis, (inner, outer) in enumerate(((4, 6), (0, 8))):
        part = dot(scaled, long(near[inner : inner + 2], 0)).astype(bf16)
        part = jnp.concatenate([part[:GRID], part[GRID:]], axis=1)
        table = jnp.concatenate([near[outer], near[outer + 1]], axis=1)
        field = dot(table, jnp.concatenate([part, part], axis=0))
        for beam in range(2):
            out[beam, axis * GRID : (axis + 1) * GRID, :] = field[
                :, beam * GRID : (beam + 1) * GRID
            ].astype(bf16)


def kick_kernel(count, index, gains, strengths, fields, queries, out):
    particles = queries.shape[2]
    width = particles // 8
    here = index[0]
    block = 2 * width
    cells = lax.broadcasted_iota(jnp.int32, (GRID, block), 0).astype(f32)
    bands = lax.broadcasted_iota(jnp.int32, (BANDS, block), 0).astype(f32)
    for offset in reversed(range(REACH)):
        for beam in range(2):
            sign = 1 if beam == 0 else -1
            target = lax.rem(here - sign * offset + count, count)
            source = queries.at[target]
            base = 4 * beam

            def weight_of(stop, group):
                mark = source[base + 3 : base + 4, group * width : (group + 1) * width].astype(f32)
                mark = mark * (gains[stop] * strengths[stop])
                return jnp.concatenate([mark, mark], axis=1)

            middle = gains[offset] if offset < STOPS else None
            up = weight_of(offset - 1, offset - 1) if offset else None
            down = weight_of(offset + 1, STOPS + offset) if offset < STOPS - 1 else None
            for start in range(0, particles, block):
                rows = source[base + 1 : base + 2, start : start + block].astype(f32)
                cols = source[base + 2 : base + 3, start : start + block].astype(f32)
                band = jnp.floor(cols * (1.0 / OFFSET_CELLS))
                inside = jnp.broadcast_to(cols - band * OFFSET_CELLS, (BANDS, block))
                hot = jnp.where(cells == rows, 1.0, 0.0).astype(bf16)
                values = dot(fields[1 - beam], hot)
                picked = [jnp.zeros((BANDS, block), f32) for _ in range(2)]
                for place in range(OFFSET_CELLS):
                    hit = inside == place
                    for axis in range(2):
                        at = axis * GRID + place * BANDS
                        picked[axis] = jnp.where(hit, values[at : at + BANDS, :], picked[axis])
                weight = jnp.zeros((BANDS, block), f32)
                if middle is not None:
                    weight = jnp.where(bands == band, middle, weight)
                if up is not None:
                    weight = jnp.where(bands == band - 1, up, weight)
                if down is not None:
                    weight = jnp.where(bands == band + 1, down, weight)
                for axis in range(2):
                    kick = jnp.sum(weight * picked[axis], axis=0, keepdims=True)
                    out[target, 2 * beam + axis : 2 * beam + axis + 1, start : start + block] = kick


def final_kernel(count, index, received, momenta, out):
    here = index[0]
    for beam in range(2):
        sign = 1 if beam == 0 else -1
        for axis in range(2):
            total = None
            for offset in range(REACH):
                source = lax.rem(here + sign * offset + count, count)
                part = received[source, 2 * beam + axis : 2 * beam + axis + 1, :]
                total = part if total is None else total + part
            out[beam, 0, axis : axis + 1, :] = momenta[beam, 0, axis : axis + 1, :] + total.astype(
                bf16
            ).astype(f32)


SMEM = pl.BlockSpec(memory_space=pltpu.SMEM)
VMEM = pl.BlockSpec(memory_space=pltpu.VMEM)
FAR = pl.BlockSpec(memory_space=pltpu.HBM)
LIMIT = pltpu.CompilerParams(vmem_limit_bytes=48 * 1024 * 1024)
SMALL = pltpu.CompilerParams(vmem_limit_bytes=16 * 1024 * 1024)


def kept_far(value):
    return pltpu.with_memory_space_constraint(value, pltpu.HBM)


def is_power_of_two(count):
    return count & (count - 1) == 0


def relative(index, step, count):
    if is_power_of_two(count):
        return jnp.bitwise_xor(index, step)
    return lax.rem(index - step + count, count)


def exchanged(value, axis, step):
    count = lax.axis_size(axis)
    if is_power_of_two(count):
        pairs = [(i, i ^ step) for i in range(count)]
    else:
        pairs = [(i, (i + step) % count) for i in range(count)]
    return lax.ppermute(value, axis, pairs)


def body(cell_index, charges, momenta, fill_pattern, encounters, green_spectrum, stop_gain, parasitic_gain):
    particles = cell_index.shape[3]
    tiles = lax.axis_size("tile")
    count = lax.axis_size("bunch")
    tables = make_tables()
    bunch = lax.axis_index("bunch").astype(jnp.int32).reshape(1)
    tile = lax.axis_index("tile").astype(jnp.int32).reshape(1)
    columns = green_spectrum.shape[1]
    pack, copies, message = pl.pallas_call(
        pack_kernel,
        out_shape=(
            jax.ShapeDtypeStruct((8, particles), bf16),
            jax.ShapeDtypeStruct((count, 8, particles), bf16),
            jax.ShapeDtypeStruct((8 * particles // GRID + columns, GRID), bf16),
        ),
        in_specs=[VMEM, VMEM, SMEM, SMEM, VMEM],
        out_specs=(VMEM, VMEM, VMEM),
        compiler_params=SMALL,
    )(
        kept_far(cell_index),
        kept_far(charges.reshape(2, particles)),
        kept_far(fill_pattern.T),
        kept_far(jnp.transpose(encounters, (1, 2, 3, 0))),
        kept_far(green_spectrum.T),
    )
    messages = [message] + [exchanged(message, "tile", step) for step in range(1, tiles)]
    queries = lax.all_to_all(copies, "bunch", split_axis=0, concat_axis=0, tiled=True)
    fields = pl.pallas_call(
        functools.partial(field_kernel, tiles),
        out_shape=jax.ShapeDtypeStruct((2, 2 * GRID, GRID), bf16),
        in_specs=[SMEM] + [VMEM] * tiles + [FAR],
        out_specs=VMEM,
        scratch_shapes=[
            pltpu.VMEM(tables.shape, bf16),
            pltpu.VMEM((GRID, GRID), bf16),
            pltpu.VMEM((3 * GRID, 2 * GRID), bf16),
            pltpu.SemaphoreType.DMA,
        ],
        compiler_params=LIMIT,
        cost_estimate=pl.CostEstimate(flops=3000000000, bytes_accessed=1000000, transcendentals=0),
    )(tile, *messages, kept_far(jnp.asarray(tables)))
    kicks = pl.pallas_call(
        functools.partial(kick_kernel, count),
        out_shape=jax.ShapeDtypeStruct((count, 4, particles), f32),
        in_specs=[SMEM, SMEM, SMEM, VMEM, VMEM],
        out_specs=VMEM,
        compiler_params=LIMIT,
    )(bunch, stop_gain, parasitic_gain, fields, queries)
    received = lax.all_to_all(kicks, "bunch", split_axis=0, concat_axis=0, tiled=True)
    return pl.pallas_call(
        functools.partial(final_kernel, count),
        out_shape=jax.ShapeDtypeStruct(momenta.shape, f32),
        in_specs=[SMEM, VMEM, VMEM],
        out_specs=VMEM,
        compiler_params=SMALL,
    )(bunch, received, momenta)


def solution(mesh):
    in_specs = (
        P(None, "bunch", None, "tile"),
        P(None, "bunch", "tile"),
        P(None, "bunch", None, "tile"),
        P(None, "bunch"),
        P(None, None, None, "bunch"),
        P(None, "tile"),
        P(),
        P(),
    )
    out_specs = P(None, "bunch", None, "tile")
    return jax.shard_map(body, mesh=mesh, in_specs=in_specs, out_specs=out_specs, check_vma=False)
```

```python
import functools
import math

import jax
import jax.numpy as jnp
import ml_dtypes
import numpy as np
from jax import lax
from jax.experimental import pallas as pl
from jax.experimental.pallas import tpu as pltpu
from jax.sharding import PartitionSpec as P

GRID = 256
HALF = GRID // 2
STOPS = 4
OFFSET_CELLS = 32
BANDS = GRID // OFFSET_CELLS
REACH = STOPS + 1
INVERSE_TABLES = 6
f32 = jnp.float32
bf16 = jnp.bfloat16


def split_table(table):
    high = table.astype(ml_dtypes.bfloat16)
    low = (table - high.astype(np.float64)).astype(ml_dtypes.bfloat16)
    return np.stack([high, low])


@functools.cache
def make_tables():
    cells = np.arange(GRID)
    wave = np.where(cells <= HALF, cells, cells - HALF)
    is_sin = cells > HALF
    angle = 2 * np.pi * ((cells[:, None] * wave[None, :]) % GRID) / GRID
    basis = np.where(is_sin[None, :], np.sin(angle), np.cos(angle))
    slope = -0.5 * (np.roll(basis, -1, 0) - np.roll(basis, 1, 0))
    order = OFFSET_CELLS * (cells % BANDS) + cells // BANDS
    here = (cells[None, :] == wave[:, None]).astype(np.float64)
    there = (cells[None, :] == (-wave[:, None]) % GRID).astype(np.float64)
    count = np.where((wave == 0) | (wave == HALF), 1.0, 2.0)[:, None] / GRID
    sign = np.where(is_sin, -1.0, 1.0)[:, None]
    even = 0.5 * (here + there) * count
    odd = 0.5 * (here - there) * count
    mixers = np.stack([even, even.T, odd * sign, -(odd * sign).T])
    forward = [split_table(basis.T), split_table(basis)]
    inverse = [split_table(table) for table in (slope.T, basis[order], slope[order])]
    tables = [*forward, mixers, *inverse]
    return np.concatenate([table.astype(ml_dtypes.bfloat16) for table in tables])


def dot(a, b):
    return jnp.dot(a, b, preferred_element_type=f32)


def dot_nt(a, b):
    return lax.dot_general(a, b, (((1,), (1,)), ((), ())), preferred_element_type=f32)


def halves(x):
    high = x.astype(bf16)
    return high, (x - high.astype(f32)).astype(bf16)


def wide(x, axis):
    high, low = halves(x)
    return jnp.concatenate([high, low, high], axis=axis)


def long(table, axis):
    return jnp.concatenate([table[0], table[0], table[1]], axis=axis)


def pack_kernel(cells, charges, fill, marks, green, out, copies, message):
    particles = charges.shape[1]
    width = particles // 8
    for beam in range(2):
        rows = [
            charges[beam : beam + 1, :].astype(f32) * fill[0, beam].astype(f32),
            cells[beam, 0, 0:1, :].astype(f32),
            cells[beam, 0, 1:2, :].astype(f32),
        ]
        group = lax.broadcasted_iota(jnp.int32, (1, particles), 1) // width
        mark = jnp.zeros((1, particles), f32)
        for offset in range(1, REACH):
            mark = jnp.where(group == offset - 1, marks[beam, 0, 0, offset - 1].astype(f32), mark)
        for offset in range(STOPS - 1):
            mark = jnp.where(group == STOPS + offset, marks[beam, 1, 0, offset + 1].astype(f32), mark)
        rows.append(mark)
        for row, value in enumerate(rows):
            out[4 * beam + row : 4 * beam + row + 1, :] = value.astype(bf16)
    for copy in range(copies.shape[0]):
        copies[copy] = out[...]
    lists = 8 * particles // GRID
    for part in range(particles // GRID):
        message[8 * part : 8 * part + 8, :] = out[:, part * GRID : (part + 1) * GRID]
    message[lists:, :] = green[...].astype(bf16)


def field_kernel(tiles, index, *refs):
    messages = refs[:tiles]
    far, out, near, gathered, densities, arrived = refs[tiles:]
    early = near.shape[0] - INVERSE_TABLES
    fetch = [
        pltpu.make_async_copy(far.at[:early], near.at[:early], arrived.at[0]),
        pltpu.make_async_copy(far.at[early:], near.at[early:], arrived.at[1]),
    ]
    for copy in fetch:
        copy.start()
    lists = messages[0].shape[0] - GRID // tiles
    columns = GRID // tiles
    for step in range(tiles):
        start = pl.multiple_of(relative(index[0], step, tiles) * columns, columns)
        gathered[pl.ds(start, columns), :] = messages[step][lists:, :]

    @pl.when(index[0] >= 0)
    def deposit():
        cells = lax.broadcasted_iota(jnp.int32, (GRID, GRID), 0).astype(f32)
        for beam in range(2):
            row_hots, col_hots = [], []
            for message in messages:
                for part in range(lists // 8):
                    base = 8 * part + 4 * beam
                    charge = message[base : base + 1, :].astype(f32)
                    rows = message[base + 1 : base + 2, :].astype(f32)
                    cols = message[base + 2 : base + 3, :].astype(f32)
                    row_hots.append(jnp.where(cells == rows, 1.0, 0.0).astype(bf16))
                    col_hots.append(jnp.where(cells == cols, charge, 0.0).astype(bf16))
            density = dot_nt(jnp.concatenate(col_hots, axis=1), jnp.concatenate(row_hots, axis=1))
            densities[:, beam * GRID : (beam + 1) * GRID] = wide(density, 0)

    fetch[0].wait()
    alpha, beta = (
        dot(near[side], turned[0]) + dot(near[side], turned[1])
        for side, turned in (
            (side, halves(dot(gathered[...], near[side + 1]))) for side in (4, 6)
        )
    )
    first = dot(long(near[0:2], 1), densities[...])
    first = jnp.concatenate([first[:, :GRID], first[:, GRID:]], axis=0)
    spectra = dot(wide(first, 1), long(near[2:4], 0))
    scaled = []
    for beam in range(2):
        spectrum = spectra[beam * GRID : (beam + 1) * GRID]
        swapped = jnp.concatenate(
            [
                jnp.concatenate([spectrum[HALF:, HALF:], spectrum[HALF:, :HALF]], axis=1),
                jnp.concatenate([spectrum[:HALF, HALF:], spectrum[:HALF, :HALF]], axis=1),
            ],
            axis=0,
        )
        scaled.append(alpha * spectrum + beta * swapped)
    fetch[1].wait()
    left = jnp.concatenate([long(near[10:12], 1), long(near[12:14], 1)], axis=0)
    part = dot(left, wide(jnp.concatenate(scaled, axis=1), 0)).astype(bf16)
    for axis, right in enumerate((8, 0)):
        rows = part[axis * GRID : (axis + 1) * GRID]
        rows = jnp.concatenate([rows[:, :GRID], rows[:, GRID:]], axis=0)
        field = dot(rows, near[right]) + dot(rows, near[right + 1])
        for beam in range(2):
            out[beam, axis * GRID : (axis + 1) * GRID, :] = field[
                beam * GRID : (beam + 1) * GRID
            ].astype(bf16)


def kick_kernel(count, index, gains, strengths, fields, queries, out):
    particles = queries.shape[2]
    width = particles // 8
    here = index[0]
    block = 2 * width
    cells = lax.broadcasted_iota(jnp.int32, (GRID, block), 0).astype(f32)
    bands = lax.broadcasted_iota(jnp.int32, (BANDS, block), 0).astype(f32)
    for offset in reversed(range(REACH)):
        for beam in range(2):
            sign = 1 if beam == 0 else -1
            target = lax.rem(here - sign * offset + count, count)
            source = queries.at[target]
            base = 4 * beam

            def weight_of(stop, group):
                mark = source[base + 3 : base + 4, group * width : (group + 1) * width].astype(f32)
                mark = mark * (gains[stop] * strengths[stop])
                return jnp.concatenate([mark, mark], axis=1)

            middle = gains[offset] if offset < STOPS else None
            up = weight_of(offset - 1, offset - 1) if offset else None
            down = weight_of(offset + 1, STOPS + offset) if offset < STOPS - 1 else None
            for start in range(0, particles, block):
                rows = source[base + 1 : base + 2, start : start + block].astype(f32)
                cols = source[base + 2 : base + 3, start : start + block].astype(f32)
                band = jnp.floor(cols * (1.0 / OFFSET_CELLS))
                inside = jnp.broadcast_to(cols - band * OFFSET_CELLS, (BANDS, block))
                hot = jnp.where(cells == rows, 1.0, 0.0).astype(bf16)
                values = dot(fields[1 - beam], hot)
                picked = [jnp.zeros((BANDS, block), f32) for _ in range(2)]
                for place in range(OFFSET_CELLS):
                    hit = inside == place
                    for axis in range(2):
                        at = axis * GRID + place * BANDS
                        picked[axis] = jnp.where(hit, values[at : at + BANDS, :], picked[axis])
                weight = jnp.zeros((BANDS, block), f32)
                if middle is not None:
                    weight = jnp.where(bands == band, middle, weight)
                if up is not None:
                    weight = jnp.where(bands == band - 1, up, weight)
                if down is not None:
                    weight = jnp.where(bands == band + 1, down, weight)
                for axis in range(2):
                    kick = jnp.sum(weight * picked[axis], axis=0, keepdims=True)
                    out[target, 2 * beam + axis : 2 * beam + axis + 1, start : start + block] = kick


def final_kernel(count, index, received, momenta, out):
    here = index[0]
    for beam in range(2):
        sign = 1 if beam == 0 else -1
        for axis in range(2):
            total = None
            for offset in range(REACH):
                source = lax.rem(here + sign * offset + count, count)
                part = received[source, 2 * beam + axis : 2 * beam + axis + 1, :]
                total = part if total is None else total + part
            out[beam, 0, axis : axis + 1, :] = momenta[beam, 0, axis : axis + 1, :] + total.astype(
                bf16
            ).astype(f32)


SMEM = pl.BlockSpec(memory_space=pltpu.SMEM)
VMEM = pl.BlockSpec(memory_space=pltpu.VMEM)
FAR = pl.BlockSpec(memory_space=pltpu.HBM)
LIMIT = pltpu.CompilerParams(vmem_limit_bytes=48 * 1024 * 1024)
SMALL = pltpu.CompilerParams(vmem_limit_bytes=16 * 1024 * 1024)


def kept_far(value):
    return pltpu.with_memory_space_constraint(value, pltpu.HBM)


def is_power_of_two(count):
    return count & (count - 1) == 0


def relative(index, step, count):
    if is_power_of_two(count):
        return jnp.bitwise_xor(index, step)
    return lax.rem(index - step + count, count)


def exchanged(value, axis, step):
    count = lax.axis_size(axis)
    if is_power_of_two(count):
        pairs = [(i, i ^ step) for i in range(count)]
    else:
        pairs = [(i, (i + step) % count) for i in range(count)]
    return lax.ppermute(value, axis, pairs)


def body(cell_index, charges, momenta, fill_pattern, encounters, green_spectrum, stop_gain, parasitic_gain):
    particles = cell_index.shape[3]
    tiles = lax.axis_size("tile")
    count = lax.axis_size("bunch")
    tables = make_tables()
    bunch = lax.axis_index("bunch").astype(jnp.int32).reshape(1)
    tile = lax.axis_index("tile").astype(jnp.int32).reshape(1)
    columns = green_spectrum.shape[1]
    pack, copies, message = pl.pallas_call(
        pack_kernel,
        out_shape=(
            jax.ShapeDtypeStruct((8, particles), bf16),
            jax.ShapeDtypeStruct((count, 8, particles), bf16),
            jax.ShapeDtypeStruct((8 * particles // GRID + columns, GRID), bf16),
        ),
        in_specs=[VMEM, VMEM, SMEM, SMEM, VMEM],
        out_specs=(VMEM, VMEM, VMEM),
        compiler_params=SMALL,
    )(
        kept_far(cell_index),
        kept_far(charges.reshape(2, particles)),
        kept_far(fill_pattern.T),
        kept_far(jnp.transpose(encounters, (1, 2, 3, 0))),
        kept_far(green_spectrum.T),
    )
    messages = [message] + [exchanged(message, "tile", step) for step in range(1, tiles)]
    queries = lax.all_to_all(copies, "bunch", split_axis=0, concat_axis=0, tiled=True)
    fields = pl.pallas_call(
        functools.partial(field_kernel, tiles),
        out_shape=jax.ShapeDtypeStruct((2, 2 * GRID, GRID), bf16),
        in_specs=[SMEM] + [VMEM] * tiles + [FAR],
        out_specs=VMEM,
        scratch_shapes=[
            pltpu.VMEM(tables.shape, bf16),
            pltpu.VMEM((GRID, GRID), bf16),
            pltpu.VMEM((3 * GRID, 2 * GRID), bf16),
            pltpu.SemaphoreType.DMA((2,)),
        ],
        compiler_params=LIMIT,
        cost_estimate=pl.CostEstimate(flops=3000000000, bytes_accessed=1000000, transcendentals=0),
    )(tile, *messages, kept_far(jnp.asarray(tables)))
    kicks = pl.pallas_call(
        functools.partial(kick_kernel, count),
        out_shape=jax.ShapeDtypeStruct((count, 4, particles), f32),
        in_specs=[SMEM, SMEM, SMEM, VMEM, VMEM],
        out_specs=VMEM,
        compiler_params=LIMIT,
    )(bunch, stop_gain, parasitic_gain, fields, queries)
    received = lax.all_to_all(kicks, "bunch", split_axis=0, concat_axis=0, tiled=True)
    return pl.pallas_call(
        functools.partial(final_kernel, count),
        out_shape=jax.ShapeDtypeStruct(momenta.shape, f32),
        in_specs=[SMEM, VMEM, VMEM],
        out_specs=VMEM,
        compiler_params=SMALL,
    )(bunch, received, momenta)


def solution(mesh):
    in_specs = (
        P(None, "bunch", None, "tile"),
        P(None, "bunch", "tile"),
        P(None, "bunch", None, "tile"),
        P(None, "bunch"),
        P(None, None, None, "bunch"),
        P(None, "tile"),
        P(),
        P(),
    )
    out_specs = P(None, "bunch", None, "tile")
    return jax.shard_map(body, mesh=mesh, in_specs=in_specs, out_specs=out_specs, check_vma=False)
```

```python
import functools
import math

import jax
import jax.numpy as jnp
import ml_dtypes
import numpy as np
from jax import lax
from jax.experimental import pallas as pl
from jax.experimental.pallas import tpu as pltpu
from jax.sharding import PartitionSpec as P

GRID = 256
HALF = GRID // 2
STOPS = 4
OFFSET_CELLS = 32
BANDS = GRID // OFFSET_CELLS
REACH = STOPS + 1
INVERSE_TABLES = 6
LANES = 128
f32 = jnp.float32
bf16 = jnp.bfloat16


def split_table(table):
    high = table.astype(ml_dtypes.bfloat16)
    low = (table - high.astype(np.float64)).astype(ml_dtypes.bfloat16)
    return np.stack([high, low])


@functools.cache
def make_tables():
    cells = np.arange(GRID)
    wave = np.where(cells <= HALF, cells, cells - HALF)
    is_sin = cells > HALF
    angle = 2 * np.pi * ((cells[:, None] * wave[None, :]) % GRID) / GRID
    basis = np.where(is_sin[None, :], np.sin(angle), np.cos(angle))
    slope = -0.5 * (np.roll(basis, -1, 0) - np.roll(basis, 1, 0))
    order = OFFSET_CELLS * (cells % BANDS) + cells // BANDS
    here = (cells[None, :] == wave[:, None]).astype(np.float64)
    there = (cells[None, :] == (-wave[:, None]) % GRID).astype(np.float64)
    count = np.where((wave == 0) | (wave == HALF), 1.0, 2.0)[:, None] / GRID
    sign = np.where(is_sin, -1.0, 1.0)[:, None]
    even = 0.5 * (here + there) * count
    odd = 0.5 * (here - there) * count
    mixers = np.stack([even, even.T, odd * sign, -(odd * sign).T])
    forward = [split_table(basis.T), split_table(basis)]
    inverse = [split_table(table) for table in (slope.T, basis[order], slope[order])]
    tables = [*forward, mixers, *inverse]
    return np.concatenate([table.astype(ml_dtypes.bfloat16) for table in tables])


def dot(a, b):
    return jnp.dot(a, b, preferred_element_type=f32)


def dot_nt(a, b):
    return lax.dot_general(a, b, (((1,), (1,)), ((), ())), preferred_element_type=f32)


def halves(x):
    high = x.astype(bf16)
    return high, (x - high.astype(f32)).astype(bf16)


def wide(x, axis):
    high, low = halves(x)
    return jnp.concatenate([high, low, high], axis=axis)


def long(table, axis):
    return jnp.concatenate([table[0], table[0], table[1]], axis=axis)


def query_rows(rows, cols, up, down):
    half = rows.shape[1] // 2
    marks = [jnp.full((1, LANES), mark, f32) for mark in (up, down, 0.0, 0.0)]
    places = [rows[:, :half], rows[:, half:], cols[:, :half], cols[:, half:]]
    return [jnp.concatenate(pair, axis=1) for pair in zip(places, marks)]


def pack_kernel(index, cells, charges, fill, marks, green, own, copies, message):
    particles = charges.shape[1]
    count = copies.shape[0]
    here = index[0]
    lists = 8 * particles // GRID
    for beam in range(2):
        sign = 1 if beam == 0 else -1
        charge = charges[beam : beam + 1, :].astype(f32) * fill[0, beam].astype(f32)
        rows = cells[beam, 0, 0:1, :].astype(f32)
        cols = cells[beam, 0, 1:2, :].astype(f32)
        for part in range(particles // GRID):
            lanes = slice(part * GRID, (part + 1) * GRID)
            for row, value in enumerate((charge, rows, cols)):
                at = 8 * part + 4 * beam + row
                message[at : at + 1, :] = value[:, lanes].astype(bf16)
        for offset in range(REACH):
            up = marks[beam, 0, 0, offset - 1].astype(f32) if offset else 0.0
            down = marks[beam, 1, 0, offset + 1].astype(f32) if offset < STOPS - 1 else 0.0
            target = own if offset == 0 else copies.at[lax.rem(here + sign * offset + count, count)]
            for row, value in enumerate(query_rows(rows, cols, up, down)):
                target[4 * beam + row : 4 * beam + row + 1, :] = value.astype(bf16)
    message[lists:, :] = green[...].astype(bf16)


def field_kernel(tiles, index, *refs):
    messages = refs[:tiles]
    far, out, near, gathered, densities, arrived = refs[tiles:]
    early = near.shape[0] - INVERSE_TABLES
    fetch = [
        pltpu.make_async_copy(far.at[:early], near.at[:early], arrived.at[0]),
        pltpu.make_async_copy(far.at[early:], near.at[early:], arrived.at[1]),
    ]
    for copy in fetch:
        copy.start()
    lists = messages[0].shape[0] - GRID // tiles
    columns = GRID // tiles
    for step in range(tiles):
        start = pl.multiple_of(relative(index[0], step, tiles) * columns, columns)
        gathered[pl.ds(start, columns), :] = messages[step][lists:, :]

    @pl.when(index[0] >= 0)
    def deposit():
        cells = lax.broadcasted_iota(jnp.int32, (GRID, GRID), 0).astype(f32)
        for beam in range(2):
            row_hots, col_hots = [], []
            for message in messages:
                for part in range(lists // 8):
                    base = 8 * part + 4 * beam
                    charge = message[base : base + 1, :].astype(f32)
                    rows = message[base + 1 : base + 2, :].astype(f32)
                    cols = message[base + 2 : base + 3, :].astype(f32)
                    row_hots.append(jnp.where(cells == rows, 1.0, 0.0).astype(bf16))
                    col_hots.append(jnp.where(cells == cols, charge, 0.0).astype(bf16))
            density = dot_nt(jnp.concatenate(col_hots, axis=1), jnp.concatenate(row_hots, axis=1))
            densities[:, beam * GRID : (beam + 1) * GRID] = wide(density, 0)

    fetch[0].wait()
    alpha, beta = (
        dot(near[side], turned[0]) + dot(near[side], turned[1])
        for side, turned in (
            (side, halves(dot(gathered[...], near[side + 1]))) for side in (4, 6)
        )
    )
    first = dot(long(near[0:2], 1), densities[...])
    first = jnp.concatenate([first[:, :GRID], first[:, GRID:]], axis=0)
    spectra = dot(wide(first, 1), long(near[2:4], 0))
    scaled = []
    for beam in range(2):
        spectrum = spectra[beam * GRID : (beam + 1) * GRID]
        swapped = jnp.concatenate(
            [
                jnp.concatenate([spectrum[HALF:, HALF:], spectrum[HALF:, :HALF]], axis=1),
                jnp.concatenate([spectrum[:HALF, HALF:], spectrum[:HALF, :HALF]], axis=1),
            ],
            axis=0,
        )
        scaled.append(alpha * spectrum + beta * swapped)
    fetch[1].wait()
    left = jnp.concatenate([long(near[10:12], 1), long(near[12:14], 1)], axis=0)
    part = dot(left, wide(jnp.concatenate(scaled, axis=1), 0)).astype(bf16)
    for axis, right in enumerate((8, 0)):
        rows = part[axis * GRID : (axis + 1) * GRID]
        rows = jnp.concatenate([rows[:, :GRID], rows[:, GRID:]], axis=0)
        field = dot(rows, near[right]) + dot(rows, near[right + 1])
        for beam in range(2):
            out[beam, axis * GRID : (axis + 1) * GRID, :] = field[
                beam * GRID : (beam + 1) * GRID
            ].astype(bf16)


def kick_kernel(count, index, gains, strengths, fields, own, queries, home, away):
    half = queries.shape[-1] - LANES
    here = index[0]
    block = 2 * LANES
    cells = lax.broadcasted_iota(jnp.int32, (GRID, block), 0).astype(f32)
    bands = lax.broadcasted_iota(jnp.int32, (BANDS, block), 0).astype(f32)
    for offset in range(REACH):
        for beam in range(2):
            sign = 1 if beam == 0 else -1
            target = lax.rem(here - sign * offset + count, count)
            source = queries.at[target] if offset else own
            base = 4 * beam

            def weight_of(stop, row):
                mark = source[base + row : base + row + 1, half:].astype(f32)
                mark = mark * (gains[stop] * strengths[stop])
                return jnp.concatenate([mark, mark], axis=1)

            middle = gains[offset] if offset < STOPS else None
            up = weight_of(offset - 1, 0) if offset else None
            down = weight_of(offset + 1, 1) if offset < STOPS - 1 else None
            for start in range(0, 2 * half, block):
                row, lanes = base + start // half, pl.ds(start % half, block)
                rows = source[row : row + 1, lanes].astype(f32)
                cols = source[row + 2 : row + 3, lanes].astype(f32)
                band = jnp.floor(cols * (1.0 / OFFSET_CELLS))
                inside = jnp.broadcast_to(cols - band * OFFSET_CELLS, (BANDS, block))
                hot = jnp.where(cells == rows, 1.0, 0.0).astype(bf16)
                values = dot(fields[1 - beam], hot)
                picked = [jnp.zeros((BANDS, block), f32) for _ in range(2)]
                for place in range(OFFSET_CELLS):
                    hit = inside == place
                    for axis in range(2):
                        at = axis * GRID + place * BANDS
                        picked[axis] = jnp.where(hit, values[at : at + BANDS, :], picked[axis])
                weight = jnp.zeros((BANDS, block), f32)
                if middle is not None:
                    weight = jnp.where(bands == band, middle, weight)
                if up is not None:
                    weight = jnp.where(bands == band - 1, up, weight)
                if down is not None:
                    weight = jnp.where(bands == band + 1, down, weight)
                kick = [jnp.sum(weight * value, axis=0, keepdims=True) for value in picked]
                kick = jnp.concatenate(kick, axis=0)
                if offset == 0:
                    home[2 * beam : 2 * beam + 2, start : start + block] = kick
                elif shared(offset, count):
                    away[target, 2 * beam : 2 * beam + 2, start : start + block] = kick.astype(bf16)
                else:
                    away[target, :, start : start + block] = jnp.concatenate(halves(kick), axis=0)


def shared(offset, count):
    return 2 * offset == count


def final_kernel(count, index, received, home, momenta, out):
    here = index[0]
    for beam in range(2):
        sign = 1 if beam == 0 else -1
        total = home[2 * beam : 2 * beam + 2, :]
        for offset in range(1, REACH):
            part = received[lax.rem(here + sign * offset + count, count)].astype(f32)
            if shared(offset, count):
                total = total + part[2 * beam : 2 * beam + 2]
            else:
                total = total + (part[:2] + part[2:])
        out[beam, 0] = momenta[beam, 0] + total.astype(bf16).astype(f32)


SMEM = pl.BlockSpec(memory_space=pltpu.SMEM)
VMEM = pl.BlockSpec(memory_space=pltpu.VMEM)
FAR = pl.BlockSpec(memory_space=pltpu.HBM)
LIMIT = pltpu.CompilerParams(vmem_limit_bytes=48 * 1024 * 1024)
SMALL = pltpu.CompilerParams(vmem_limit_bytes=16 * 1024 * 1024)


def kept_far(value):
    return pltpu.with_memory_space_constraint(value, pltpu.HBM)


def is_power_of_two(count):
    return count & (count - 1) == 0


def relative(index, step, count):
    if is_power_of_two(count):
        return jnp.bitwise_xor(index, step)
    return lax.rem(index - step + count, count)


def exchanged(value, axis, step):
    count = lax.axis_size(axis)
    if is_power_of_two(count):
        pairs = [(i, i ^ step) for i in range(count)]
    else:
        pairs = [(i, (i + step) % count) for i in range(count)]
    return lax.ppermute(value, axis, pairs)


def body(cell_index, charges, momenta, fill_pattern, encounters, green_spectrum, stop_gain, parasitic_gain):
    particles = cell_index.shape[3]
    tiles = lax.axis_size("tile")
    count = lax.axis_size("bunch")
    tables = make_tables()
    bunch = lax.axis_index("bunch").astype(jnp.int32).reshape(1)
    tile = lax.axis_index("tile").astype(jnp.int32).reshape(1)
    columns = green_spectrum.shape[1]
    own, copies, message = pl.pallas_call(
        pack_kernel,
        out_shape=(
            jax.ShapeDtypeStruct((8, particles // 2 + LANES), bf16),
            jax.ShapeDtypeStruct((count, 8, particles // 2 + LANES), bf16),
            jax.ShapeDtypeStruct((8 * particles // GRID + columns, GRID), bf16),
        ),
        in_specs=[SMEM, VMEM, VMEM, SMEM, SMEM, VMEM],
        out_specs=(VMEM, VMEM, VMEM),
        compiler_params=SMALL,
    )(
        bunch,
        kept_far(cell_index),
        kept_far(charges.reshape(2, particles)),
        kept_far(fill_pattern.T),
        kept_far(jnp.transpose(encounters, (1, 2, 3, 0))),
        kept_far(green_spectrum.T),
    )
    messages = [message] + [exchanged(message, "tile", step) for step in range(1, tiles)]
    queries = lax.all_to_all(copies, "bunch", split_axis=0, concat_axis=0, tiled=True)
    fields = pl.pallas_call(
        functools.partial(field_kernel, tiles),
        out_shape=jax.ShapeDtypeStruct((2, 2 * GRID, GRID), bf16),
        in_specs=[SMEM] + [VMEM] * tiles + [FAR],
        out_specs=VMEM,
        scratch_shapes=[
            pltpu.VMEM(tables.shape, bf16),
            pltpu.VMEM((GRID, GRID), bf16),
            pltpu.VMEM((3 * GRID, 2 * GRID), bf16),
            pltpu.SemaphoreType.DMA((2,)),
        ],
        compiler_params=LIMIT,
        cost_estimate=pl.CostEstimate(flops=3000000000, bytes_accessed=1000000, transcendentals=0),
    )(tile, *messages, kept_far(jnp.asarray(tables)))
    home, away = pl.pallas_call(
        functools.partial(kick_kernel, count),
        out_shape=(
            jax.ShapeDtypeStruct((4, particles), f32),
            jax.ShapeDtypeStruct((count, 4, particles), bf16),
        ),
        in_specs=[SMEM, SMEM, SMEM, VMEM, VMEM, VMEM],
        out_specs=(VMEM, VMEM),
        compiler_params=LIMIT,
    )(bunch, stop_gain, parasitic_gain, fields, own, queries)
    received = lax.all_to_all(away, "bunch", split_axis=0, concat_axis=0, tiled=True)
    return pl.pallas_call(
        functools.partial(final_kernel, count),
        out_shape=jax.ShapeDtypeStruct(momenta.shape, f32),
        in_specs=[SMEM, VMEM, VMEM, VMEM],
        out_specs=VMEM,
        compiler_params=SMALL,
    )(bunch, received, home, momenta)


def solution(mesh):
    in_specs = (
        P(None, "bunch", None, "tile"),
        P(None, "bunch", "tile"),
        P(None, "bunch", None, "tile"),
        P(None, "bunch"),
        P(None, None, None, "bunch"),
        P(None, "tile"),
        P(),
        P(),
    )
    out_specs = P(None, "bunch", None, "tile")
    return jax.shard_map(body, mesh=mesh, in_specs=in_specs, out_specs=out_specs, check_vma=False)
```

```python
import functools
import math

import jax
import jax.numpy as jnp
import ml_dtypes
import numpy as np
from jax import lax
from jax.experimental import pallas as pl
from jax.experimental.pallas import tpu as pltpu
from jax.sharding import PartitionSpec as P

GRID = 256
HALF = GRID // 2
STOPS = 4
OFFSET_CELLS = 32
BANDS = GRID // OFFSET_CELLS
REACH = STOPS + 1
INVERSE_TABLES = 6
LANES = 128
f32 = jnp.float32
bf16 = jnp.bfloat16


def split_table(table):
    high = table.astype(ml_dtypes.bfloat16)
    low = (table - high.astype(np.float64)).astype(ml_dtypes.bfloat16)
    return np.stack([high, low])


@functools.cache
def make_tables():
    cells = np.arange(GRID)
    wave = np.where(cells <= HALF, cells, cells - HALF)
    is_sin = cells > HALF
    angle = 2 * np.pi * ((cells[:, None] * wave[None, :]) % GRID) / GRID
    basis = np.where(is_sin[None, :], np.sin(angle), np.cos(angle))
    slope = -0.5 * (np.roll(basis, -1, 0) - np.roll(basis, 1, 0))
    order = OFFSET_CELLS * (cells % BANDS) + cells // BANDS
    here = (cells[None, :] == wave[:, None]).astype(np.float64)
    there = (cells[None, :] == (-wave[:, None]) % GRID).astype(np.float64)
    count = np.where((wave == 0) | (wave == HALF), 1.0, 2.0)[:, None] / GRID
    sign = np.where(is_sin, -1.0, 1.0)[:, None]
    even = 0.5 * (here + there) * count
    odd = 0.5 * (here - there) * count
    mixers = np.stack([even, even.T, odd * sign, -(odd * sign).T])
    forward = [split_table(basis.T), split_table(basis)]
    inverse = [split_table(table) for table in (slope.T, basis[order], slope[order])]
    tables = [*forward, mixers, *inverse]
    return np.concatenate([table.astype(ml_dtypes.bfloat16) for table in tables])


def dot(a, b):
    return jnp.dot(a, b, preferred_element_type=f32)


def dot_nt(a, b):
    return lax.dot_general(a, b, (((1,), (1,)), ((), ())), preferred_element_type=f32)


def halves(x):
    high = x.astype(bf16)
    return high, (x - high.astype(f32)).astype(bf16)


def wide(x, axis):
    high, low = halves(x)
    return jnp.concatenate([high, low, high], axis=axis)


def long(table, axis):
    return jnp.concatenate([table[0], table[0], table[1]], axis=axis)


def query_rows(rows, cols, up, down):
    half = rows.shape[1] // 2
    marks = [jnp.full((1, LANES), mark, f32) for mark in (up, down, 0.0, 0.0)]
    places = [rows[:, :half], rows[:, half:], cols[:, :half], cols[:, half:]]
    return [jnp.concatenate(pair, axis=1) for pair in zip(places, marks)]


def pack_kernel(cells, charges, fill, marks, gains, strengths, green, own, copies, message, factors):
    particles = charges.shape[1]
    count = copies.shape[0]
    here = lax.axis_index("bunch")
    lists = 8 * particles // GRID
    for beam in range(2):
        sign = 1 if beam == 0 else -1
        charge = charges[beam : beam + 1, :].astype(f32) * fill[0, beam].astype(f32)
        rows = cells[beam, 0, 0:1, :].astype(f32)
        cols = cells[beam, 0, 1:2, :].astype(f32)
        for part in range(particles // GRID):
            lanes = slice(part * GRID, (part + 1) * GRID)
            for row, value in enumerate((charge, rows, cols)):
                at = 8 * part + 4 * beam + row
                message[at : at + 1, :] = value[:, lanes].astype(bf16)
        for offset in range(REACH):
            up = marks[beam, 0, 0, offset - 1].astype(f32) if offset else 0.0
            down = marks[beam, 1, 0, offset + 1].astype(f32) if offset < STOPS - 1 else 0.0
            target = own if offset == 0 else copies.at[lax.rem(here + sign * offset + count, count)]
            for row, value in enumerate(query_rows(rows, cols, up, down)):
                target[4 * beam + row : 4 * beam + row + 1, :] = value.astype(bf16)
    message[lists:, :] = green[...].astype(bf16)
    for stop in range(STOPS):
        factors[stop : stop + 1, :] = jnp.full((1, 2 * LANES), gains[stop], f32)
        product = gains[stop] * strengths[stop]
        factors[STOPS + stop : STOPS + stop + 1, :] = jnp.full((1, 2 * LANES), product, f32)


def field_kernel(tiles, *refs):
    here = lax.axis_index("tile")
    messages = refs[:tiles]
    far, out, near, gathered, densities, arrived = refs[tiles:]
    early = near.shape[0] - INVERSE_TABLES
    fetch = [
        pltpu.make_async_copy(far.at[:early], near.at[:early], arrived.at[0]),
        pltpu.make_async_copy(far.at[early:], near.at[early:], arrived.at[1]),
    ]
    for copy in fetch:
        copy.start()
    lists = messages[0].shape[0] - GRID // tiles
    columns = GRID // tiles
    for step in range(tiles):
        start = pl.multiple_of(relative(here, step, tiles) * columns, columns)
        gathered[pl.ds(start, columns), :] = messages[step][lists:, :]

    @pl.when(here >= 0)
    def deposit():
        cells = lax.broadcasted_iota(jnp.int32, (GRID, GRID), 0).astype(f32)
        for beam in range(2):
            row_hots, col_hots = [], []
            for message in messages:
                for part in range(lists // 8):
                    base = 8 * part + 4 * beam
                    charge = message[base : base + 1, :].astype(f32)
                    rows = message[base + 1 : base + 2, :].astype(f32)
                    cols = message[base + 2 : base + 3, :].astype(f32)
                    row_hots.append(jnp.where(cells == rows, 1.0, 0.0).astype(bf16))
                    col_hots.append(jnp.where(cells == cols, charge, 0.0).astype(bf16))
            density = dot_nt(jnp.concatenate(col_hots, axis=1), jnp.concatenate(row_hots, axis=1))
            densities[:, beam * GRID : (beam + 1) * GRID] = wide(density, 0)

    fetch[0].wait()
    alpha, beta = (
        dot(near[side], turned[0]) + dot(near[side], turned[1])
        for side, turned in (
            (side, halves(dot(gathered[...], near[side + 1]))) for side in (4, 6)
        )
    )
    first = dot(long(near[0:2], 1), densities[...])
    first = jnp.concatenate([first[:, :GRID], first[:, GRID:]], axis=0)
    spectra = dot(wide(first, 1), long(near[2:4], 0))
    scaled = []
    for beam in range(2):
        spectrum = spectra[beam * GRID : (beam + 1) * GRID]
        swapped = jnp.concatenate(
            [
                jnp.concatenate([spectrum[HALF:, HALF:], spectrum[HALF:, :HALF]], axis=1),
                jnp.concatenate([spectrum[:HALF, HALF:], spectrum[:HALF, :HALF]], axis=1),
            ],
            axis=0,
        )
        scaled.append(alpha * spectrum + beta * swapped)
    fetch[1].wait()
    left = jnp.concatenate([long(near[10:12], 1), long(near[12:14], 1)], axis=0)
    part = dot(left, wide(jnp.concatenate(scaled, axis=1), 0)).astype(bf16)
    for axis, right in enumerate((8, 0)):
        rows = part[axis * GRID : (axis + 1) * GRID]
        rows = jnp.concatenate([rows[:, :GRID], rows[:, GRID:]], axis=0)
        field = dot(rows, near[right]) + dot(rows, near[right + 1])
        for beam in range(2):
            out[beam, axis * GRID : (axis + 1) * GRID, :] = field[
                beam * GRID : (beam + 1) * GRID
            ].astype(bf16)


def kick_kernel(count, factors, fields, own, queries, home, away):
    half = queries.shape[-1] - LANES
    here = lax.axis_index("bunch")
    block = 2 * LANES
    cells = lax.broadcasted_iota(jnp.int32, (GRID, block), 0).astype(f32)
    bands = lax.broadcasted_iota(jnp.int32, (BANDS, block), 0).astype(f32)
    for offset in range(REACH):
        for beam in range(2):
            sign = 1 if beam == 0 else -1
            target = lax.rem(here - sign * offset + count, count)
            source = queries.at[target] if offset else own
            base = 4 * beam

            def weight_of(stop, row):
                mark = source[base + row : base + row + 1, half:].astype(f32)
                return jnp.concatenate([mark, mark], axis=1) * factors[STOPS + stop : STOPS + stop + 1, :]

            middle = factors[offset : offset + 1, :] if offset < STOPS else None
            up = weight_of(offset - 1, 0) if offset else None
            down = weight_of(offset + 1, 1) if offset < STOPS - 1 else None
            for start in range(0, 2 * half, block):
                row, lanes = base + start // half, pl.ds(start % half, block)
                rows = source[row : row + 1, lanes].astype(f32)
                cols = source[row + 2 : row + 3, lanes].astype(f32)
                band = jnp.floor(cols * (1.0 / OFFSET_CELLS))
                inside = jnp.broadcast_to(cols - band * OFFSET_CELLS, (BANDS, block))
                hot = jnp.where(cells == rows, 1.0, 0.0).astype(bf16)
                values = dot(fields[1 - beam], hot)
                picked = [jnp.zeros((BANDS, block), f32) for _ in range(2)]
                for place in range(OFFSET_CELLS):
                    hit = inside == place
                    for axis in range(2):
                        at = axis * GRID + place * BANDS
                        picked[axis] = jnp.where(hit, values[at : at + BANDS, :], picked[axis])
                weight = jnp.zeros((BANDS, block), f32)
                if middle is not None:
                    weight = jnp.where(bands == band, middle, weight)
                if up is not None:
                    weight = jnp.where(bands == band - 1, up, weight)
                if down is not None:
                    weight = jnp.where(bands == band + 1, down, weight)
                kick = [jnp.sum(weight * value, axis=0, keepdims=True) for value in picked]
                kick = jnp.concatenate(kick, axis=0)
                if offset == 0:
                    home[2 * beam : 2 * beam + 2, start : start + block] = kick
                elif shared(offset, count):
                    away[target, 2 * beam : 2 * beam + 2, start : start + block] = kick.astype(bf16)
                else:
                    away[target, :, start : start + block] = jnp.concatenate(halves(kick), axis=0)


def shared(offset, count):
    return 2 * offset == count


def final_kernel(count, received, home, momenta, out):
    here = lax.axis_index("bunch")
    for beam in range(2):
        sign = 1 if beam == 0 else -1
        total = home[2 * beam : 2 * beam + 2, :]
        for offset in range(1, REACH):
            part = received[lax.rem(here + sign * offset + count, count)].astype(f32)
            if shared(offset, count):
                total = total + part[2 * beam : 2 * beam + 2]
            else:
                total = total + (part[:2] + part[2:])
        out[beam, 0] = momenta[beam, 0] + total.astype(bf16).astype(f32)


SMEM = pl.BlockSpec(memory_space=pltpu.SMEM)
VMEM = pl.BlockSpec(memory_space=pltpu.VMEM)
FAR = pl.BlockSpec(memory_space=pltpu.HBM)
LIMIT = pltpu.CompilerParams(vmem_limit_bytes=48 * 1024 * 1024)
SMALL = pltpu.CompilerParams(vmem_limit_bytes=16 * 1024 * 1024)


def kept_far(value):
    return pltpu.with_memory_space_constraint(value, pltpu.HBM)


def is_power_of_two(count):
    return count & (count - 1) == 0


def relative(index, step, count):
    if is_power_of_two(count):
        return jnp.bitwise_xor(index, step)
    return lax.rem(index - step + count, count)


def exchanged(value, axis, step):
    count = lax.axis_size(axis)
    if is_power_of_two(count):
        pairs = [(i, i ^ step) for i in range(count)]
    else:
        pairs = [(i, (i + step) % count) for i in range(count)]
    return lax.ppermute(value, axis, pairs)


def body(cell_index, charges, momenta, fill_pattern, encounters, green_spectrum, stop_gain, parasitic_gain):
    particles = cell_index.shape[3]
    tiles = lax.axis_size("tile")
    count = lax.axis_size("bunch")
    tables = make_tables()
    columns = green_spectrum.shape[1]
    own, copies, message, factors = pl.pallas_call(
        pack_kernel,
        out_shape=(
            jax.ShapeDtypeStruct((8, particles // 2 + LANES), bf16),
            jax.ShapeDtypeStruct((count, 8, particles // 2 + LANES), bf16),
            jax.ShapeDtypeStruct((8 * particles // GRID + columns, GRID), bf16),
            jax.ShapeDtypeStruct((2 * STOPS, 2 * LANES), f32),
        ),
        in_specs=[VMEM, VMEM, SMEM, SMEM, SMEM, SMEM, VMEM],
        out_specs=(VMEM, VMEM, VMEM, VMEM),
        compiler_params=SMALL,
    )(
        kept_far(cell_index),
        kept_far(charges.reshape(2, particles)),
        kept_far(fill_pattern.T),
        kept_far(jnp.transpose(encounters, (1, 2, 3, 0))),
        kept_far(stop_gain),
        kept_far(parasitic_gain),
        kept_far(green_spectrum.T),
    )
    messages = [message] + [exchanged(message, "tile", step) for step in range(1, tiles)]
    queries = lax.all_to_all(copies, "bunch", split_axis=0, concat_axis=0, tiled=True)
    fields = pl.pallas_call(
        functools.partial(field_kernel, tiles),
        out_shape=jax.ShapeDtypeStruct((2, 2 * GRID, GRID), bf16),
        in_specs=[VMEM] * tiles + [FAR],
        out_specs=VMEM,
        scratch_shapes=[
            pltpu.VMEM(tables.shape, bf16),
            pltpu.VMEM((GRID, GRID), bf16),
            pltpu.VMEM((3 * GRID, 2 * GRID), bf16),
            pltpu.SemaphoreType.DMA((2,)),
        ],
        compiler_params=LIMIT,
        cost_estimate=pl.CostEstimate(flops=3000000000, bytes_accessed=1000000, transcendentals=0),
    )(*messages, kept_far(jnp.asarray(tables)))
    home, away = pl.pallas_call(
        functools.partial(kick_kernel, count),
        out_shape=(
            jax.ShapeDtypeStruct((4, particles), f32),
            jax.ShapeDtypeStruct((count, 4, particles), bf16),
        ),
        in_specs=[VMEM, VMEM, VMEM, VMEM],
        out_specs=(VMEM, VMEM),
        compiler_params=LIMIT,
    )(factors, fields, own, queries)
    received = lax.all_to_all(away, "bunch", split_axis=0, concat_axis=0, tiled=True)
    return pl.pallas_call(
        functools.partial(final_kernel, count),
        out_shape=jax.ShapeDtypeStruct(momenta.shape, f32),
        in_specs=[VMEM, VMEM, VMEM],
        out_specs=VMEM,
        compiler_params=SMALL,
    )(received, home, momenta)


def solution(mesh):
    in_specs = (
        P(None, "bunch", None, "tile"),
        P(None, "bunch", "tile"),
        P(None, "bunch", None, "tile"),
        P(None, "bunch"),
        P(None, None, None, "bunch"),
        P(None, "tile"),
        P(),
        P(),
    )
    out_specs = P(None, "bunch", None, "tile")
    return jax.shard_map(body, mesh=mesh, in_specs=in_specs, out_specs=out_specs, check_vma=False)
```

```python
import functools
import math

import jax
import jax.numpy as jnp
import ml_dtypes
import numpy as np
from jax import lax
from jax.experimental import pallas as pl
from jax.experimental.pallas import tpu as pltpu
from jax.sharding import PartitionSpec as P

GRID = 256
HALF = GRID // 2
STOPS = 4
OFFSET_CELLS = 32
BANDS = GRID // OFFSET_CELLS
REACH = STOPS + 1
INVERSE_TABLES = 6
LANES = 128
f32 = jnp.float32
bf16 = jnp.bfloat16


def split_table(table):
    high = table.astype(ml_dtypes.bfloat16)
    low = (table - high.astype(np.float64)).astype(ml_dtypes.bfloat16)
    return np.stack([high, low])


@functools.cache
def make_tables():
    cells = np.arange(GRID)
    wave = np.where(cells <= HALF, cells, cells - HALF)
    is_sin = cells > HALF
    angle = 2 * np.pi * ((cells[:, None] * wave[None, :]) % GRID) / GRID
    basis = np.where(is_sin[None, :], np.sin(angle), np.cos(angle))
    slope = -0.5 * (np.roll(basis, -1, 0) - np.roll(basis, 1, 0))
    order = OFFSET_CELLS * (cells % BANDS) + cells // BANDS
    here = (cells[None, :] == wave[:, None]).astype(np.float64)
    there = (cells[None, :] == (-wave[:, None]) % GRID).astype(np.float64)
    count = np.where((wave == 0) | (wave == HALF), 1.0, 2.0)[:, None] / GRID
    sign = np.where(is_sin, -1.0, 1.0)[:, None]
    even = 0.5 * (here + there) * count
    odd = 0.5 * (here - there) * count
    mixers = np.stack([even, even.T, odd * sign, -(odd * sign).T])
    forward = [split_table(basis.T), split_table(basis)]
    inverse = [split_table(table) for table in (slope.T, basis[order], slope[order])]
    tables = [*forward, mixers, *inverse]
    return np.concatenate([table.astype(ml_dtypes.bfloat16) for table in tables])


def dot(a, b):
    return jnp.dot(a, b, preferred_element_type=f32)


def dot_nt(a, b):
    return lax.dot_general(a, b, (((1,), (1,)), ((), ())), preferred_element_type=f32)


def halves(x):
    high = x.astype(bf16)
    return high, (x - high.astype(f32)).astype(bf16)


def wide(x, axis):
    high, low = halves(x)
    return jnp.concatenate([high, low, high], axis=axis)


def long(table, axis):
    return jnp.concatenate([table[0], table[0], table[1]], axis=axis)


def query_rows(rows, cols, up, down):
    half = rows.shape[1] // 2
    marks = [jnp.full((1, LANES), mark, f32) for mark in (up, down, 0.0, 0.0)]
    places = [rows[:, :half], rows[:, half:], cols[:, :half], cols[:, half:]]
    return [jnp.concatenate(pair, axis=1) for pair in zip(places, marks)]


def deposit(messages, lists, beam):
    cells = lax.broadcasted_iota(jnp.int32, (GRID, GRID), 0).astype(f32)
    row_hots, col_hots = [], []
    for message in messages:
        for part in range(lists // 8):
            base = 8 * part + 4 * beam
            charge = message[base : base + 1, :].astype(f32)
            rows = message[base + 1 : base + 2, :].astype(f32)
            cols = message[base + 2 : base + 3, :].astype(f32)
            row_hots.append(jnp.where(cells == rows, 1.0, 0.0).astype(bf16))
            col_hots.append(jnp.where(cells == cols, charge, 0.0).astype(bf16))
    return dot_nt(jnp.concatenate(col_hots, axis=1), jnp.concatenate(row_hots, axis=1))


def pack_kernel(cells, charges, fill, marks, gains, strengths, green, own, copies, message, factors, far, partial, sent):
    particles = charges.shape[1]
    count = copies.shape[0]
    here = lax.axis_index("bunch")
    lists = 8 * particles // GRID
    for beam in range(2):
        sign = 1 if beam == 0 else -1
        charge = charges[beam : beam + 1, :].astype(f32) * fill[0, beam].astype(f32)
        rows = cells[beam, 0, 0:1, :].astype(f32)
        cols = cells[beam, 0, 1:2, :].astype(f32)
        for part in range(particles // GRID):
            lanes = slice(part * GRID, (part + 1) * GRID)
            for row, value in enumerate((charge, rows, cols)):
                at = 8 * part + 4 * beam + row
                message[at : at + 1, :] = value[:, lanes].astype(bf16)
        for offset in range(REACH):
            up = marks[beam, 0, 0, offset - 1].astype(f32) if offset else 0.0
            down = marks[beam, 1, 0, offset + 1].astype(f32) if offset < STOPS - 1 else 0.0
            target = own if offset == 0 else copies.at[count - 1 - lax.rem(here + sign * offset + count, count)]
            for row, value in enumerate(query_rows(rows, cols, up, down)):
                target[4 * beam + row : 4 * beam + row + 1, :] = value.astype(bf16)

    message[lists:, :] = green[...].astype(bf16)
    for stop in range(STOPS):
        factors[stop : stop + 1, :] = jnp.full((1, 2 * LANES), gains[stop], f32)
        product = gains[stop] * strengths[stop]
        factors[STOPS + stop : STOPS + stop + 1, :] = jnp.full((1, 2 * LANES), product, f32)

    @pl.when(is_early())
    def start():
        pltpu.make_async_copy(copies, far, sent).start()

    @pl.when(is_early())
    def work():
        for beam in range(2):
            partial[:, beam * GRID : (beam + 1) * GRID] = deposit([message], lists, beam)
        pltpu.make_async_copy(copies, far, sent).wait()


def is_early():
    return lax.axis_index("tile") < lax.axis_size("tile") // 2


def late_kernel(copies, far, out, sent):
    @pl.when(jnp.logical_not(is_early()))
    def write():
        copy = pltpu.make_async_copy(copies, out, sent)
        copy.start()
        copy.wait()


def field_kernel(tiles, *refs):
    here = lax.axis_index("tile")
    messages = refs[:tiles]
    partial, far, out, near, gathered, densities, arrived = refs[tiles:]
    early = near.shape[0] - INVERSE_TABLES
    fetch = [
        pltpu.make_async_copy(far.at[:early], near.at[:early], arrived.at[0]),
        pltpu.make_async_copy(far.at[early:], near.at[early:], arrived.at[1]),
    ]
    for copy in fetch:
        copy.start()
    lists = messages[0].shape[0] - GRID // tiles
    columns = GRID // tiles
    for step, message in zip(steps_of(tiles), messages):
        start = pl.multiple_of(relative(here, step, tiles) * columns, columns)
        gathered[pl.ds(start, columns), :] = message[lists:, :]

    @pl.when(is_early())
    def add_others():
        for beam in range(2):
            lanes = slice(beam * GRID, (beam + 1) * GRID)
            density = partial[:, lanes] + deposit(messages[1:], lists, beam)
            densities[:, lanes] = wide(density, 0)

    @pl.when(jnp.logical_not(is_early()))
    def add_all():
        for beam in range(2):
            density = deposit(messages, lists, beam)
            densities[:, beam * GRID : (beam + 1) * GRID] = wide(density, 0)

    fetch[0].wait()
    alpha, beta = (
        dot(near[side], turned[0]) + dot(near[side], turned[1])
        for side, turned in (
            (side, halves(dot(gathered[...], near[side + 1]))) for side in (4, 6)
        )
    )
    first = dot(long(near[0:2], 1), densities[...])
    first = jnp.concatenate([first[:, :GRID], first[:, GRID:]], axis=0)
    spectra = dot(wide(first, 1), long(near[2:4], 0))
    scaled = []
    for beam in range(2):
        spectrum = spectra[beam * GRID : (beam + 1) * GRID]
        swapped = jnp.concatenate(
            [
                jnp.concatenate([spectrum[HALF:, HALF:], spectrum[HALF:, :HALF]], axis=1),
                jnp.concatenate([spectrum[:HALF, HALF:], spectrum[:HALF, :HALF]], axis=1),
            ],
            axis=0,
        )
        scaled.append(alpha * spectrum + beta * swapped)
    fetch[1].wait()
    left = jnp.concatenate([long(near[10:12], 1), long(near[12:14], 1)], axis=0)
    part = dot(left, wide(jnp.concatenate(scaled, axis=1), 0)).astype(bf16)
    for axis, right in enumerate((8, 0)):
        rows = part[axis * GRID : (axis + 1) * GRID]
        rows = jnp.concatenate([rows[:, :GRID], rows[:, GRID:]], axis=0)
        field = dot(rows, near[right]) + dot(rows, near[right + 1])
        for beam in range(2):
            out[beam, axis * GRID : (axis + 1) * GRID, :] = field[
                beam * GRID : (beam + 1) * GRID
            ].astype(bf16)


def kick_kernel(count, factors, fields, own, queries, home, away):
    half = queries.shape[-1] - LANES
    here = lax.axis_index("bunch")
    block = 2 * LANES
    cells = lax.broadcasted_iota(jnp.int32, (GRID, block), 0).astype(f32)
    bands = lax.broadcasted_iota(jnp.int32, (BANDS, block), 0).astype(f32)
    for offset in range(REACH):
        for beam in range(2):
            sign = 1 if beam == 0 else -1
            target = count - 1 - lax.rem(here - sign * offset + count, count)
            source = queries.at[target] if offset else own
            base = 4 * beam

            def weight_of(stop, row):
                mark = source[base + row : base + row + 1, half:].astype(f32)
                return jnp.concatenate([mark, mark], axis=1) * factors[STOPS + stop : STOPS + stop + 1, :]

            middle = factors[offset : offset + 1, :] if offset < STOPS else None
            up = weight_of(offset - 1, 0) if offset else None
            down = weight_of(offset + 1, 1) if offset < STOPS - 1 else None
            for start in range(0, 2 * half, block):
                row, lanes = base + start // half, pl.ds(start % half, block)
                rows = source[row : row + 1, lanes].astype(f32)
                cols = source[row + 2 : row + 3, lanes].astype(f32)
                band = jnp.floor(cols * (1.0 / OFFSET_CELLS))
                inside = jnp.broadcast_to(cols - band * OFFSET_CELLS, (BANDS, block))
                hot = jnp.where(cells == rows, 1.0, 0.0).astype(bf16)
                values = dot(fields[1 - beam], hot)
                picked = [jnp.zeros((BANDS, block), f32) for _ in range(2)]
                for place in range(OFFSET_CELLS):
                    hit = inside == place
                    for axis in range(2):
                        at = axis * GRID + place * BANDS
                        picked[axis] = jnp.where(hit, values[at : at + BANDS, :], picked[axis])
                weight = jnp.zeros((BANDS, block), f32)
                if middle is not None:
                    weight = jnp.where(bands == band, middle, weight)
                if up is not None:
                    weight = jnp.where(bands == band - 1, up, weight)
                if down is not None:
                    weight = jnp.where(bands == band + 1, down, weight)
                kick = [jnp.sum(weight * value, axis=0, keepdims=True) for value in picked]
                kick = jnp.concatenate(kick, axis=0)
                if offset == 0:
                    home[2 * beam : 2 * beam + 2, start : start + block] = kick
                elif shared(offset, count):
                    away[target, 2 * beam : 2 * beam + 2, start : start + block] = kick.astype(bf16)
                else:
                    away[target, :, start : start + block] = jnp.concatenate(halves(kick), axis=0)


def shared(offset, count):
    return 2 * offset == count


def final_kernel(count, received, home, momenta, out):
    here = lax.axis_index("bunch")
    for beam in range(2):
        sign = 1 if beam == 0 else -1
        total = home[2 * beam : 2 * beam + 2, :]
        for offset in range(1, REACH):
            part = received[count - 1 - lax.rem(here + sign * offset + count, count)].astype(f32)
            if shared(offset, count):
                total = total + part[2 * beam : 2 * beam + 2]
            else:
                total = total + (part[:2] + part[2:])
        out[beam, 0] = momenta[beam, 0] + total.astype(bf16).astype(f32)


SMEM = pl.BlockSpec(memory_space=pltpu.SMEM)
VMEM = pl.BlockSpec(memory_space=pltpu.VMEM)
FAR = pl.BlockSpec(memory_space=pltpu.HBM)
LIMIT = pltpu.CompilerParams(vmem_limit_bytes=48 * 1024 * 1024)
SMALL = pltpu.CompilerParams(vmem_limit_bytes=16 * 1024 * 1024)


def kept_far(value):
    return pltpu.with_memory_space_constraint(value, pltpu.HBM)


def steps_of(tiles):
    return [0, *[1, 3, 2]] if tiles == 4 else list(range(tiles))


def is_power_of_two(count):
    return count & (count - 1) == 0


def relative(index, step, count):
    if is_power_of_two(count):
        return jnp.bitwise_xor(index, step)
    return lax.rem(index - step + count, count)


def exchanged(value, axis, step):
    count = lax.axis_size(axis)
    if is_power_of_two(count):
        pairs = [(i, i ^ step) for i in range(count)]
    else:
        pairs = [(i, (i + step) % count) for i in range(count)]
    return lax.ppermute(value, axis, pairs)


def body(cell_index, charges, momenta, fill_pattern, encounters, green_spectrum, stop_gain, parasitic_gain):
    particles = cell_index.shape[3]
    tiles = lax.axis_size("tile")
    count = lax.axis_size("bunch")
    tables = make_tables()
    columns = green_spectrum.shape[1]
    own, staged, message, factors, copies, partial = pl.pallas_call(
        pack_kernel,
        out_shape=(
            jax.ShapeDtypeStruct((8, particles // 2 + LANES), bf16),
            jax.ShapeDtypeStruct((count, 8, particles // 2 + LANES), bf16),
            jax.ShapeDtypeStruct((8 * particles // GRID + columns, GRID), bf16),
            jax.ShapeDtypeStruct((2 * STOPS, 2 * LANES), f32),
            jax.ShapeDtypeStruct((count, 8, particles // 2 + LANES), bf16),
            jax.ShapeDtypeStruct((GRID, 2 * GRID), f32),
        ),
        in_specs=[VMEM, VMEM, SMEM, SMEM, SMEM, SMEM, VMEM],
        out_specs=(VMEM, VMEM, VMEM, VMEM, FAR, VMEM),
        scratch_shapes=[pltpu.SemaphoreType.DMA],
        compiler_params=SMALL,
    )(
        kept_far(cell_index),
        kept_far(charges.reshape(2, particles)),
        kept_far(fill_pattern.T),
        kept_far(jnp.transpose(encounters, (1, 2, 3, 0))),
        kept_far(stop_gain),
        kept_far(parasitic_gain),
        kept_far(green_spectrum.T),
    )
    copies = pl.pallas_call(
        late_kernel,
        out_shape=jax.ShapeDtypeStruct(copies.shape, bf16),
        in_specs=[VMEM, FAR],
        out_specs=FAR,
        scratch_shapes=[pltpu.SemaphoreType.DMA],
        input_output_aliases={1: 0},
        compiler_params=SMALL,
    )(staged, copies)
    messages = [message] + [exchanged(message, "tile", step) for step in steps_of(tiles)[1:]]
    queries = lax.all_to_all(copies, "bunch", split_axis=0, concat_axis=0, tiled=True, axis_index_groups=[list(reversed(range(count)))])
    fields = pl.pallas_call(
        functools.partial(field_kernel, tiles),
        out_shape=jax.ShapeDtypeStruct((2, 2 * GRID, GRID), bf16),
        in_specs=[VMEM] * (tiles + 1) + [FAR],
        out_specs=VMEM,
        scratch_shapes=[
            pltpu.VMEM(tables.shape, bf16),
            pltpu.VMEM((GRID, GRID), bf16),
            pltpu.VMEM((3 * GRID, 2 * GRID), bf16),
            pltpu.SemaphoreType.DMA((2,)),
        ],
        compiler_params=LIMIT,
        cost_estimate=pl.CostEstimate(flops=3000000000, bytes_accessed=1000000, transcendentals=0),
    )(*messages, partial, kept_far(jnp.asarray(tables)))
    home, away = pl.pallas_call(
        functools.partial(kick_kernel, count),
        out_shape=(
            jax.ShapeDtypeStruct((4, particles), f32),
            jax.ShapeDtypeStruct((count, 4, particles), bf16),
        ),
        in_specs=[VMEM, VMEM, VMEM, VMEM],
        out_specs=(VMEM, VMEM),
        compiler_params=LIMIT,
    )(factors, fields, own, queries)
    received = lax.all_to_all(away, "bunch", split_axis=0, concat_axis=0, tiled=True, axis_index_groups=[list(reversed(range(count)))])
    return pl.pallas_call(
        functools.partial(final_kernel, count),
        out_shape=jax.ShapeDtypeStruct(momenta.shape, f32),
        in_specs=[VMEM, VMEM, VMEM],
        out_specs=VMEM,
        compiler_params=SMALL,
    )(received, home, momenta)


def solution(mesh):
    in_specs = (
        P(None, "bunch", None, "tile"),
        P(None, "bunch", "tile"),
        P(None, "bunch", None, "tile"),
        P(None, "bunch"),
        P(None, None, None, "bunch"),
        P(None, "tile"),
        P(),
        P(),
    )
    out_specs = P(None, "bunch", None, "tile")
    return jax.shard_map(body, mesh=mesh, in_specs=in_specs, out_specs=out_specs, check_vma=False)
```

```python
import functools
import math

import jax
import jax.numpy as jnp
import ml_dtypes
import numpy as np
from jax import lax
from jax.experimental import pallas as pl
from jax.experimental.pallas import tpu as pltpu
from jax.sharding import PartitionSpec as P

GRID = 256
HALF = GRID // 2
STOPS = 4
OFFSET_CELLS = 32
BANDS = GRID // OFFSET_CELLS
REACH = STOPS + 1
INVERSE_TABLES = 6
LANES = 128
f32 = jnp.float32
bf16 = jnp.bfloat16


def split_table(table):
    high = table.astype(ml_dtypes.bfloat16)
    low = (table - high.astype(np.float64)).astype(ml_dtypes.bfloat16)
    return np.stack([high, low])


@functools.cache
def make_tables():
    cells = np.arange(GRID)
    wave = np.where(cells <= HALF, cells, cells - HALF)
    is_sin = cells > HALF
    angle = 2 * np.pi * ((cells[:, None] * wave[None, :]) % GRID) / GRID
    basis = np.where(is_sin[None, :], np.sin(angle), np.cos(angle))
    slope = -0.5 * (np.roll(basis, -1, 0) - np.roll(basis, 1, 0))
    order = OFFSET_CELLS * (cells % BANDS) + cells // BANDS
    here = (cells[None, :] == wave[:, None]).astype(np.float64)
    there = (cells[None, :] == (-wave[:, None]) % GRID).astype(np.float64)
    count = np.where((wave == 0) | (wave == HALF), 1.0, 2.0)[:, None] / GRID
    sign = np.where(is_sin, -1.0, 1.0)[:, None]
    even = 0.5 * (here + there) * count
    odd = 0.5 * (here - there) * count
    mixers = np.stack([even, even.T, odd * sign, -(odd * sign).T])
    forward = [split_table(basis.T), split_table(basis)]
    inverse = [split_table(table) for table in (slope.T, basis[order], slope[order])]
    tables = [*forward, mixers, *inverse]
    return np.concatenate([table.astype(ml_dtypes.bfloat16) for table in tables])


def dot(a, b):
    return jnp.dot(a, b, preferred_element_type=f32)


def dot_nt(a, b):
    return lax.dot_general(a, b, (((1,), (1,)), ((), ())), preferred_element_type=f32)


def halves(x):
    high = x.astype(bf16)
    return high, (x - high.astype(f32)).astype(bf16)


def wide(x, axis):
    high, low = halves(x)
    return jnp.concatenate([high, low, high], axis=axis)


def long(table, axis):
    return jnp.concatenate([table[0], table[0], table[1]], axis=axis)


def query_rows(rows, cols, up, down):
    half = rows.shape[1] // 2
    marks = [jnp.full((1, LANES), mark, f32) for mark in (up, down, 0.0, 0.0)]
    places = [rows[:, :half], rows[:, half:], cols[:, :half], cols[:, half:]]
    return [jnp.concatenate(pair, axis=1) for pair in zip(places, marks)]


def deposit(messages, columns, beam):
    cells = lax.broadcasted_iota(jnp.int32, (GRID, GRID), 0).astype(f32)
    row_hots, col_hots = [], []
    for message in messages:
        for part in range((message.shape[0] - columns) // 6):
            base = columns + 6 * part + 3 * beam
            charge = message[base : base + 1, :].astype(f32)
            rows = message[base + 1 : base + 2, :].astype(f32)
            cols = message[base + 2 : base + 3, :].astype(f32)
            row_hots.append(jnp.where(cells == rows, 1.0, 0.0).astype(bf16))
            col_hots.append(jnp.where(cells == cols, charge, 0.0).astype(bf16))
    return dot_nt(jnp.concatenate(col_hots, axis=1), jnp.concatenate(row_hots, axis=1))


def pack_kernel(cells, charges, fill, marks, gains, strengths, green, own, copies, message, factors, far, partial, sent):
    particles = charges.shape[1]
    count = copies.shape[0]
    here = lax.axis_index("bunch")
    columns = green.shape[0]
    message[:columns, :] = green[...].astype(bf16)
    for beam in range(2):
        sign = 1 if beam == 0 else -1
        charge = charges[beam : beam + 1, :].astype(f32) * fill[0, beam].astype(f32)
        rows = cells[beam, 0, 0:1, :].astype(f32)
        cols = cells[beam, 0, 1:2, :].astype(f32)
        for part in range(particles // GRID):
            lanes = slice(part * GRID, (part + 1) * GRID)
            for row, value in enumerate((charge, rows, cols)):
                at = columns + 6 * part + 3 * beam + row
                message[at : at + 1, :] = value[:, lanes].astype(bf16)
        for offset in range(REACH):
            up = marks[beam, 0, 0, offset - 1].astype(f32) if offset else 0.0
            down = marks[beam, 1, 0, offset + 1].astype(f32) if offset < STOPS - 1 else 0.0
            target = own if offset == 0 else copies.at[count - 1 - lax.rem(here + sign * offset + count, count)]
            for row, value in enumerate(query_rows(rows, cols, up, down)):
                target[4 * beam + row : 4 * beam + row + 1, :] = value.astype(bf16)

    for stop in range(STOPS):
        factors[stop : stop + 1, :] = jnp.full((1, 2 * LANES), gains[stop], f32)
        product = gains[stop] * strengths[stop]
        factors[STOPS + stop : STOPS + stop + 1, :] = jnp.full((1, 2 * LANES), product, f32)

    @pl.when(is_early())
    def start():
        pltpu.make_async_copy(copies, far, sent).start()

    @pl.when(is_early())
    def work():
        for beam in range(2):
            partial[:, beam * GRID : (beam + 1) * GRID] = deposit([message], columns, beam)
        pltpu.make_async_copy(copies, far, sent).wait()


def is_early():
    return lax.axis_index("tile") < lax.axis_size("tile") // 2


def late_kernel(copies, far, out, sent):
    @pl.when(jnp.logical_not(is_early()))
    def write():
        copy = pltpu.make_async_copy(copies, out, sent)
        copy.start()
        copy.wait()


def field_kernel(tiles, *refs):
    here = lax.axis_index("tile")
    messages = refs[:tiles]
    partial, far, out, near, gathered, densities, arrived = refs[tiles:]
    early = near.shape[0] - INVERSE_TABLES
    fetch = [
        pltpu.make_async_copy(far.at[:early], near.at[:early], arrived.at[0]),
        pltpu.make_async_copy(far.at[early:], near.at[early:], arrived.at[1]),
    ]
    for copy in fetch:
        copy.start()
    columns = GRID // tiles
    for step, message in zip(steps_of(tiles), messages):
        start = pl.multiple_of(relative(here, step, tiles) * columns, columns)
        gathered[pl.ds(start, columns), :] = message[:columns, :]

    @pl.when(is_early())
    def add_others():
        for beam in range(2):
            lanes = slice(beam * GRID, (beam + 1) * GRID)
            density = partial[:, lanes] + deposit(messages[1:], columns, beam)
            densities[:, lanes] = wide(density, 0)

    @pl.when(jnp.logical_not(is_early()))
    def add_all():
        for beam in range(2):
            density = deposit(messages, columns, beam)
            densities[:, beam * GRID : (beam + 1) * GRID] = wide(density, 0)

    fetch[0].wait()
    alpha, beta = (
        dot(near[side], turned[0]) + dot(near[side], turned[1])
        for side, turned in (
            (side, halves(dot(gathered[...], near[side + 1]))) for side in (4, 6)
        )
    )
    first = dot(long(near[0:2], 1), densities[...])
    first = jnp.concatenate([first[:, :GRID], first[:, GRID:]], axis=0)
    spectra = dot(wide(first, 1), long(near[2:4], 0))
    scaled = []
    for beam in range(2):
        spectrum = spectra[beam * GRID : (beam + 1) * GRID]
        swapped = jnp.concatenate(
            [
                jnp.concatenate([spectrum[HALF:, HALF:], spectrum[HALF:, :HALF]], axis=1),
                jnp.concatenate([spectrum[:HALF, HALF:], spectrum[:HALF, :HALF]], axis=1),
            ],
            axis=0,
        )
        scaled.append(alpha * spectrum + beta * swapped)
    fetch[1].wait()
    left = jnp.concatenate([long(near[10:12], 1), long(near[12:14], 1)], axis=0)
    part = dot(left, wide(jnp.concatenate(scaled, axis=1), 0)).astype(bf16)
    for axis, right in enumerate((8, 0)):
        rows = part[axis * GRID : (axis + 1) * GRID]
        rows = jnp.concatenate([rows[:, :GRID], rows[:, GRID:]], axis=0)
        field = dot(rows, near[right]) + dot(rows, near[right + 1])
        for beam in range(2):
            out[beam, axis * GRID : (axis + 1) * GRID, :] = field[
                beam * GRID : (beam + 1) * GRID
            ].astype(bf16)


def kick_kernel(count, factors, fields, own, queries, home, away):
    half = queries.shape[-1] - LANES
    here = lax.axis_index("bunch")
    block = 2 * LANES
    cells = lax.broadcasted_iota(jnp.int32, (GRID, block), 0).astype(f32)
    bands = lax.broadcasted_iota(jnp.int32, (BANDS, block), 0).astype(f32)
    for offset in range(REACH):
        for beam in range(2):
            sign = 1 if beam == 0 else -1
            target = count - 1 - lax.rem(here - sign * offset + count, count)
            source = queries.at[target] if offset else own
            base = 4 * beam

            def weight_of(stop, row):
                mark = source[base + row : base + row + 1, half:].astype(f32)
                return jnp.concatenate([mark, mark], axis=1) * factors[STOPS + stop : STOPS + stop + 1, :]

            middle = factors[offset : offset + 1, :] if offset < STOPS else None
            up = weight_of(offset - 1, 0) if offset else None
            down = weight_of(offset + 1, 1) if offset < STOPS - 1 else None
            for start in range(0, 2 * half, block):
                row, lanes = base + start // half, pl.ds(start % half, block)
                rows = source[row : row + 1, lanes].astype(f32)
                cols = source[row + 2 : row + 3, lanes].astype(f32)
                band = jnp.floor(cols * (1.0 / OFFSET_CELLS))
                inside = jnp.broadcast_to(cols - band * OFFSET_CELLS, (BANDS, block))
                hot = jnp.where(cells == rows, 1.0, 0.0).astype(bf16)
                values = dot(fields[1 - beam], hot)
                picked = [jnp.zeros((BANDS, block), f32) for _ in range(2)]
                for place in range(OFFSET_CELLS):
                    hit = inside == place
                    for axis in range(2):
                        at = axis * GRID + place * BANDS
                        picked[axis] = jnp.where(hit, values[at : at + BANDS, :], picked[axis])
                weight = jnp.zeros((BANDS, block), f32)
                if middle is not None:
                    weight = jnp.where(bands == band, middle, weight)
                if up is not None:
                    weight = jnp.where(bands == band - 1, up, weight)
                if down is not None:
                    weight = jnp.where(bands == band + 1, down, weight)
                kick = [jnp.sum(weight * value, axis=0, keepdims=True) for value in picked]
                kick = jnp.concatenate(kick, axis=0)
                if offset == 0:
                    home[2 * beam : 2 * beam + 2, start : start + block] = kick
                elif shared(offset, count):
                    away[target, 2 * beam : 2 * beam + 2, start : start + block] = kick.astype(bf16)
                else:
                    away[target, :, start : start + block] = jnp.concatenate(halves(kick), axis=0)


def shared(offset, count):
    return 2 * offset == count


def final_kernel(count, received, home, momenta, out):
    here = lax.axis_index("bunch")
    for beam in range(2):
        sign = 1 if beam == 0 else -1
        total = home[2 * beam : 2 * beam + 2, :]
        for offset in range(1, REACH):
            part = received[count - 1 - lax.rem(here + sign * offset + count, count)].astype(f32)
            if shared(offset, count):
                total = total + part[2 * beam : 2 * beam + 2]
            else:
                total = total + (part[:2] + part[2:])
        out[beam, 0] = momenta[beam, 0] + total.astype(bf16).astype(f32)


SMEM = pl.BlockSpec(memory_space=pltpu.SMEM)
VMEM = pl.BlockSpec(memory_space=pltpu.VMEM)
FAR = pl.BlockSpec(memory_space=pltpu.HBM)
LIMIT = pltpu.CompilerParams(vmem_limit_bytes=48 * 1024 * 1024)
SMALL = pltpu.CompilerParams(vmem_limit_bytes=16 * 1024 * 1024)


def kept_far(value):
    return pltpu.with_memory_space_constraint(value, pltpu.HBM)


def steps_of(tiles):
    return [0, *[1, 3, 2]] if tiles == 4 else list(range(tiles))


def is_power_of_two(count):
    return count & (count - 1) == 0


def relative(index, step, count):
    if is_power_of_two(count):
        return jnp.bitwise_xor(index, step)
    return lax.rem(index - step + count, count)


def exchanged(value, axis, step):
    count = lax.axis_size(axis)
    if is_power_of_two(count):
        pairs = [(i, i ^ step) for i in range(count)]
    else:
        pairs = [(i, (i + step) % count) for i in range(count)]
    return lax.ppermute(value, axis, pairs)


def body(cell_index, charges, momenta, fill_pattern, encounters, green_spectrum, stop_gain, parasitic_gain):
    particles = cell_index.shape[3]
    tiles = lax.axis_size("tile")
    count = lax.axis_size("bunch")
    tables = make_tables()
    columns = green_spectrum.shape[1]
    own, staged, message, factors, copies, partial = pl.pallas_call(
        pack_kernel,
        out_shape=(
            jax.ShapeDtypeStruct((8, particles // 2 + LANES), bf16),
            jax.ShapeDtypeStruct((count, 8, particles // 2 + LANES), bf16),
            jax.ShapeDtypeStruct((columns + 6 * particles // GRID, GRID), bf16),
            jax.ShapeDtypeStruct((2 * STOPS, 2 * LANES), f32),
            jax.ShapeDtypeStruct((count, 8, particles // 2 + LANES), bf16),
            jax.ShapeDtypeStruct((GRID, 2 * GRID), f32),
        ),
        in_specs=[VMEM, VMEM, SMEM, SMEM, SMEM, SMEM, VMEM],
        out_specs=(VMEM, VMEM, VMEM, VMEM, FAR, VMEM),
        scratch_shapes=[pltpu.SemaphoreType.DMA],
        compiler_params=SMALL,
    )(
        kept_far(cell_index),
        kept_far(charges.reshape(2, particles)),
        kept_far(fill_pattern.T),
        kept_far(jnp.transpose(encounters, (1, 2, 3, 0))),
        kept_far(stop_gain),
        kept_far(parasitic_gain),
        kept_far(green_spectrum.T),
    )
    copies = pl.pallas_call(
        late_kernel,
        out_shape=jax.ShapeDtypeStruct(copies.shape, bf16),
        in_specs=[VMEM, FAR],
        out_specs=FAR,
        scratch_shapes=[pltpu.SemaphoreType.DMA],
        input_output_aliases={1: 0},
        compiler_params=SMALL,
    )(staged, copies)
    messages = [message] + [exchanged(message, "tile", step) for step in steps_of(tiles)[1:]]
    queries = lax.all_to_all(copies, "bunch", split_axis=0, concat_axis=0, tiled=True, axis_index_groups=[list(reversed(range(count)))])
    fields = pl.pallas_call(
        functools.partial(field_kernel, tiles),
        out_shape=jax.ShapeDtypeStruct((2, 2 * GRID, GRID), bf16),
        in_specs=[VMEM] * (tiles + 1) + [FAR],
        out_specs=VMEM,
        scratch_shapes=[
            pltpu.VMEM(tables.shape, bf16),
            pltpu.VMEM((GRID, GRID), bf16),
            pltpu.VMEM((3 * GRID, 2 * GRID), bf16),
            pltpu.SemaphoreType.DMA((2,)),
        ],
        compiler_params=LIMIT,
        cost_estimate=pl.CostEstimate(flops=3000000000, bytes_accessed=1000000, transcendentals=0),
    )(*messages, partial, kept_far(jnp.asarray(tables)))
    home, away = pl.pallas_call(
        functools.partial(kick_kernel, count),
        out_shape=(
            jax.ShapeDtypeStruct((4, particles), f32),
            jax.ShapeDtypeStruct((count, 4, particles), bf16),
        ),
        in_specs=[VMEM, VMEM, VMEM, VMEM],
        out_specs=(VMEM, VMEM),
        compiler_params=LIMIT,
    )(factors, fields, own, queries)
    received = lax.all_to_all(away, "bunch", split_axis=0, concat_axis=0, tiled=True, axis_index_groups=[list(reversed(range(count)))])
    return pl.pallas_call(
        functools.partial(final_kernel, count),
        out_shape=jax.ShapeDtypeStruct(momenta.shape, f32),
        in_specs=[VMEM, VMEM, VMEM],
        out_specs=VMEM,
        compiler_params=SMALL,
    )(received, home, momenta)


def solution(mesh):
    in_specs = (
        P(None, "bunch", None, "tile"),
        P(None, "bunch", "tile"),
        P(None, "bunch", None, "tile"),
        P(None, "bunch"),
        P(None, None, None, "bunch"),
        P(None, "tile"),
        P(),
        P(),
    )
    out_specs = P(None, "bunch", None, "tile")
    return jax.shard_map(body, mesh=mesh, in_specs=in_specs, out_specs=out_specs, check_vma=False)
```

```python
import functools
import math

import jax
import jax.numpy as jnp
import ml_dtypes
import numpy as np
from jax import lax
from jax.experimental import pallas as pl
from jax.experimental.pallas import tpu as pltpu
from jax.sharding import PartitionSpec as P

GRID = 256
HALF = GRID // 2
STOPS = 4
OFFSET_CELLS = 32
BANDS = GRID // OFFSET_CELLS
REACH = STOPS + 1
INVERSE_TABLES = 6
LANES = 128
f32 = jnp.float32
bf16 = jnp.bfloat16


def split_table(table):
    high = table.astype(ml_dtypes.bfloat16)
    low = (table - high.astype(np.float64)).astype(ml_dtypes.bfloat16)
    return np.stack([high, low])


@functools.cache
def make_tables():
    cells = np.arange(GRID)
    wave = np.where(cells <= HALF, cells, cells - HALF)
    is_sin = cells > HALF
    angle = 2 * np.pi * ((cells[:, None] * wave[None, :]) % GRID) / GRID
    basis = np.where(is_sin[None, :], np.sin(angle), np.cos(angle))
    slope = -0.5 * (np.roll(basis, -1, 0) - np.roll(basis, 1, 0))
    order = OFFSET_CELLS * (cells % BANDS) + cells // BANDS
    here = (cells[None, :] == wave[:, None]).astype(np.float64)
    there = (cells[None, :] == (-wave[:, None]) % GRID).astype(np.float64)
    count = np.where((wave == 0) | (wave == HALF), 1.0, 2.0)[:, None] / GRID
    sign = np.where(is_sin, -1.0, 1.0)[:, None]
    even = 0.5 * (here + there) * count
    odd = 0.5 * (here - there) * count
    mixers = np.stack([even, even.T, odd * sign, -(odd * sign).T])
    forward = [split_table(basis.T), split_table(basis)]
    inverse = [split_table(table) for table in (slope.T, basis[order], slope[order])]
    tables = [*forward, mixers, *inverse]
    return np.concatenate([table.astype(ml_dtypes.bfloat16) for table in tables])


def dot(a, b):
    return jnp.dot(a, b, preferred_element_type=f32)


def dot_nt(a, b):
    return lax.dot_general(a, b, (((1,), (1,)), ((), ())), preferred_element_type=f32)


def halves(x):
    high = x.astype(bf16)
    return high, (x - high.astype(f32)).astype(bf16)


def wide(x, axis):
    high, low = halves(x)
    return jnp.concatenate([high, low, high], axis=axis)


def long(table, axis):
    return jnp.concatenate([table[0], table[0], table[1]], axis=axis)


def query_rows(rows, cols, up, down):
    half = rows.shape[1] // 2
    marks = [jnp.full((1, LANES), mark, f32) for mark in (up, down, 0.0, 0.0)]
    places = [rows[:, :half], rows[:, half:], cols[:, :half], cols[:, half:]]
    return [jnp.concatenate(pair, axis=1) for pair in zip(places, marks)]


def deposit(messages, columns, beam):
    cells = lax.broadcasted_iota(jnp.int32, (GRID, GRID), 0).astype(f32)
    row_hots, col_hots = [], []
    for message in messages:
        for part in range((message.shape[0] - columns) // 6):
            base = columns + 6 * part + 3 * beam
            charge = message[base : base + 1, :].astype(f32)
            rows = message[base + 1 : base + 2, :].astype(f32)
            cols = message[base + 2 : base + 3, :].astype(f32)
            row_hots.append(jnp.where(cells == rows, 1.0, 0.0).astype(bf16))
            col_hots.append(jnp.where(cells == cols, charge, 0.0).astype(bf16))
    return dot_nt(jnp.concatenate(col_hots, axis=1), jnp.concatenate(row_hots, axis=1))


def pack_kernel(cells, charges, fill, marks, gains, strengths, green, own, copies, message, factors, far, partial, sent):
    particles = charges.shape[1]
    count = copies.shape[0]
    here = lax.axis_index("bunch")
    columns = green.shape[0]
    message[:columns, :] = green[...].astype(bf16)
    for beam in range(2):
        sign = 1 if beam == 0 else -1
        charge = charges[beam : beam + 1, :].astype(f32) * fill[0, beam].astype(f32)
        rows = cells[beam, 0, 0:1, :].astype(f32)
        cols = cells[beam, 0, 1:2, :].astype(f32)
        for part in range(particles // GRID):
            lanes = slice(part * GRID, (part + 1) * GRID)
            for row, value in enumerate((charge, rows, cols)):
                at = columns + 6 * part + 3 * beam + row
                message[at : at + 1, :] = value[:, lanes].astype(bf16)
        for offset in range(REACH):
            up = marks[beam, 0, 0, offset - 1].astype(f32) if offset else 0.0
            down = marks[beam, 1, 0, offset + 1].astype(f32) if offset < STOPS - 1 else 0.0
            target = own if offset == 0 else copies.at[count - 1 - lax.rem(here + sign * offset + count, count)]
            for row, value in enumerate(query_rows(rows, cols, up, down)):
                target[4 * beam + row : 4 * beam + row + 1, :] = value.astype(bf16)

    for stop in range(STOPS):
        factors[stop : stop + 1, :] = jnp.full((1, 2 * LANES), gains[stop], f32)
        product = gains[stop] * strengths[stop]
        factors[STOPS + stop : STOPS + stop + 1, :] = jnp.full((1, 2 * LANES), product, f32)

    @pl.when(is_early())
    def start():
        pltpu.make_async_copy(copies, far, sent).start()

    @pl.when(is_early())
    def work():
        for beam in range(2):
            partial[:, beam * GRID : (beam + 1) * GRID] = deposit([message], columns, beam)
        pltpu.make_async_copy(copies, far, sent).wait()


def is_early():
    return lax.axis_index("tile") < 1


def late_kernel(copies, far, out, sent):
    @pl.when(jnp.logical_not(is_early()))
    def write():
        copy = pltpu.make_async_copy(copies, out, sent)
        copy.start()
        copy.wait()


def field_kernel(tiles, *refs):
    here = lax.axis_index("tile")
    messages = refs[:tiles]
    partial, far, out, near, gathered, densities, arrived = refs[tiles:]
    early = near.shape[0] - INVERSE_TABLES
    fetch = [
        pltpu.make_async_copy(far.at[:early], near.at[:early], arrived.at[0]),
        pltpu.make_async_copy(far.at[early:], near.at[early:], arrived.at[1]),
    ]
    for copy in fetch:
        copy.start()
    columns = GRID // tiles
    for step, message in zip(steps_of(tiles), messages):
        start = pl.multiple_of(relative(here, step, tiles) * columns, columns)
        gathered[pl.ds(start, columns), :] = message[:columns, :]

    @pl.when(is_early())
    def add_others():
        for beam in range(2):
            lanes = slice(beam * GRID, (beam + 1) * GRID)
            density = partial[:, lanes] + deposit(messages[1:], columns, beam)
            densities[:, lanes] = wide(density, 0)

    @pl.when(jnp.logical_not(is_early()))
    def add_all():
        for beam in range(2):
            density = deposit(messages, columns, beam)
            densities[:, beam * GRID : (beam + 1) * GRID] = wide(density, 0)

    fetch[0].wait()
    alpha, beta = (
        dot(near[side], turned[0]) + dot(near[side], turned[1])
        for side, turned in (
            (side, halves(dot(gathered[...], near[side + 1]))) for side in (4, 6)
        )
    )
    first = dot(long(near[0:2], 1), densities[...])
    first = jnp.concatenate([first[:, :GRID], first[:, GRID:]], axis=0)
    spectra = dot(wide(first, 1), long(near[2:4], 0))
    scaled = []
    for beam in range(2):
        spectrum = spectra[beam * GRID : (beam + 1) * GRID]
        swapped = jnp.concatenate(
            [
                jnp.concatenate([spectrum[HALF:, HALF:], spectrum[HALF:, :HALF]], axis=1),
                jnp.concatenate([spectrum[:HALF, HALF:], spectrum[:HALF, :HALF]], axis=1),
            ],
            axis=0,
        )
        scaled.append(alpha * spectrum + beta * swapped)
    fetch[1].wait()
    left = jnp.concatenate([long(near[10:12], 1), long(near[12:14], 1)], axis=0)
    part = dot(left, wide(jnp.concatenate(scaled, axis=1), 0)).astype(bf16)
    for axis, right in enumerate((8, 0)):
        rows = part[axis * GRID : (axis + 1) * GRID]
        rows = jnp.concatenate([rows[:, :GRID], rows[:, GRID:]], axis=0)
        field = dot(rows, near[right]) + dot(rows, near[right + 1])
        for beam in range(2):
            out[beam, axis * GRID : (axis + 1) * GRID, :] = field[
                beam * GRID : (beam + 1) * GRID
            ].astype(bf16)


def kick_kernel(count, factors, fields, own, queries, home, away):
    half = queries.shape[-1] - LANES
    here = lax.axis_index("bunch")
    block = 2 * LANES
    cells = lax.broadcasted_iota(jnp.int32, (GRID, block), 0).astype(f32)
    bands = lax.broadcasted_iota(jnp.int32, (BANDS, block), 0).astype(f32)
    for offset in range(REACH):
        for beam in range(2):
            sign = 1 if beam == 0 else -1
            target = count - 1 - lax.rem(here - sign * offset + count, count)
            source = queries.at[target] if offset else own
            base = 4 * beam

            def weight_of(stop, row):
                mark = source[base + row : base + row + 1, half:].astype(f32)
                return jnp.concatenate([mark, mark], axis=1) * factors[STOPS + stop : STOPS + stop + 1, :]

            middle = factors[offset : offset + 1, :] if offset < STOPS else None
            up = weight_of(offset - 1, 0) if offset else None
            down = weight_of(offset + 1, 1) if offset < STOPS - 1 else None
            for start in range(0, 2 * half, block):
                row, lanes = base + start // half, pl.ds(start % half, block)
                rows = source[row : row + 1, lanes].astype(f32)
                cols = source[row + 2 : row + 3, lanes].astype(f32)
                band = jnp.floor(cols * (1.0 / OFFSET_CELLS))
                inside = jnp.broadcast_to(cols - band * OFFSET_CELLS, (BANDS, block))
                hot = jnp.where(cells == rows, 1.0, 0.0).astype(bf16)
                values = dot(fields[1 - beam], hot)
                picked = [jnp.zeros((BANDS, block), f32) for _ in range(2)]
                for place in range(OFFSET_CELLS):
                    hit = inside == place
                    for axis in range(2):
                        at = axis * GRID + place * BANDS
                        picked[axis] = jnp.where(hit, values[at : at + BANDS, :], picked[axis])
                weight = jnp.zeros((BANDS, block), f32)
                if middle is not None:
                    weight = jnp.where(bands == band, middle, weight)
                if up is not None:
                    weight = jnp.where(bands == band - 1, up, weight)
                if down is not None:
                    weight = jnp.where(bands == band + 1, down, weight)
                kick = [jnp.sum(weight * value, axis=0, keepdims=True) for value in picked]
                kick = jnp.concatenate(kick, axis=0)
                if offset == 0:
                    home[2 * beam : 2 * beam + 2, start : start + block] = kick
                elif shared(offset, count):
                    away[target, 2 * beam : 2 * beam + 2, start : start + block] = kick.astype(bf16)
                else:
                    away[target, :, start : start + block] = jnp.concatenate(halves(kick), axis=0)


def shared(offset, count):
    return 2 * offset == count


def final_kernel(count, received, home, momenta, out):
    here = lax.axis_index("bunch")
    for beam in range(2):
        sign = 1 if beam == 0 else -1
        total = home[2 * beam : 2 * beam + 2, :]
        for offset in range(1, REACH):
            part = received[count - 1 - lax.rem(here + sign * offset + count, count)].astype(f32)
            if shared(offset, count):
                total = total + part[2 * beam : 2 * beam + 2]
            else:
                total = total + (part[:2] + part[2:])
        out[beam, 0] = momenta[beam, 0] + total.astype(bf16).astype(f32)


SMEM = pl.BlockSpec(memory_space=pltpu.SMEM)
VMEM = pl.BlockSpec(memory_space=pltpu.VMEM)
FAR = pl.BlockSpec(memory_space=pltpu.HBM)
LIMIT = pltpu.CompilerParams(vmem_limit_bytes=48 * 1024 * 1024)
SMALL = pltpu.CompilerParams(vmem_limit_bytes=16 * 1024 * 1024)


def kept_far(value):
    return pltpu.with_memory_space_constraint(value, pltpu.HBM)


def steps_of(tiles):
    return [0, *[1, 3, 2]] if tiles == 4 else list(range(tiles))


def is_power_of_two(count):
    return count & (count - 1) == 0


def relative(index, step, count):
    if is_power_of_two(count):
        return jnp.bitwise_xor(index, step)
    return lax.rem(index - step + count, count)


def exchanged(value, axis, step):
    count = lax.axis_size(axis)
    if is_power_of_two(count):
        pairs = [(i, i ^ step) for i in range(count)]
    else:
        pairs = [(i, (i + step) % count) for i in range(count)]
    return lax.ppermute(value, axis, pairs)


def body(cell_index, charges, momenta, fill_pattern, encounters, green_spectrum, stop_gain, parasitic_gain):
    particles = cell_index.shape[3]
    tiles = lax.axis_size("tile")
    count = lax.axis_size("bunch")
    tables = make_tables()
    columns = green_spectrum.shape[1]
    own, staged, message, factors, copies, partial = pl.pallas_call(
        pack_kernel,
        out_shape=(
            jax.ShapeDtypeStruct((8, particles // 2 + LANES), bf16),
            jax.ShapeDtypeStruct((count, 8, particles // 2 + LANES), bf16),
            jax.ShapeDtypeStruct((columns + 6 * particles // GRID, GRID), bf16),
            jax.ShapeDtypeStruct((2 * STOPS, 2 * LANES), f32),
            jax.ShapeDtypeStruct((count, 8, particles // 2 + LANES), bf16),
            jax.ShapeDtypeStruct((GRID, 2 * GRID), f32),
        ),
        in_specs=[VMEM, VMEM, SMEM, SMEM, SMEM, SMEM, VMEM],
        out_specs=(VMEM, VMEM, VMEM, VMEM, FAR, VMEM),
        scratch_shapes=[pltpu.SemaphoreType.DMA],
        compiler_params=SMALL,
    )(
        kept_far(cell_index),
        kept_far(charges.reshape(2, particles)),
        kept_far(fill_pattern.T),
        kept_far(jnp.transpose(encounters, (1, 2, 3, 0))),
        kept_far(stop_gain),
        kept_far(parasitic_gain),
        kept_far(green_spectrum.T),
    )
    copies = pl.pallas_call(
        late_kernel,
        out_shape=jax.ShapeDtypeStruct(copies.shape, bf16),
        in_specs=[VMEM, FAR],
        out_specs=FAR,
        scratch_shapes=[pltpu.SemaphoreType.DMA],
        input_output_aliases={1: 0},
        compiler_params=SMALL,
    )(staged, copies)
    messages = [message] + [exchanged(message, "tile", step) for step in steps_of(tiles)[1:]]
    queries = lax.all_to_all(copies, "bunch", split_axis=0, concat_axis=0, tiled=True, axis_index_groups=[list(reversed(range(count)))])
    fields = pl.pallas_call(
        functools.partial(field_kernel, tiles),
        out_shape=jax.ShapeDtypeStruct((2, 2 * GRID, GRID), bf16),
        in_specs=[VMEM] * (tiles + 1) + [FAR],
        out_specs=VMEM,
        scratch_shapes=[
            pltpu.VMEM(tables.shape, bf16),
            pltpu.VMEM((GRID, GRID), bf16),
            pltpu.VMEM((3 * GRID, 2 * GRID), bf16),
            pltpu.SemaphoreType.DMA((2,)),
        ],
        compiler_params=LIMIT,
        cost_estimate=pl.CostEstimate(flops=3000000000, bytes_accessed=1000000, transcendentals=0),
    )(*messages, partial, kept_far(jnp.asarray(tables)))
    home, away = pl.pallas_call(
        functools.partial(kick_kernel, count),
        out_shape=(
            jax.ShapeDtypeStruct((4, particles), f32),
            jax.ShapeDtypeStruct((count, 4, particles), bf16),
        ),
        in_specs=[VMEM, VMEM, VMEM, VMEM],
        out_specs=(VMEM, VMEM),
        compiler_params=LIMIT,
    )(factors, fields, own, queries)
    received = lax.all_to_all(away, "bunch", split_axis=0, concat_axis=0, tiled=True, axis_index_groups=[list(reversed(range(count)))])
    return pl.pallas_call(
        functools.partial(final_kernel, count),
        out_shape=jax.ShapeDtypeStruct(momenta.shape, f32),
        in_specs=[VMEM, VMEM, VMEM],
        out_specs=VMEM,
        compiler_params=SMALL,
    )(received, home, momenta)


def solution(mesh):
    in_specs = (
        P(None, "bunch", None, "tile"),
        P(None, "bunch", "tile"),
        P(None, "bunch", None, "tile"),
        P(None, "bunch"),
        P(None, None, None, "bunch"),
        P(None, "tile"),
        P(),
        P(),
    )
    out_specs = P(None, "bunch", None, "tile")
    return jax.shard_map(body, mesh=mesh, in_specs=in_specs, out_specs=out_specs, check_vma=False)
```

```python
import functools
import math

import jax
import jax.numpy as jnp
import ml_dtypes
import numpy as np
from jax import lax
from jax.experimental import pallas as pl
from jax.experimental.pallas import tpu as pltpu
from jax.sharding import PartitionSpec as P

GRID = 256
HALF = GRID // 2
STOPS = 4
OFFSET_CELLS = 32
BANDS = GRID // OFFSET_CELLS
REACH = STOPS + 1
INVERSE_TABLES = 6
LANES = 128
f32 = jnp.float32
bf16 = jnp.bfloat16


def split_table(table):
    high = table.astype(ml_dtypes.bfloat16)
    low = (table - high.astype(np.float64)).astype(ml_dtypes.bfloat16)
    return np.stack([high, low])


@functools.cache
def make_tables():
    cells = np.arange(GRID)
    wave = np.where(cells <= HALF, cells, cells - HALF)
    is_sin = cells > HALF
    angle = 2 * np.pi * ((cells[:, None] * wave[None, :]) % GRID) / GRID
    basis = np.where(is_sin[None, :], np.sin(angle), np.cos(angle))
    slope = -0.5 * (np.roll(basis, -1, 0) - np.roll(basis, 1, 0))
    order = OFFSET_CELLS * (cells % BANDS) + cells // BANDS
    here = (cells[None, :] == wave[:, None]).astype(np.float64)
    there = (cells[None, :] == (-wave[:, None]) % GRID).astype(np.float64)
    count = np.where((wave == 0) | (wave == HALF), 1.0, 2.0)[:, None] / GRID
    sign = np.where(is_sin, -1.0, 1.0)[:, None]
    even = 0.5 * (here + there) * count
    odd = 0.5 * (here - there) * count
    mixers = np.stack([even, even.T, odd * sign, -(odd * sign).T])
    forward = [split_table(basis.T), split_table(basis)]
    inverse = [split_table(table) for table in (slope.T, basis[order], slope[order])]
    tables = [*forward, mixers, *inverse]
    return np.concatenate([table.astype(ml_dtypes.bfloat16) for table in tables])


def dot(a, b):
    return jnp.dot(a, b, preferred_element_type=f32)


def dot_nt(a, b):
    return lax.dot_general(a, b, (((1,), (1,)), ((), ())), preferred_element_type=f32)


def halves(x):
    high = x.astype(bf16)
    return high, (x - high.astype(f32)).astype(bf16)


def wide(x, axis):
    high, low = halves(x)
    return jnp.concatenate([high, low, high], axis=axis)


def long(table, axis):
    return jnp.concatenate([table[0], table[0], table[1]], axis=axis)


def query_rows(rows, cols, up, down):
    half = rows.shape[1] // 2
    marks = [jnp.full((1, LANES), mark, f32) for mark in (up, down, 0.0, 0.0)]
    places = [rows[:, :half], rows[:, half:], cols[:, :half], cols[:, half:]]
    return [jnp.concatenate(pair, axis=1) for pair in zip(places, marks)]


def deposit(messages, columns, beam):
    cells = lax.broadcasted_iota(jnp.int32, (GRID, GRID), 0).astype(f32)
    row_hots, col_hots = [], []
    for message in messages:
        for part in range((message.shape[0] - columns) // 6):
            base = columns + 6 * part + 3 * beam
            charge = message[base : base + 1, :].astype(f32)
            rows = message[base + 1 : base + 2, :].astype(f32)
            cols = message[base + 2 : base + 3, :].astype(f32)
            row_hots.append(jnp.where(cells == rows, 1.0, 0.0).astype(bf16))
            col_hots.append(jnp.where(cells == cols, charge, 0.0).astype(bf16))
    return dot_nt(jnp.concatenate(col_hots, axis=1), jnp.concatenate(row_hots, axis=1))


def pack_kernel(cells, charges, fill, marks, gains, strengths, green, own, copies, message, factors, far, partial, sent):
    particles = charges.shape[1]
    count = copies.shape[0]
    here = lax.axis_index("bunch")
    columns = green.shape[0]
    message[:columns, :] = green[...].astype(bf16)
    for beam in range(2):
        sign = 1 if beam == 0 else -1
        charge = charges[beam : beam + 1, :].astype(f32) * fill[0, beam].astype(f32)
        rows = cells[beam, 0, 0:1, :].astype(f32)
        cols = cells[beam, 0, 1:2, :].astype(f32)
        for part in range(particles // GRID):
            lanes = slice(part * GRID, (part + 1) * GRID)
            for row, value in enumerate((charge, rows, cols)):
                at = columns + 6 * part + 3 * beam + row
                message[at : at + 1, :] = value[:, lanes].astype(bf16)
        for offset in range(REACH):
            up = marks[beam, 0, 0, offset - 1].astype(f32) if offset else 0.0
            down = marks[beam, 1, 0, offset + 1].astype(f32) if offset < STOPS - 1 else 0.0
            target = own if offset == 0 else copies.at[count - 1 - lax.rem(here + sign * offset + count, count)]
            for row, value in enumerate(query_rows(rows, cols, up, down)):
                target[4 * beam + row : 4 * beam + row + 1, :] = value.astype(bf16)

    for stop in range(STOPS):
        factors[stop : stop + 1, :] = jnp.full((1, 2 * LANES), gains[stop], f32)
        product = gains[stop] * strengths[stop]
        factors[STOPS + stop : STOPS + stop + 1, :] = jnp.full((1, 2 * LANES), product, f32)

    @pl.when(is_early())
    def start():
        pltpu.make_async_copy(copies, far, sent).start()

    @pl.when(is_early())
    def work():
        for beam in range(2):
            partial[:, beam * GRID : (beam + 1) * GRID] = deposit([message], columns, beam)
        pltpu.make_async_copy(copies, far, sent).wait()


def is_early():
    return lax.axis_index("tile") < 1


def late_kernel(copies, far, out, sent):
    @pl.when(jnp.logical_not(is_early()))
    def write():
        copy = pltpu.make_async_copy(copies, out, sent)
        copy.start()
        copy.wait()


def field_kernel(tiles, *refs):
    here = lax.axis_index("tile")
    messages = refs[:tiles]
    partial, far, out, near, gathered, densities, arrived = refs[tiles:]
    early = near.shape[0] - INVERSE_TABLES
    fetch = [
        pltpu.make_async_copy(far.at[:early], near.at[:early], arrived.at[0]),
        pltpu.make_async_copy(far.at[early:], near.at[early:], arrived.at[1]),
    ]
    for copy in fetch:
        copy.start()
    columns = GRID // tiles
    for step, message in zip(steps_of(tiles), messages):
        start = pl.multiple_of(relative(here, step, tiles) * columns, columns)
        gathered[pl.ds(start, columns), :] = message[:columns, :]

    @pl.when(is_early())
    def add_others():
        for beam in range(2):
            lanes = slice(beam * GRID, (beam + 1) * GRID)
            density = partial[:, lanes] + deposit(messages[1:], columns, beam)
            densities[:, lanes] = wide(density, 0)

    @pl.when(jnp.logical_not(is_early()))
    def add_all():
        for beam in range(2):
            density = deposit(messages, columns, beam)
            densities[:, beam * GRID : (beam + 1) * GRID] = wide(density, 0)

    fetch[0].wait()
    alpha, beta = (
        dot(near[side], turned[0]) + dot(near[side], turned[1])
        for side, turned in (
            (side, halves(dot(gathered[...], near[side + 1]))) for side in (4, 6)
        )
    )
    first = dot(long(near[0:2], 1), densities[...])
    first = jnp.concatenate([first[:, :GRID], first[:, GRID:]], axis=0)
    spectra = dot(wide(first, 1), long(near[2:4], 0))
    scaled = []
    for beam in range(2):
        spectrum = spectra[beam * GRID : (beam + 1) * GRID]
        swapped = jnp.concatenate(
            [
                jnp.concatenate([spectrum[HALF:, HALF:], spectrum[HALF:, :HALF]], axis=1),
                jnp.concatenate([spectrum[:HALF, HALF:], spectrum[:HALF, :HALF]], axis=1),
            ],
            axis=0,
        )
        scaled.append(alpha * spectrum + beta * swapped)
    fetch[1].wait()
    left = jnp.concatenate([long(near[10:12], 1), long(near[12:14], 1)], axis=0)
    part = dot(left, wide(jnp.concatenate(scaled, axis=1), 0)).astype(bf16)
    for axis, right in enumerate((8, 0)):
        rows = part[axis * GRID : (axis + 1) * GRID]
        rows = jnp.concatenate([rows[:, :GRID], rows[:, GRID:]], axis=0)
        field = dot(rows, near[right]) + dot(rows, near[right + 1])
        for beam in range(2):
            out[beam, axis * GRID : (axis + 1) * GRID, :] = field[
                beam * GRID : (beam + 1) * GRID
            ].astype(bf16)


def kick_kernel(count, factors, fields, own, queries, home, away):
    half = queries.shape[-1] - LANES
    here = lax.axis_index("bunch")
    block = 2 * LANES
    cells = lax.broadcasted_iota(jnp.int32, (GRID, block), 0).astype(f32)
    bands = lax.broadcasted_iota(jnp.int32, (BANDS, block), 0).astype(f32)
    for offset in range(REACH):
        for beam in range(2):
            sign = 1 if beam == 0 else -1
            partner = lax.rem(here - sign * offset + count, count)
            target = back_slot(partner, count)
            source = queries.at[count - 1 - partner] if offset else own
            base = 4 * beam

            def weight_of(stop, row):
                mark = source[base + row : base + row + 1, half:].astype(f32)
                return jnp.concatenate([mark, mark], axis=1) * factors[STOPS + stop : STOPS + stop + 1, :]

            middle = factors[offset : offset + 1, :] if offset < STOPS else None
            up = weight_of(offset - 1, 0) if offset else None
            down = weight_of(offset + 1, 1) if offset < STOPS - 1 else None
            for start in range(0, 2 * half, block):
                row, lanes = base + start // half, pl.ds(start % half, block)
                rows = source[row : row + 1, lanes].astype(f32)
                cols = source[row + 2 : row + 3, lanes].astype(f32)
                band = jnp.floor(cols * (1.0 / OFFSET_CELLS))
                inside = jnp.broadcast_to(cols - band * OFFSET_CELLS, (BANDS, block))
                hot = jnp.where(cells == rows, 1.0, 0.0).astype(bf16)
                values = dot(fields[1 - beam], hot)
                picked = [jnp.zeros((BANDS, block), f32) for _ in range(2)]
                for place in range(OFFSET_CELLS):
                    hit = inside == place
                    for axis in range(2):
                        at = axis * GRID + place * BANDS
                        picked[axis] = jnp.where(hit, values[at : at + BANDS, :], picked[axis])
                weight = jnp.zeros((BANDS, block), f32)
                if middle is not None:
                    weight = jnp.where(bands == band, middle, weight)
                if up is not None:
                    weight = jnp.where(bands == band - 1, up, weight)
                if down is not None:
                    weight = jnp.where(bands == band + 1, down, weight)
                kick = [jnp.sum(weight * value, axis=0, keepdims=True) for value in picked]
                kick = jnp.concatenate(kick, axis=0)
                if offset == 0:
                    home[2 * beam : 2 * beam + 2, start : start + block] = kick
                elif shared(offset, count):
                    away[target, 2 * beam : 2 * beam + 2, start : start + block] = kick.astype(bf16)
                else:
                    away[target, :, start : start + block] = jnp.concatenate(halves(kick), axis=0)


def shared(offset, count):
    return 2 * offset == count


def final_kernel(count, received, home, momenta, out):
    here = lax.axis_index("bunch")
    for beam in range(2):
        sign = 1 if beam == 0 else -1
        total = home[2 * beam : 2 * beam + 2, :]
        for offset in range(1, REACH):
            part = received[back_slot(lax.rem(here + sign * offset + count, count), count)].astype(f32)
            if shared(offset, count):
                total = total + part[2 * beam : 2 * beam + 2]
            else:
                total = total + (part[:2] + part[2:])
        out[beam, 0] = momenta[beam, 0] + total.astype(bf16).astype(f32)


SMEM = pl.BlockSpec(memory_space=pltpu.SMEM)
VMEM = pl.BlockSpec(memory_space=pltpu.VMEM)
FAR = pl.BlockSpec(memory_space=pltpu.HBM)
LIMIT = pltpu.CompilerParams(vmem_limit_bytes=48 * 1024 * 1024)
SMALL = pltpu.CompilerParams(vmem_limit_bytes=16 * 1024 * 1024)


def kept_far(value):
    return pltpu.with_memory_space_constraint(value, pltpu.HBM)


def steps_of(tiles):
    return [0, *[1, 3, 2]] if tiles == 4 else list(range(tiles))


def back_slot(device, count):
    return jnp.where(lax.rem(device, 2) == 1, (count - 1 - device) // 2, count // 2 + (count - 2 - device) // 2)


def is_power_of_two(count):
    return count & (count - 1) == 0


def relative(index, step, count):
    if is_power_of_two(count):
        return jnp.bitwise_xor(index, step)
    return lax.rem(index - step + count, count)


def exchanged(value, axis, step):
    count = lax.axis_size(axis)
    if is_power_of_two(count):
        pairs = [(i, i ^ step) for i in range(count)]
    else:
        pairs = [(i, (i + step) % count) for i in range(count)]
    return lax.ppermute(value, axis, pairs)


def body(cell_index, charges, momenta, fill_pattern, encounters, green_spectrum, stop_gain, parasitic_gain):
    particles = cell_index.shape[3]
    tiles = lax.axis_size("tile")
    count = lax.axis_size("bunch")
    tables = make_tables()
    columns = green_spectrum.shape[1]
    own, staged, message, factors, copies, partial = pl.pallas_call(
        pack_kernel,
        out_shape=(
            jax.ShapeDtypeStruct((8, particles // 2 + LANES), bf16),
            jax.ShapeDtypeStruct((count, 8, particles // 2 + LANES), bf16),
            jax.ShapeDtypeStruct((columns + 6 * particles // GRID, GRID), bf16),
            jax.ShapeDtypeStruct((2 * STOPS, 2 * LANES), f32),
            jax.ShapeDtypeStruct((count, 8, particles // 2 + LANES), bf16),
            jax.ShapeDtypeStruct((GRID, 2 * GRID), f32),
        ),
        in_specs=[VMEM, VMEM, SMEM, SMEM, SMEM, SMEM, VMEM],
        out_specs=(VMEM, VMEM, VMEM, VMEM, FAR, VMEM),
        scratch_shapes=[pltpu.SemaphoreType.DMA],
        compiler_params=SMALL,
    )(
        kept_far(cell_index),
        kept_far(charges.reshape(2, particles)),
        kept_far(fill_pattern.T),
        kept_far(jnp.transpose(encounters, (1, 2, 3, 0))),
        kept_far(stop_gain),
        kept_far(parasitic_gain),
        kept_far(green_spectrum.T),
    )
    copies = pl.pallas_call(
        late_kernel,
        out_shape=jax.ShapeDtypeStruct(copies.shape, bf16),
        in_specs=[VMEM, FAR],
        out_specs=FAR,
        scratch_shapes=[pltpu.SemaphoreType.DMA],
        input_output_aliases={1: 0},
        compiler_params=SMALL,
    )(staged, copies)
    messages = [message] + [exchanged(message, "tile", step) for step in steps_of(tiles)[1:]]
    queries = lax.all_to_all(copies, "bunch", split_axis=0, concat_axis=0, tiled=True, axis_index_groups=[list(reversed(range(count)))])
    fields = pl.pallas_call(
        functools.partial(field_kernel, tiles),
        out_shape=jax.ShapeDtypeStruct((2, 2 * GRID, GRID), bf16),
        in_specs=[VMEM] * (tiles + 1) + [FAR],
        out_specs=VMEM,
        scratch_shapes=[
            pltpu.VMEM(tables.shape, bf16),
            pltpu.VMEM((GRID, GRID), bf16),
            pltpu.VMEM((3 * GRID, 2 * GRID), bf16),
            pltpu.SemaphoreType.DMA((2,)),
        ],
        compiler_params=LIMIT,
        cost_estimate=pl.CostEstimate(flops=3000000000, bytes_accessed=1000000, transcendentals=0),
    )(*messages, partial, kept_far(jnp.asarray(tables)))
    home, away = pl.pallas_call(
        functools.partial(kick_kernel, count),
        out_shape=(
            jax.ShapeDtypeStruct((4, particles), f32),
            jax.ShapeDtypeStruct((count, 4, particles), bf16),
        ),
        in_specs=[VMEM, VMEM, VMEM, VMEM],
        out_specs=(VMEM, VMEM),
        compiler_params=LIMIT,
    )(factors, fields, own, queries)
    order = [*reversed(range(1, count, 2)), *reversed(range(0, count, 2))]
    received = lax.all_to_all(
        away, "bunch", split_axis=0, concat_axis=0, tiled=True, axis_index_groups=[order]
    )
    return pl.pallas_call(
        functools.partial(final_kernel, count),
        out_shape=jax.ShapeDtypeStruct(momenta.shape, f32),
        in_specs=[VMEM, VMEM, VMEM],
        out_specs=VMEM,
        compiler_params=SMALL,
    )(received, home, momenta)


def solution(mesh):
    in_specs = (
        P(None, "bunch", None, "tile"),
        P(None, "bunch", "tile"),
        P(None, "bunch", None, "tile"),
        P(None, "bunch"),
        P(None, None, None, "bunch"),
        P(None, "tile"),
        P(),
        P(),
    )
    out_specs = P(None, "bunch", None, "tile")
    return jax.shard_map(body, mesh=mesh, in_specs=in_specs, out_specs=out_specs, check_vma=False)
```

```python
import functools
import math

import jax
import jax.numpy as jnp
import ml_dtypes
import numpy as np
from jax import lax
from jax.experimental import pallas as pl
from jax.experimental.pallas import tpu as pltpu
from jax.sharding import PartitionSpec as P

GRID = 256
HALF = GRID // 2
STOPS = 4
OFFSET_CELLS = 32
BANDS = GRID // OFFSET_CELLS
REACH = STOPS + 1
FORWARD_TABLES = 4
INVERSE_TABLES = 6
LANES = 128
f32 = jnp.float32
bf16 = jnp.bfloat16


def split_table(table):
    high = table.astype(ml_dtypes.bfloat16)
    low = (table - high.astype(np.float64)).astype(ml_dtypes.bfloat16)
    return np.stack([high, low])


@functools.cache
def make_tables():
    cells = np.arange(GRID)
    wave = np.where(cells <= HALF, cells, cells - HALF)
    is_sin = cells > HALF
    angle = 2 * np.pi * ((cells[:, None] * wave[None, :]) % GRID) / GRID
    basis = np.where(is_sin[None, :], np.sin(angle), np.cos(angle))
    slope = -0.5 * (np.roll(basis, -1, 0) - np.roll(basis, 1, 0))
    order = OFFSET_CELLS * (cells % BANDS) + cells // BANDS
    here = (cells[None, :] == wave[:, None]).astype(np.float64)
    there = (cells[None, :] == (-wave[:, None]) % GRID).astype(np.float64)
    count = np.where((wave == 0) | (wave == HALF), 1.0, 2.0)[:, None] / GRID
    sign = np.where(is_sin, -1.0, 1.0)[:, None]
    even = 0.5 * (here + there) * count
    odd = 0.5 * (here - there) * count
    mixers = np.stack([even, even.T, odd * sign, -(odd * sign).T])
    forward = [split_table(basis.T), split_table(basis)]
    inverse = [split_table(table) for table in (slope.T, basis[order], slope[order])]
    tables = [*forward, mixers, *inverse]
    return np.concatenate([table.astype(ml_dtypes.bfloat16) for table in tables])


def dot(a, b):
    return jnp.dot(a, b, preferred_element_type=f32)


def dot_nt(a, b):
    return lax.dot_general(a, b, (((1,), (1,)), ((), ())), preferred_element_type=f32)


def halves(x):
    high = x.astype(bf16)
    return high, (x - high.astype(f32)).astype(bf16)


def wide(x, axis):
    high, low = halves(x)
    return jnp.concatenate([high, low, high], axis=axis)


def long(table, axis):
    return jnp.concatenate([table[0], table[0], table[1]], axis=axis)


def query_rows(rows, cols, up, down):
    half = rows.shape[1] // 2
    marks = [jnp.full((1, LANES), mark, f32) for mark in (up, down, 0.0, 0.0)]
    places = [rows[:, :half], rows[:, half:], cols[:, :half], cols[:, half:]]
    return [jnp.concatenate(pair, axis=1) for pair in zip(places, marks)]


def deposit(messages, columns, beam):
    cells = lax.broadcasted_iota(jnp.int32, (GRID, GRID), 0).astype(f32)
    row_hots, col_hots = [], []
    for message in messages:
        for part in range((message.shape[0] - columns) // 6):
            base = columns + 6 * part + 3 * beam
            charge = message[base : base + 1, :].astype(f32)
            rows = message[base + 1 : base + 2, :].astype(f32)
            cols = message[base + 2 : base + 3, :].astype(f32)
            row_hots.append(jnp.where(cells == rows, 1.0, 0.0).astype(bf16))
            col_hots.append(jnp.where(cells == cols, charge, 0.0).astype(bf16))
    return dot_nt(jnp.concatenate(col_hots, axis=1), jnp.concatenate(row_hots, axis=1))


def pack_kernel(cells, charges, fill, marks, gains, strengths, green, own, copies, message, factors, far, partial, sent):
    particles = charges.shape[1]
    count = copies.shape[0]
    here = lax.axis_index("bunch")
    columns = green.shape[0]
    message[:columns, :] = green[...].astype(bf16)
    for beam in range(2):
        sign = 1 if beam == 0 else -1
        charge = charges[beam : beam + 1, :].astype(f32) * fill[0, beam].astype(f32)
        rows = cells[beam, 0, 0:1, :].astype(f32)
        cols = cells[beam, 0, 1:2, :].astype(f32)
        for part in range(particles // GRID):
            lanes = slice(part * GRID, (part + 1) * GRID)
            for row, value in enumerate((charge, rows, cols)):
                at = columns + 6 * part + 3 * beam + row
                message[at : at + 1, :] = value[:, lanes].astype(bf16)
        for offset in range(REACH):
            up = marks[beam, 0, 0, offset - 1].astype(f32) if offset else 0.0
            down = marks[beam, 1, 0, offset + 1].astype(f32) if offset < STOPS - 1 else 0.0
            target = own if offset == 0 else copies.at[count - 1 - lax.rem(here + sign * offset + count, count)]
            for row, value in enumerate(query_rows(rows, cols, up, down)):
                target[4 * beam + row : 4 * beam + row + 1, :] = value.astype(bf16)

    for stop in range(STOPS):
        factors[stop : stop + 1, :] = jnp.full((1, 2 * LANES), gains[stop], f32)
        product = gains[stop] * strengths[stop]
        factors[STOPS + stop : STOPS + stop + 1, :] = jnp.full((1, 2 * LANES), product, f32)

    @pl.when(is_early())
    def start():
        pltpu.make_async_copy(copies, far, sent).start()

    @pl.when(is_early())
    def work():
        for beam in range(2):
            partial[:, beam * GRID : (beam + 1) * GRID] = deposit([message], columns, beam)
        pltpu.make_async_copy(copies, far, sent).wait()


def is_early():
    return lax.axis_index("tile") < 1


def late_kernel(copies, far, out, sent):
    @pl.when(jnp.logical_not(is_early()))
    def write():
        copy = pltpu.make_async_copy(copies, out, sent)
        copy.start()
        copy.wait()


def field_kernel(tiles, *refs):
    here = lax.axis_index("tile")
    messages = refs[:tiles]
    partial, far, out, near, gathered, densities, arrived = refs[tiles:]
    cuts = (0, FORWARD_TABLES, near.shape[0] - INVERSE_TABLES, near.shape[0])
    fetch = [
        pltpu.make_async_copy(far.at[start:end], near.at[start:end], arrived.at[which])
        for which, (start, end) in enumerate(zip(cuts, cuts[1:]))
    ]
    for copy in fetch:
        copy.start()
    columns = GRID // tiles
    for step, message in zip(steps_of(tiles), messages):
        start = pl.multiple_of(relative(here, step, tiles) * columns, columns)
        gathered[pl.ds(start, columns), :] = message[:columns, :]

    @pl.when(is_early())
    def add_others():
        for beam in range(2):
            lanes = slice(beam * GRID, (beam + 1) * GRID)
            density = partial[:, lanes] + deposit(messages[1:], columns, beam)
            densities[:, lanes] = wide(density, 0)

    @pl.when(jnp.logical_not(is_early()))
    def add_all():
        for beam in range(2):
            density = deposit(messages, columns, beam)
            densities[:, beam * GRID : (beam + 1) * GRID] = wide(density, 0)

    fetch[0].wait()
    first = dot(long(near[0:2], 1), densities[...])
    first = jnp.concatenate([first[:, :GRID], first[:, GRID:]], axis=0)
    fetch[1].wait()
    alpha, beta = (
        dot(near[side], turned[0]) + dot(near[side], turned[1])
        for side, turned in (
            (side, halves(dot(gathered[...], near[side + 1]))) for side in (4, 6)
        )
    )
    spectra = dot(wide(first, 1), long(near[2:4], 0))
    scaled = []
    for beam in range(2):
        spectrum = spectra[beam * GRID : (beam + 1) * GRID]
        swapped = jnp.concatenate(
            [
                jnp.concatenate([spectrum[HALF:, HALF:], spectrum[HALF:, :HALF]], axis=1),
                jnp.concatenate([spectrum[:HALF, HALF:], spectrum[:HALF, :HALF]], axis=1),
            ],
            axis=0,
        )
        scaled.append(alpha * spectrum + beta * swapped)
    fetch[2].wait()
    left = jnp.concatenate([long(near[10:12], 1), long(near[12:14], 1)], axis=0)
    part = dot(left, wide(jnp.concatenate(scaled, axis=1), 0)).astype(bf16)
    for axis, right in enumerate((8, 0)):
        rows = part[axis * GRID : (axis + 1) * GRID]
        rows = jnp.concatenate([rows[:, :GRID], rows[:, GRID:]], axis=0)
        field = dot(rows, near[right]) + dot(rows, near[right + 1])
        for beam in range(2):
            out[beam, axis * GRID : (axis + 1) * GRID, :] = field[
                beam * GRID : (beam + 1) * GRID
            ].astype(bf16)


def kick_kernel(count, factors, fields, own, queries, home, away):
    half = queries.shape[-1] - LANES
    here = lax.axis_index("bunch")
    block = 2 * LANES
    cells = lax.broadcasted_iota(jnp.int32, (GRID, block), 0).astype(f32)
    bands = lax.broadcasted_iota(jnp.int32, (BANDS, block), 0).astype(f32)
    for offset in range(REACH):
        for beam in range(2):
            sign = 1 if beam == 0 else -1
            target = count - 1 - lax.rem(here - sign * offset + count, count)
            source = queries.at[target] if offset else own
            base = 4 * beam

            def weight_of(stop, row):
                mark = source[base + row : base + row + 1, half:].astype(f32)
                return jnp.concatenate([mark, mark], axis=1) * factors[STOPS + stop : STOPS + stop + 1, :]

            middle = factors[offset : offset + 1, :] if offset < STOPS else None
            up = weight_of(offset - 1, 0) if offset else None
            down = weight_of(offset + 1, 1) if offset < STOPS - 1 else None
            for start in range(0, 2 * half, block):
                row, lanes = base + start // half, pl.ds(start % half, block)
                rows = source[row : row + 1, lanes].astype(f32)
                cols = source[row + 2 : row + 3, lanes].astype(f32)
                band = jnp.floor(cols * (1.0 / OFFSET_CELLS))
                inside = jnp.broadcast_to(cols - band * OFFSET_CELLS, (BANDS, block))
                hot = jnp.where(cells == rows, 1.0, 0.0).astype(bf16)
                values = dot(fields[1 - beam], hot)
                picked = [jnp.zeros((BANDS, block), f32) for _ in range(2)]
                for place in range(OFFSET_CELLS):
                    hit = inside == place
                    for axis in range(2):
                        at = axis * GRID + place * BANDS
                        picked[axis] = jnp.where(hit, values[at : at + BANDS, :], picked[axis])
                weight = jnp.zeros((BANDS, block), f32)
                if middle is not None:
                    weight = jnp.where(bands == band, middle, weight)
                if up is not None:
                    weight = jnp.where(bands == band - 1, up, weight)
                if down is not None:
                    weight = jnp.where(bands == band + 1, down, weight)
                kick = [jnp.sum(weight * value, axis=0, keepdims=True) for value in picked]
                kick = jnp.concatenate(kick, axis=0)
                if offset == 0:
                    home[2 * beam : 2 * beam + 2, start : start + block] = kick
                elif shared(offset, count):
                    away[target, 2 * beam : 2 * beam + 2, start : start + block] = kick.astype(bf16)
                else:
                    away[target, :, start : start + block] = jnp.concatenate(halves(kick), axis=0)


def shared(offset, count):
    return 2 * offset == count


def final_kernel(count, received, home, momenta, out):
    here = lax.axis_index("bunch")
    for beam in range(2):
        sign = 1 if beam == 0 else -1
        total = home[2 * beam : 2 * beam + 2, :]
        for offset in range(1, REACH):
            part = received[count - 1 - lax.rem(here + sign * offset + count, count)].astype(f32)
            if shared(offset, count):
                total = total + part[2 * beam : 2 * beam + 2]
            else:
                total = total + (part[:2] + part[2:])
        out[beam, 0] = momenta[beam, 0] + total.astype(bf16).astype(f32)


SMEM = pl.BlockSpec(memory_space=pltpu.SMEM)
VMEM = pl.BlockSpec(memory_space=pltpu.VMEM)
FAR = pl.BlockSpec(memory_space=pltpu.HBM)
LIMIT = pltpu.CompilerParams(vmem_limit_bytes=48 * 1024 * 1024)
SMALL = pltpu.CompilerParams(vmem_limit_bytes=16 * 1024 * 1024)


def kept_far(value):
    return pltpu.with_memory_space_constraint(value, pltpu.HBM)


def steps_of(tiles):
    return [0, *[1, 3, 2]] if tiles == 4 else list(range(tiles))


def is_power_of_two(count):
    return count & (count - 1) == 0


def relative(index, step, count):
    if is_power_of_two(count):
        return jnp.bitwise_xor(index, step)
    return lax.rem(index - step + count, count)


def exchanged(value, axis, step):
    count = lax.axis_size(axis)
    if is_power_of_two(count):
        pairs = [(i, i ^ step) for i in range(count)]
    else:
        pairs = [(i, (i + step) % count) for i in range(count)]
    return lax.ppermute(value, axis, pairs)


def body(cell_index, charges, momenta, fill_pattern, encounters, green_spectrum, stop_gain, parasitic_gain):
    particles = cell_index.shape[3]
    tiles = lax.axis_size("tile")
    count = lax.axis_size("bunch")
    tables = make_tables()
    columns = green_spectrum.shape[1]
    own, staged, message, factors, copies, partial = pl.pallas_call(
        pack_kernel,
        out_shape=(
            jax.ShapeDtypeStruct((8, particles // 2 + LANES), bf16),
            jax.ShapeDtypeStruct((count, 8, particles // 2 + LANES), bf16),
            jax.ShapeDtypeStruct((columns + 6 * particles // GRID, GRID), bf16),
            jax.ShapeDtypeStruct((2 * STOPS, 2 * LANES), f32),
            jax.ShapeDtypeStruct((count, 8, particles // 2 + LANES), bf16),
            jax.ShapeDtypeStruct((GRID, 2 * GRID), f32),
        ),
        in_specs=[VMEM, VMEM, SMEM, SMEM, SMEM, SMEM, VMEM],
        out_specs=(VMEM, VMEM, VMEM, VMEM, FAR, VMEM),
        scratch_shapes=[pltpu.SemaphoreType.DMA],
        compiler_params=SMALL,
    )(
        kept_far(cell_index),
        kept_far(charges.reshape(2, particles)),
        kept_far(fill_pattern.T),
        kept_far(jnp.transpose(encounters, (1, 2, 3, 0))),
        kept_far(stop_gain),
        kept_far(parasitic_gain),
        kept_far(green_spectrum.T),
    )
    copies = pl.pallas_call(
        late_kernel,
        out_shape=jax.ShapeDtypeStruct(copies.shape, bf16),
        in_specs=[VMEM, FAR],
        out_specs=FAR,
        scratch_shapes=[pltpu.SemaphoreType.DMA],
        input_output_aliases={1: 0},
        compiler_params=SMALL,
    )(staged, copies)
    messages = [message] + [exchanged(message, "tile", step) for step in steps_of(tiles)[1:]]
    queries = lax.all_to_all(copies, "bunch", split_axis=0, concat_axis=0, tiled=True, axis_index_groups=[list(reversed(range(count)))])
    fields = pl.pallas_call(
        functools.partial(field_kernel, tiles),
        out_shape=jax.ShapeDtypeStruct((2, 2 * GRID, GRID), bf16),
        in_specs=[VMEM] * (tiles + 1) + [FAR],
        out_specs=VMEM,
        scratch_shapes=[
            pltpu.VMEM(tables.shape, bf16),
            pltpu.VMEM((GRID, GRID), bf16),
            pltpu.VMEM((3 * GRID, 2 * GRID), bf16),
            pltpu.SemaphoreType.DMA((3,)),
        ],
        compiler_params=LIMIT,
        cost_estimate=pl.CostEstimate(flops=3000000000, bytes_accessed=1000000, transcendentals=0),
    )(*messages, partial, kept_far(jnp.asarray(tables)))
    home, away = pl.pallas_call(
        functools.partial(kick_kernel, count),
        out_shape=(
            jax.ShapeDtypeStruct((4, particles), f32),
            jax.ShapeDtypeStruct((count, 4, particles), bf16),
        ),
        in_specs=[VMEM, VMEM, VMEM, VMEM],
        out_specs=(VMEM, VMEM),
        compiler_params=LIMIT,
    )(factors, fields, own, queries)
    received = lax.all_to_all(away, "bunch", split_axis=0, concat_axis=0, tiled=True, axis_index_groups=[list(reversed(range(count)))])
    return pl.pallas_call(
        functools.partial(final_kernel, count),
        out_shape=jax.ShapeDtypeStruct(momenta.shape, f32),
        in_specs=[VMEM, VMEM, VMEM],
        out_specs=VMEM,
        compiler_params=SMALL,
    )(received, home, momenta)


def solution(mesh):
    in_specs = (
        P(None, "bunch", None, "tile"),
        P(None, "bunch", "tile"),
        P(None, "bunch", None, "tile"),
        P(None, "bunch"),
        P(None, None, None, "bunch"),
        P(None, "tile"),
        P(),
        P(),
    )
    out_specs = P(None, "bunch", None, "tile")
    return jax.shard_map(body, mesh=mesh, in_specs=in_specs, out_specs=out_specs, check_vma=False)
```
